128 devices in a mesh: dp: 8 (over z_hi, y), ctx: 16 (over x, z_lo, core).
Axes of the slice: x: 4, y: 4, z: 4 (z_hi: 2, z_lo: 2; z = z_hi * 2 + z_lo), core: 2. Of those that a mesh axis runs over, the one named last changes fastest.
Arguments:
- queries: bfloat16 [8, 2048, 4096], P('dp', 'ctx'), may hold values from -6 to 6
- keys: bfloat16 [8, 2048, 512], P('dp', 'ctx'), may hold values from -6 to 6
- values: bfloat16 [8, 2048, 512], P('dp', 'ctx'), may hold values from -6 to 6
- saved: bfloat16 [8, 2048, 4096], P('dp', 'ctx'), may hold values from -6 to 6
- out_grad: bfloat16 [8, 2048, 4096], P('dp', 'ctx'), may hold values from -6 to 6
- doc_ids: int32 [8, 2048], P('dp', 'ctx'), may hold values from 0 to 2, never falling along the last dimension, each value on 1 to 1024 neighbouring positions
- inputs: bfloat16 [8, 2048, 4096], P('dp', 'ctx'), may hold values from -6 to 6
- bmat: bfloat16 [8, 2048, 512], P('dp', 'ctx'), may hold values from -1.1953125 to 1.1953125
- cmat: bfloat16 [8, 2048, 512], P('dp', 'ctx'), may hold values from -1.1953125 to 1.1953125
- step: float32 [8, 2048, 128], P('dp', 'ctx'), may hold values from 0.25 to 1
- alog: float32 [128], replicated, may hold values from -9 to -3
- skip: float32 [128], replicated, may hold values from 0.5 to 1.5
Outputs:
- grad_keys: bfloat16 [8, 2048, 512], P('dp', 'ctx')
- grad_values: bfloat16 [8, 2048, 512], P('dp', 'ctx')
- grad_inputs: bfloat16 [8, 2048, 4096], P('dp', 'ctx')
- grad_decay: float32 [2, 128], replicated
The draws below stay inside these ranges and needn't reach their ends.
Inputs may be any that keep to these rules, and one draw needn't show every extreme that they name: `doc_ids`: numbers never fall along a sequence; each document has at least one position and one has exactly 1024.
All inputs are finite; a program needn't handle non-finite values.
Results may differ from the reference program's by a relative error of at most 0.0045.
The reference program's roundings to bfloat16 on the way count: a program that leaves them out, or rounds other values in their place, can miss the bound.
Values may be sent and summed in bfloat16 or wider, within the bound.
A program may use at most 256 MiB of HBM per device.

```python
import math
import jax
import jax.numpy as jnp
import numpy as np
from jax import lax

TOK_DEV = 128
QHEADS = 32
KVHEADS = 4
HEAD_DIM = 128
SSM_HEADS = 128
SSM_DIM = 32
STATE = 128
GROUPS = 4
SEQ = 2048
BATCH = 8
N_CTX = 16


def draw_queries(key, part):
    key = jax.random.fold_in(key, 11)
    drawn = jnp.clip(jax.random.normal(key, (BATCH, SEQ, QHEADS * HEAD_DIM), jnp.float32), -6.0, 6.0)
    return drawn.astype(jnp.bfloat16)


def draw_keys(key, part):
    key = jax.random.fold_in(key, 12)
    drawn = jnp.clip(jax.random.normal(key, (BATCH, SEQ, KVHEADS * HEAD_DIM), jnp.float32), -6.0, 6.0)
    return drawn.astype(jnp.bfloat16)


def steps_of(key, shape, split, smallest, largest):
    def one(dim, shards_of):
        steps = jax.random.uniform(jax.random.fold_in(jax.random.fold_in(key, 6), dim), (shards_of,), jnp.float32, smallest / len(split), largest / len(split))
        return jnp.repeat(jnp.exp(steps), shape[dim] // shards_of).reshape((-1,) + (1,) * (len(shape) - dim - 1))

    factor_of = one(*split[0])
    for cut in split[1:]:
        factor_of = factor_of * one(*cut)
    return factor_of


def profile(count, total, limit, lean):
    portions = [(1 << 20) // math.isqrt(rank ** lean) + 1 for rank in range(2, count + 1)]
    surplus, given = total - limit - (count - 1), [1] * (count - 1)
    while surplus > 0:
        movable = [i for i in range(count - 1) if given[i] < limit]
        mass, left = sum([portions[i] for i in movable]), surplus
        for i in movable:
            extra = min(limit - given[i], max(1, left * portions[i] // mass), surplus)
            given[i] = given[i] + extra
            surplus = surplus - extra
    return np.array([limit] + given)


def uneven_parts(stream_key, number_of, total, most, skew):
    if number_of == 2:
        one = jax.random.randint(stream_key, (), max(1, total - most), min(most, total - 1) + 1)
        return jnp.stack([one, total - one])
    sizes = jnp.asarray(profile(number_of, total, most, skew), jnp.int32)
    twos = (number_of - 1) // 2
    source_of, receiver = sizes[1:1 + 2 * twos:2], sizes[2:2 + 2 * twos:2]
    margin = jnp.minimum(source_of - 1, most - receiver)
    passed = jax.random.randint(jax.random.fold_in(stream_key, 1), (twos,), 0, 1 << 20) % (margin + 1)
    sizes = sizes.at[1:1 + 2 * twos:2].set(source_of - passed).at[2:2 + 2 * twos:2].set(receiver + passed)
    return sizes[jax.random.permutation(jax.random.fold_in(stream_key, 2), number_of)]


def gaussian(key, dims, deviation, bound, pieces=(), kind=jnp.bfloat16):
    values = deviation * jax.random.normal(key, dims, jnp.float32)
    if pieces:
        values = values * steps_of(key, dims, pieces, -0.22, 0.18)
    return jnp.clip(values, -bound, bound).astype(kind)


def setup_inputs(seed: int = 0) -> dict:
    seeds = jax.random.split(jax.random.key(seed), 13)
    queries = draw_queries(jax.random.fold_in(seeds[12], 71), 0)
    keys = draw_keys(jax.random.fold_in(seeds[12], 71), 0)
    values = gaussian(seeds[2], (BATCH, SEQ, KVHEADS * HEAD_DIM), 1.0, 6.0, ((0, 8), (1, 16)))
    saved = gaussian(seeds[3], (BATCH, SEQ, QHEADS * HEAD_DIM), 1.0, 6.0, ((0, 8), (1, 16)))
    out_grad = gaussian(seeds[4], (BATCH, SEQ, QHEADS * HEAD_DIM), 1.0, 6.0, ((0, 8), (1, 16)))
    doc_ids = jax.vmap(lambda own: jnp.searchsorted(jnp.cumsum(uneven_parts(own, 3, SEQ, SEQ // 2, 0)), jnp.arange(SEQ), side="right"))(jax.random.split(seeds[5], BATCH)).reshape((BATCH, SEQ)).astype(jnp.int32)
    inputs = gaussian(seeds[6], (BATCH, SEQ, SSM_HEADS * SSM_DIM), 1.0, 6.0, ((0, 8), (1, 16)))
    bmat = gaussian(seeds[7], (BATCH, SEQ, GROUPS * STATE), 0.2, 1.1953125, ((0, 8), (1, 16)))
    cmat = gaussian(seeds[8], (BATCH, SEQ, GROUPS * STATE), 0.2, 1.1953125, ((0, 8), (1, 16)))
    step = jnp.clip(jnp.exp(math.log(1.0) - 1.3862944 * jax.random.uniform(seeds[9], (BATCH, SEQ, SSM_HEADS), jnp.float32) ** steps_of(seeds[9], (BATCH, SEQ, SSM_HEADS), ((0, 8), (1, 16)), -0.2, 0.2)), 0.25, 1.0)
    alog = jnp.clip(jax.random.uniform(seeds[10], (SSM_HEADS,), jnp.float32, -9.0, -3.0), -9.0, -3.0)
    skip = jnp.clip(jax.random.uniform(seeds[11], (SSM_HEADS,), jnp.float32, 0.5, 1.5), 0.5, 1.5)
    return {"queries": queries, "keys": keys, "values": values, "saved": saved, "out_grad": out_grad, "doc_ids": doc_ids, "inputs": inputs, "bmat": bmat, "cmat": cmat, "step": step, "alog": alog, "skip": skip}


HIGHEST = lax.Precision.HIGHEST

def storage_positions(rows, per_dev, count):
    half = per_dev // 2
    device = rows // per_dev
    within = rows % per_dev
    block = jnp.where(within < half, device, 2 * count - 1 - device)
    return (block * half + within % half).astype(jnp.int32)

def span_whole(step, keep, alog):
    total = jnp.cumsum(-step * jnp.exp(alog)[None, :], axis=0)
    resets = jnp.cumsum(1.0 - keep)
    return jnp.exp(total[-1]) * (resets[-1] == 0).astype(jnp.float32)

def ssd_span(inputs, bmat, cmat, step, keep, alog, skip, h_in):
    rows = inputs.shape[0]
    heads = alog.shape[0]
    groups = bmat.shape[1] // STATE
    ratio = heads // groups
    total = jnp.cumsum(-step * jnp.exp(alog)[None, :], axis=0)
    resets = jnp.cumsum(1.0 - keep)
    xheads = inputs.reshape(rows, heads, -1)
    bgroup = bmat.astype(jnp.float32).reshape(rows, groups, STATE)
    cgroup = cmat.astype(jnp.float32).reshape(rows, groups, STATE)
    bheads = jnp.repeat(bgroup, ratio, axis=1)
    cheads = jnp.repeat(cgroup, ratio, axis=1)
    order = jnp.arange(rows)
    same = (order[:, None] >= order[None, :]) & (resets[:, None] == resets[None, :])
    diff = total[:, None, :] - total[None, :, :]
    lmat = jnp.where(same[:, :, None], jnp.exp(jnp.where(same[:, :, None], diff, 0.0)), 0.0)
    inner = jnp.einsum('tgn,sgn->tsg', cgroup, bgroup)
    inner = jnp.repeat(inner, ratio, axis=2)
    weights = inner * lmat * step[None, :, :]
    intra = jnp.einsum('tsh,shp->thp', weights, xheads, precision=HIGHEST)
    entry = jnp.exp(total) * (resets == 0).astype(jnp.float32)[:, None]
    carried = jnp.einsum('hpn,thn->thp', h_in, cheads, precision=HIGHEST) * entry[:, :, None]
    output = intra + carried + skip[None, :, None] * xheads
    tail = jnp.exp(total[-1][None, :] - total) * (resets == resets[-1]).astype(jnp.float32)[:, None]
    whole = jnp.exp(total[-1]) * (resets[-1] == 0).astype(jnp.float32)
    fresh = jnp.einsum('shp,shn->hpn', (tail * step)[:, :, None] * xheads, bheads, precision=HIGHEST)
    h_out = whole[:, None, None] * h_in + fresh
    return (output.reshape(rows, -1), h_out)

def tile_terms(qgroup, dgroup, lse, delta, kgroup, vgroup, mask):
    scale = HEAD_DIM ** (-0.5)
    scores = jnp.einsum('qhd,kd->hqk', qgroup.astype(jnp.float32), kgroup.astype(jnp.float32)) * scale
    probs = jnp.where(mask[None], jnp.exp(scores - lse[:, :, None]), 0.0)
    dprobs = jnp.einsum('qhd,kd->hqk', dgroup.astype(jnp.float32), vgroup.astype(jnp.float32))
    dscores = (probs * (dprobs - delta[:, :, None]) * scale).astype(jnp.bfloat16)
    return (probs.astype(jnp.bfloat16), dscores)

def attention_grads(queries, keys, values, saved, out_grad, ids):
    rows = queries.shape[0]
    ratio = QHEADS // KVHEADS
    width = ratio * HEAD_DIM
    pos = storage_positions(jnp.arange(rows, dtype=jnp.int32), TOK_DEV, N_CTX)
    docs = jnp.take(ids, pos)
    mask = (pos[None, :] <= pos[:, None]) & (docs[None, :] == docs[:, None])

    def per_group(group):
        qgroup = lax.dynamic_slice_in_dim(queries, group * width, width, 1).reshape(rows, ratio, HEAD_DIM)
        dgroup = lax.dynamic_slice_in_dim(out_grad, group * width, width, 1).reshape(rows, ratio, HEAD_DIM)
        ogroup = lax.dynamic_slice_in_dim(saved, group * width, width, 1).reshape(rows, ratio, HEAD_DIM)
        kgroup = lax.dynamic_slice_in_dim(keys, group * HEAD_DIM, HEAD_DIM, 1)
        vgroup = lax.dynamic_slice_in_dim(values, group * HEAD_DIM, HEAD_DIM, 1)
        scores = jnp.einsum('qhd,kd->hqk', qgroup.astype(jnp.float32), kgroup.astype(jnp.float32)) * HEAD_DIM ** (-0.5)
        lse = jax.nn.logsumexp(jnp.where(mask[None], scores, -jnp.inf), axis=-1)
        delta = lax.optimization_barrier(jnp.sum(dgroup.astype(jnp.float32) * ogroup.astype(jnp.float32), axis=-1)).T
        probs_b, dscores = tile_terms(qgroup, dgroup, lse, delta, kgroup, vgroup, mask)
        dscores32 = dscores.astype(jnp.float32)
        grad_q = jnp.einsum('hqk,kd->qhd', dscores32, kgroup.astype(jnp.float32)).astype(jnp.bfloat16)
        grad_k = jnp.einsum('hqk,qhd->kd', dscores32, qgroup.astype(jnp.float32))
        grad_v = jnp.einsum('hqk,qhd->kd', probs_b.astype(jnp.float32), dgroup.astype(jnp.float32))
        return (grad_q.reshape(rows, width), grad_k, grad_v)
    grad_q, grad_k, grad_v = lax.map(per_group, jnp.arange(KVHEADS, dtype=jnp.int32))
    grad_q = jnp.transpose(grad_q, (1, 0, 2)).reshape(rows, -1)
    grad_k = jnp.transpose(grad_k, (1, 0, 2)).reshape(rows, -1).astype(jnp.bfloat16)
    grad_v = jnp.transpose(grad_v, (1, 0, 2)).reshape(rows, -1).astype(jnp.bfloat16)
    return (grad_q, grad_k, grad_v)

def to_positions(grad_q):
    rows = grad_q.shape[0]
    half = TOK_DEV // 2
    places = jnp.arange(rows, dtype=jnp.int32)
    block = places // half
    owner = jnp.where(block < N_CTX, block, 2 * N_CTX - 1 - block)
    slot = (block >= N_CTX).astype(jnp.int32)
    source = (owner * TOK_DEV + slot * half + places % half).astype(jnp.int32)
    return jnp.take(grad_q, source, axis=0)

def ssd_grads(inputs, bmat, cmat, step, ids, alog, skip, cotangent):
    rows = inputs.shape[0]
    count = rows // TOK_DEV
    previous = jnp.concatenate([jnp.full((1,), -1, jnp.int32), ids[:-1]])
    keep = (ids == previous).astype(jnp.float32)

    def blocks(array):
        return array.reshape((count, TOK_DEV) + array.shape[1:])

    def forward(inputs32, alog_in, skip_in):

        def advance(state, block):
            out, state = ssd_span(block[0], block[1], block[2], block[3], block[4], alog_in, skip_in, state)
            return (state, out)
        start = jnp.zeros((SSM_HEADS, SSM_DIM, STATE), jnp.float32)
        _, outs = lax.scan(advance, start, (blocks(inputs32), blocks(bmat), blocks(cmat), blocks(step), blocks(keep)))
        return outs.reshape(rows, -1)
    _, pullback = jax.vjp(forward, inputs.astype(jnp.float32), alog, skip)
    grad_x, grad_a, grad_s = pullback(cotangent.astype(jnp.float32))
    return (grad_x.astype(jnp.bfloat16), grad_a, grad_s)

def reference(queries, keys, values, saved, out_grad, doc_ids, inputs, bmat, cmat, step, alog, skip):

    def one(items):
        q_in, k_in, v_in, o_in, d_in, ids, x_in, b_in, c_in, s_in = items
        grad_q, grad_k, grad_v = attention_grads(q_in, k_in, v_in, o_in, d_in, ids)
        cotangent = to_positions(grad_q)
        grad_x, grad_a, grad_s = ssd_grads(x_in, b_in, c_in, s_in, ids, alog, skip, cotangent)
        return (grad_k, grad_v, grad_x, grad_a, grad_s)
    grad_k, grad_v, grad_x, grad_a, grad_s = lax.map(one, (queries, keys, values, saved, out_grad, doc_ids, inputs, bmat, cmat, step))
    return (grad_k, grad_v, grad_x, jnp.stack([lax.optimization_barrier(jnp.sum(grad_a, axis=0)), lax.optimization_barrier(jnp.sum(grad_s, axis=0))]))
```

```python
import functools

import jax
import jax.numpy as jnp
from jax import lax
from jax.experimental import pallas as pl
from jax.experimental.pallas import tpu as pltpu
from jax.sharding import PartitionSpec as P

QHEADS = 32
KVHEADS = 4
HEAD_DIM = 128
SSM_HEADS = 128
SSM_DIM = 32
STATE = 128
SEQ = 2048
ROWS = 128
HALF = 64
CTX = 16
DP = 8
WIDTH = 256
OWN = 8
BLOCK = 256
SPAN = 5
SCALE = HEAD_DIM ** (-0.5)
FAR = -1e30

MESH = pl.DeviceIdType.MESH
HIGHEST = lax.Precision.HIGHEST
F32 = jnp.float32
BF16 = jnp.bfloat16


def dot(a, b, dims, precision=None):
    return lax.dot_general(a, b, (dims, ((), ())), precision=precision, preferred_element_type=F32)


NN = ((1,), (0,))
NT = ((1,), (1,))
TN = ((0,), (0,))


def three(a):
    high = a.astype(BF16)
    rest = a - high.astype(F32)
    mid = rest.astype(BF16)
    low = (rest - mid.astype(F32)).astype(BF16)
    return high, mid, low


def greet(axis, count):
    me = lax.axis_index(axis)
    barrier = pltpu.get_barrier_semaphore()

    def one(off, _):
        pl.semaphore_signal(barrier, inc=1, device_id={axis: lax.rem(me + off, count)}, device_id_type=MESH)
        return 0

    lax.fori_loop(1, count, one, 0)


def await_greetings(total):
    pl.semaphore_wait(pltpu.get_barrier_semaphore(), total)


def pack_small(out_grad, saved, ids, step, alog, small):
    ones = jnp.ones((8, HEAD_DIM), F32)
    sub = lax.broadcasted_iota(jnp.int32, (8, ROWS), 0)
    docs = jnp.broadcast_to(ids[...].astype(F32), (8, ROWS))
    rate = step[0] * -jnp.exp(alog[...])
    upto = lax.broadcasted_iota(jnp.int32, (ROWS, ROWS), 0) <= lax.broadcasted_iota(jnp.int32, (ROWS, ROWS), 1)
    totals = dot(rate, upto.astype(F32), TN, HIGHEST)
    steps = step[0].T
    for j in range(CTX):
        small[j, 0:8, :] = steps[8 * j : 8 * j + 8]
        small[j, 8:16, :] = totals[8 * j : 8 * j + 8]

    def one(j, _):
        deltas = []
        for h in range(2):
            cols = pl.ds(pl.multiple_of(WIDTH * j + HEAD_DIM * h, HEAD_DIM), HEAD_DIM)
            product = out_grad[0, :, cols].astype(F32) * saved[0, :, cols].astype(F32)
            deltas.append(dot(ones, product, NT, HIGHEST))
        small[j, 16:24, :] = jnp.where(sub == 0, deltas[0], jnp.where(sub == 1, deltas[1], docs))
        return 0

    lax.fori_loop(0, CTX, one, 0)


def in_moves(peer, place, arrays, landed):
    q, d, k, v, x, b, c, small = arrays
    lq, ld, lk, lv, lx, lb, lc, ls = landed
    wide = pl.ds(pl.multiple_of(peer * WIDTH, WIDTH), WIDTH)
    narrow = pl.ds(pl.multiple_of(peer // 4 * HEAD_DIM, HEAD_DIM), HEAD_DIM)
    early = pl.ds(pl.multiple_of(place * HALF, HALF), HALF)
    late = pl.ds(pl.multiple_of((2 * CTX - 1 - place) * HALF, HALF), HALF)
    here = pl.ds(pl.multiple_of(place * ROWS, ROWS), ROWS)
    first, second = pl.ds(0, HALF), pl.ds(HALF, HALF)
    moves = []
    for src, dst in ((k, lk), (v, lv)):
        moves.append((src.at[0, second, narrow], dst.at[late, :]))
        moves.append((src.at[0, first, narrow], dst.at[early, :]))
    for src, dst in ((q, lq), (d, ld)):
        moves.append((src.at[0, second, wide], dst.at[late, :]))
    for src, dst in ((q, lq), (d, ld)):
        moves.append((src.at[0, first, wide], dst.at[early, :]))
    for src, dst in ((b, lb), (c, lc)):
        moves.append((src.at[0, :, narrow], dst.at[here, :]))
    moves.append((x.at[0, :, wide], lx.at[here, :]))
    moves.append((small.at[peer], ls.at[place]))
    return moves


KINDS = 12


def in_kernel(q, d, k, v, x, b, c, dv, o, ids, step, alog, *rest):
    landed = rest[:8]
    small, send_sem, recv_sem, own_sem = rest[8:]
    me = lax.axis_index("ctx")
    arrays = (q, d, k, v, x, b, c, small)

    def remote(kind, to, frm):
        src, dst = in_moves(to, frm, arrays, landed)[kind]
        return src, dst

    def send(off, kinds):
        to = lax.rem(me + off, CTX)
        for kind in kinds:
            src, dst = remote(kind, to, me)
            pltpu.make_async_remote_copy(
                src_ref=src, dst_ref=dst, send_sem=send_sem.at[kind, to], recv_sem=recv_sem.at[kind, me],
                device_id={"ctx": to}, device_id_type=MESH,
            ).start()

    greet("ctx", CTX)
    await_greetings(CTX - 1)
    bulk = tuple(range(KINDS - 1))
    for kinds in (bulk,):
        lax.fori_loop(1, CTX, lambda off, _: (send(off, kinds), 0)[1], 0)
    for kind in bulk:
        src, dst = remote(kind, me, me)
        pltpu.make_async_copy(src, dst, own_sem.at[kind]).start()
    pack_small(dv, o, ids, step, alog, small)
    lax.fori_loop(1, CTX, lambda off, _: (send(off, (KINDS - 1,)), 0)[1], 0)
    src, dst = remote(KINDS - 1, me, me)
    pltpu.make_async_copy(src, dst, own_sem.at[KINDS - 1]).start()

    def finish(off, _):
        to = lax.rem(me + off, CTX)
        frm = lax.rem(me + CTX - off, CTX)
        for kind in range(KINDS):
            src, dst = remote(kind, to, frm)
            copy = pltpu.make_async_remote_copy(
                src_ref=src, dst_ref=dst, send_sem=send_sem.at[kind, to], recv_sem=recv_sem.at[kind, frm],
                device_id={"ctx": to}, device_id_type=MESH,
            )
            copy.wait_send()
            copy.wait_recv()
        return 0

    lax.fori_loop(1, CTX, finish, 0)
    for kind in range(KINDS):
        src, dst = remote(kind, me, me)
        pltpu.make_async_copy(src, dst, own_sem.at[kind]).wait()


def exchange_in(q, k, v, o, d, ids, x, b, c, step, alog):
    hbm = pl.BlockSpec(memory_space=pl.ANY)
    vmem = pl.BlockSpec(memory_space=pltpu.VMEM)
    shapes = (
        [jax.ShapeDtypeStruct((SEQ, WIDTH), BF16)] * 2
        + [jax.ShapeDtypeStruct((SEQ, HEAD_DIM), BF16)] * 2
        + [jax.ShapeDtypeStruct((SEQ, WIDTH), BF16)]
        + [jax.ShapeDtypeStruct((SEQ, STATE), BF16)] * 2
        + [jax.ShapeDtypeStruct((CTX, 24, ROWS), F32)]
    )
    return pl.pallas_call(
        in_kernel,
        out_shape=shapes,
        in_specs=[hbm] * 7 + [vmem] * 5,
        out_specs=[hbm] * 8,
        scratch_shapes=[
            pltpu.VMEM((CTX, 24, ROWS), F32),
            pltpu.SemaphoreType.DMA((KINDS, CTX)),
            pltpu.SemaphoreType.DMA((KINDS, CTX)),
            pltpu.SemaphoreType.DMA((KINDS,)),
        ],
        compiler_params=pltpu.CompilerParams(
            collective_id=0, has_side_effects=True, vmem_limit_bytes=32 * 2**20
        ),
        name="exchange_in",
    )(q, d, k, v, x, b, c, d, o, ids, step, alog)


def spread_columns(small, dcol, doccol):
    row = lax.broadcasted_iota(jnp.int32, (24, 3 * ROWS), 0) % 8
    lane = lax.broadcasted_iota(jnp.int32, (24, 3 * ROWS), 1) // ROWS
    pick = jnp.where(row == lane, 1.0, 0.0).astype(BF16)
    doccol[0:8, :] = jnp.full((8, ROWS), -1.0, F32)

    def one(src, _):
        parts = jnp.concatenate([p.astype(F32) for p in three(small[src, 16:24, :])], axis=0).astype(BF16)
        wide = dot(parts, pick, TN)
        early = pl.multiple_of(src * HALF, HALF)
        late = pl.multiple_of((2 * CTX - 1 - src) * HALF, HALF)
        dcol[pl.ds(early, HALF), :] = wide[:HALF, : 2 * ROWS]
        dcol[pl.ds(late, HALF), :] = wide[HALF:, : 2 * ROWS]
        doccol[pl.ds(pl.multiple_of(8 + src * ROWS, 8), ROWS), :] = wide[:, 2 * ROWS :]
        return 0

    lax.fori_loop(0, CTX, one, 0)


def attention_block(i, q, d, k, v, small, dcol, doccol, dk, dv, cot, q2, d2, s_ref, m_ref, l_ref, dq):
    base = pl.multiple_of(i * BLOCK, BLOCK)
    rows = pl.ds(base, BLOCK)
    q2[:BLOCK, :] = q[rows, :HEAD_DIM]
    q2[BLOCK:, :] = q[rows, HEAD_DIM:]
    d2[:BLOCK, :] = d[rows, :HEAD_DIM]
    d2[BLOCK:, :] = d[rows, HEAD_DIM:]
    m_ref[...] = jnp.full(m_ref.shape, FAR, F32)
    l_ref[...] = jnp.zeros(l_ref.shape, F32)
    dq[...] = jnp.zeros(dq.shape, F32)
    first = jnp.maximum(i - (SPAN - 1), 0)
    ahead = lax.broadcasted_iota(jnp.int32, (BLOCK, BLOCK), 0) - lax.broadcasted_iota(jnp.int32, (BLOCK, BLOCK), 1)

    def scores(j, _):
        keys = k[pl.ds(pl.multiple_of(j * BLOCK, BLOCK), BLOCK), :]
        own = doccol[pl.ds(pl.multiple_of(8 + base, 8), BLOCK), :]
        own = jnp.concatenate([own, own], axis=1)
        theirs = jnp.concatenate([small[2 * j, 18:19, :], small[2 * j + 1, 18:19, :]], axis=1)
        allowed = (own == theirs) & (ahead >= (j - i) * BLOCK)
        for h in range(2):
            part = pl.ds(h * BLOCK, BLOCK)
            s = jnp.where(allowed, dot(q2[part, :], keys, NT), FAR)
            s_ref[j - first, part, :] = s
            m_ref[part, :] = jnp.maximum(m_ref[part, :], jnp.maximum(s[:, :ROWS], s[:, ROWS:]))
        return 0

    lax.fori_loop(first, i + 1, scores, 0)
    m_ref[...] = jnp.broadcast_to(jnp.max(m_ref[...], axis=1, keepdims=True), m_ref.shape)

    def exps(j, _):
        for h in range(2):
            part = pl.ds(h * BLOCK, BLOCK)
            m = m_ref[part, :]
            e = jnp.exp((s_ref[j - first, part, :] - jnp.concatenate([m, m], axis=1)) * SCALE)
            s_ref[j - first, part, :] = e
            l_ref[part, :] += e[:, :ROWS] + e[:, ROWS:]
        return 0

    lax.fori_loop(first, i + 1, exps, 0)
    l_ref[...] = jnp.broadcast_to(1.0 / jnp.sum(l_ref[...], axis=1, keepdims=True), l_ref.shape)

    def grads(j, _):
        there = pl.ds(pl.multiple_of(j * BLOCK, BLOCK), BLOCK)
        keys, vals = k[there, :], v[there, :]
        probs, scaled = [], []
        for h in range(2):
            part = pl.ds(h * BLOCK, BLOCK)
            inv = l_ref[part, :]
            p = s_ref[j - first, part, :] * jnp.concatenate([inv, inv], axis=1)
            delta = dcol[rows, h * ROWS : (h + 1) * ROWS]
            dp = dot(d2[part, :], vals, NT) - jnp.concatenate([delta, delta], axis=1)
            ds = (p * dp * SCALE).astype(BF16)
            dq[part, :] += dot(ds, keys, NN)
            probs.append(p.astype(BF16))
            scaled.append(ds)
        dk[there, :] += dot(jnp.concatenate(scaled, axis=0), q2[...], TN)
        dv[there, :] += dot(jnp.concatenate(probs, axis=0), d2[...], TN)
        return 0

    lax.fori_loop(first, i + 1, grads, 0)
    cot[:, :HEAD_DIM] = dq[:BLOCK, :].astype(BF16)
    cot[:, HEAD_DIM:] = dq[BLOCK:, :].astype(BF16)


def spread_matrix(spread):
    row = lax.broadcasted_iota(jnp.int32, spread.shape, 0)
    lane = lax.broadcasted_iota(jnp.int32, spread.shape, 1)
    head = row % OWN
    a = (lane < 1024) & (row < 24) & (lane // ROWS == head)
    b = (lane >= 1024) & (lane < 1280) & (row < 24) & ((lane - 1024) // SSM_DIM == head)
    c = (lane >= 1280) & (row >= 24) & ((lane - 1280) // SSM_DIM == head)
    spread[...] = jnp.where(a | b | c, 1.0, 0.0).astype(BF16)


def ssm_chunk(c, at, x, b, cm, small, doccol, cot, skip, spread, gstate, gtimed, acc_a, acc_s, dx):
    base = pl.multiple_of(c * ROWS, ROWS)
    here = pl.ds(base, ROWS)
    bc, cc = b[here, :], cm[here, :]
    xc = x[here, :].astype(F32)
    dyb = cot[at : at + ROWS, :]
    dy = dyb.astype(F32)
    steps, totals = small[c, 0:8, :], small[c, 8:16, :]
    parts = jnp.concatenate([p.astype(F32) for p in three(totals) + three(steps)], axis=0).astype(BF16)
    wide = dot(parts, spread[...], TN)
    te, se = wide[:, 1024:1280], wide[:, 1280:1536]
    docs = doccol[pl.ds(pl.multiple_of(8 + base, 8), ROWS), :]
    before = doccol[pl.ds(7 + base, 1), :]
    last = doccol[pl.ds(7 + ROWS + base, 1), :]
    docrow = small[c, 18:19, :]
    sub = lax.broadcasted_iota(jnp.int32, (ROWS, ROWS), 0)
    lane = lax.broadcasted_iota(jnp.int32, (ROWS, ROWS), 1)
    inner = jnp.where((sub <= lane) & (docs == docrow), dot(bc, cc, NT), 0.0)

    plain, timed = [], []
    for half in range(2):
        dyh = dyb[:, half * 128 : half * 128 + 128]
        total = None
        for pair in range(2):
            tops, lows, rights = [], [], []
            for one in range(2):
                local = 2 * pair + one
                h = 4 * half + local
                gap = totals[h : h + 1, :] - wide[:, ROWS * h : ROWS * h + ROWS]
                w = inner * jnp.exp(gap)
                tops.append(w.astype(BF16))
                lows.append((w * gap).astype(BF16))
                rights.append(jnp.where(lane // SSM_DIM == local, dyh.astype(F32), 0.0).astype(BF16))
            left = jnp.concatenate([jnp.concatenate(tops, axis=1), jnp.concatenate(lows, axis=1)], axis=0)
            out = dot(left, jnp.concatenate(rights, axis=0), NN)
            total = out if total is None else total + out
        plain.append(total[:ROWS])
        timed.append(total[ROWS:])
    intra = jnp.concatenate(plain, axis=1)
    intra_t = jnp.concatenate(timed, axis=1)

    both = jnp.concatenate([gstate[...], gtimed[...]], axis=1).astype(BF16)
    inter = dot(bc, both, NN)
    te_last = te[ROWS - 1 : ROWS, :]
    docs2 = jnp.concatenate([docs, docs], axis=1)
    before2 = jnp.concatenate([before, before], axis=1)
    last2 = jnp.concatenate([last, last], axis=1)
    left_time = te_last - te
    leave = jnp.where(docs2 == last2, jnp.exp(left_time), 0.0)
    got = intra + leave * inter[:, :WIDTH]
    got_t = intra_t + leave * (left_time * inter[:, :WIDTH] + inter[:, WIDTH:])
    dx[here, :] = (se * got + skip[...] * dy).astype(BF16)
    acc_a[...] += se * xc * got_t
    acc_s[...] += dy * xc

    enter = jnp.where(docs2 == before2, jnp.exp(te), 0.0)
    dye = dy * enter
    fresh = dot(cc, jnp.concatenate([dye, dye * te], axis=1).astype(BF16), TN)
    whole = jnp.where(last2 == before2, jnp.exp(te_last), 0.0)
    old = gstate[...]
    gtimed[...] = whole * (gtimed[...] + te_last * old) + fresh[:, WIDTH:]
    gstate[...] = whole * old + fresh[:, :WIDTH]


def finish_decay(me, acc_a, acc_s):
    sums = jnp.concatenate(
        [jnp.sum(acc_a[...], axis=0, keepdims=True), jnp.sum(acc_s[...], axis=0, keepdims=True), jnp.zeros((6, WIDTH), F32)],
        axis=0,
    )
    lane = lax.broadcasted_iota(jnp.int32, (WIDTH, SSM_HEADS), 0)
    head = lax.broadcasted_iota(jnp.int32, (WIDTH, SSM_HEADS), 1)
    place = jnp.where(lane // SSM_DIM + me * OWN == head, 1.0, 0.0)
    return dot(sums, place, NN, HIGHEST)


def compute_kernel(q, d, k, v, x, b, c, small, skip, dx, gk, gv, decay,
                   dk, dv, cot, q2, d2, s_ref, m_ref, l_ref, dq, dcol, doccol, spread, gstate, gtimed, acc_a, acc_s):
    me = lax.axis_index("ctx")
    for ref in (dk, dv, gstate, gtimed, acc_a, acc_s):
        ref[...] = jnp.zeros(ref.shape, F32)
    spread_columns(small, dcol, doccol)
    spread_matrix(spread)

    def step(n, _):
        i = SEQ // BLOCK - 1 - n
        attention_block(i, q, d, k, v, small, dcol, doccol, dk, dv, cot, q2, d2, s_ref, m_ref, l_ref, dq)
        for sub in (1, 0):
            ssm_chunk(2 * i + sub, sub * ROWS, x, b, c, small, doccol, cot, skip, spread, gstate, gtimed, acc_a, acc_s, dx)
        return 0

    lax.fori_loop(0, SEQ // BLOCK, step, 0)
    gk[...] = dk[...].astype(BF16)
    gv[...] = dv[...].astype(BF16)
    decay[...] = finish_decay(me, acc_a, acc_s)


COMPUTE_SCRATCH = [
    pltpu.VMEM((SEQ, HEAD_DIM), F32),
    pltpu.VMEM((SEQ, HEAD_DIM), F32),
    pltpu.VMEM((BLOCK, WIDTH), BF16),
    pltpu.VMEM((2 * BLOCK, HEAD_DIM), BF16),
    pltpu.VMEM((2 * BLOCK, HEAD_DIM), BF16),
    pltpu.VMEM((SPAN, 2 * BLOCK, BLOCK), F32),
    pltpu.VMEM((2 * BLOCK, ROWS), F32),
    pltpu.VMEM((2 * BLOCK, ROWS), F32),
    pltpu.VMEM((2 * BLOCK, HEAD_DIM), F32),
    pltpu.VMEM((SEQ, 2 * ROWS), F32),
    pltpu.VMEM((SEQ + 8, ROWS), F32),
    pltpu.VMEM((48, 1536), BF16),
    pltpu.VMEM((STATE, WIDTH), F32),
    pltpu.VMEM((STATE, WIDTH), F32),
    pltpu.VMEM((ROWS, WIDTH), F32),
    pltpu.VMEM((ROWS, WIDTH), F32),
]


def compute(q, d, k, v, x, b, c, small, skip):
    vmem = pl.BlockSpec(memory_space=pltpu.VMEM)
    return pl.pallas_call(
        compute_kernel,
        out_shape=[
            jax.ShapeDtypeStruct((SEQ, WIDTH), BF16),
            jax.ShapeDtypeStruct((SEQ, HEAD_DIM), BF16),
            jax.ShapeDtypeStruct((SEQ, HEAD_DIM), BF16),
            jax.ShapeDtypeStruct((8, SSM_HEADS), F32),
        ],
        in_specs=[vmem] * 9,
        out_specs=[vmem] * 4,
        scratch_shapes=COMPUTE_SCRATCH,
        compiler_params=pltpu.CompilerParams(vmem_limit_bytes=48 * 2**20),
        name="head_gradients",
    )(q, d, k, v, x, b, c, small, skip)


def out_moves(peer, place, arrays, landed):
    dx, gk, gv, decay = arrays
    lx, lk, lv, ld = landed
    early = pl.ds(pl.multiple_of(peer * HALF, HALF), HALF)
    late = pl.ds(pl.multiple_of((2 * CTX - 1 - peer) * HALF, HALF), HALF)
    here = pl.ds(pl.multiple_of(peer * ROWS, ROWS), ROWS)
    wide = pl.ds(pl.multiple_of(place * WIDTH, WIDTH), WIDTH)
    first, second = pl.ds(0, HALF), pl.ds(HALF, HALF)
    moves = []
    for src, dst in ((gk, lk), (gv, lv)):
        moves.append((src.at[late, :], dst.at[place, second, :]))
        moves.append((src.at[early, :], dst.at[place, first, :]))
    moves.append((dx.at[here, :], lx.at[0, :, wide]))
    moves.append((decay, ld.at[place]))
    return moves


OUT_KINDS = 6


def out_kernel(dx, gk, gv, decay, grad_x, grad_k, grad_v, grad_d,
               lk, lv, ld, seq_decay, all_decay, send_sem, recv_sem, own_sem, dp_send, dp_recv, dp_own):
    me = lax.axis_index("ctx")
    row = lax.axis_index("dp")
    arrays, landed = (dx, gk, gv, decay), (grad_x, lk, lv, ld)
    greet("ctx", CTX)
    greet("dp", DP)
    await_greetings(CTX - 1 + DP - 1)

    def send(off, _):
        to = lax.rem(me + off, CTX)
        for kind, (src, dst) in enumerate(out_moves(to, me, arrays, landed)):
            pltpu.make_async_remote_copy(
                src_ref=src, dst_ref=dst, send_sem=send_sem.at[kind, to], recv_sem=recv_sem.at[kind, me],
                device_id={"ctx": to}, device_id_type=MESH,
            ).start()
        return 0

    lax.fori_loop(1, CTX, send, 0)
    own = [pltpu.make_async_copy(src, dst, own_sem.at[kind])
           for kind, (src, dst) in enumerate(out_moves(me, me, arrays, landed))]
    for copy in own:
        copy.start()

    def finish(off, kinds):
        to = lax.rem(me + off, CTX)
        frm = lax.rem(me + CTX - off, CTX)
        gone = out_moves(to, me, arrays, landed)
        come = out_moves(me, frm, arrays, landed)
        for kind in kinds:
            pltpu.make_async_remote_copy(
                src_ref=gone[kind][0], dst_ref=gone[kind][1], send_sem=send_sem.at[kind, to],
                recv_sem=recv_sem.at[kind, frm], device_id={"ctx": to}, device_id_type=MESH,
            ).wait_send()
            pltpu.make_async_remote_copy(
                src_ref=come[kind][0], dst_ref=come[kind][1], send_sem=send_sem.at[kind, to],
                recv_sem=recv_sem.at[kind, frm], device_id={"ctx": to}, device_id_type=MESH,
            ).wait_recv()

    lax.fori_loop(1, CTX, lambda off, _: (finish(off, (5,)), 0)[1], 0)
    own[5].wait()
    seq_decay[...] = jnp.sum(ld[...], axis=0)

    def dp_copy(to, frm):
        return pltpu.make_async_remote_copy(
            src_ref=seq_decay, dst_ref=all_decay.at[frm], send_sem=dp_send.at[to], recv_sem=dp_recv.at[frm],
            device_id={"dp": to}, device_id_type=MESH,
        )

    lax.fori_loop(1, DP, lambda off, _: (dp_copy(lax.rem(row + off, DP), row).start(), 0)[1], 0)
    mine = pltpu.make_async_copy(seq_decay, all_decay.at[row], dp_own)
    mine.start()

    lax.fori_loop(1, CTX, lambda off, _: (finish(off, (0, 1, 2, 3, 4)), 0)[1], 0)
    for copy in own[:5]:
        copy.wait()
    for group in range(KVHEADS):
        cols = pl.ds(group * HEAD_DIM, HEAD_DIM)
        for src, dst in ((lk, grad_k), (lv, grad_v)):
            total = src[4 * group].astype(F32)
            for other in range(1, 4):
                total += src[4 * group + other].astype(F32)
            dst[0, :, cols] = total.astype(BF16)

    def dp_finish(off, _):
        copy = dp_copy(lax.rem(row + off, DP), lax.rem(row + DP - off, DP))
        copy.wait_send()
        copy.wait_recv()
        return 0

    lax.fori_loop(1, DP, dp_finish, 0)
    mine.wait()
    total = all_decay[0]
    for other in range(1, DP):
        total += all_decay[other]
    grad_d[...] = total[:2]


def exchange_out(dx, gk, gv, decay):
    hbm = pl.BlockSpec(memory_space=pl.ANY)
    vmem = pl.BlockSpec(memory_space=pltpu.VMEM)
    return pl.pallas_call(
        out_kernel,
        out_shape=[
            jax.ShapeDtypeStruct((1, ROWS, SSM_HEADS * SSM_DIM), BF16),
            jax.ShapeDtypeStruct((1, ROWS, KVHEADS * HEAD_DIM), BF16),
            jax.ShapeDtypeStruct((1, ROWS, KVHEADS * HEAD_DIM), BF16),
            jax.ShapeDtypeStruct((2, SSM_HEADS), F32),
        ],
        in_specs=[hbm] * 4,
        out_specs=[hbm, vmem, vmem, vmem],
        scratch_shapes=[
            pltpu.VMEM((CTX, ROWS, HEAD_DIM), BF16),
            pltpu.VMEM((CTX, ROWS, HEAD_DIM), BF16),
            pltpu.VMEM((CTX, 8, SSM_HEADS), F32),
            pltpu.VMEM((8, SSM_HEADS), F32),
            pltpu.VMEM((DP, 8, SSM_HEADS), F32),
            pltpu.SemaphoreType.DMA((OUT_KINDS, CTX)),
            pltpu.SemaphoreType.DMA((OUT_KINDS, CTX)),
            pltpu.SemaphoreType.DMA((OUT_KINDS,)),
            pltpu.SemaphoreType.DMA((DP,)),
            pltpu.SemaphoreType.DMA((DP,)),
            pltpu.SemaphoreType.DMA,
        ],
        compiler_params=pltpu.CompilerParams(
            collective_id=1, has_side_effects=True, vmem_limit_bytes=32 * 2**20
        ),
        name="exchange_out",
    )(dx, gk, gv, decay)


def shards(queries, keys, values, saved, out_grad, doc_ids, inputs, bmat, cmat, step, alog, skip):
    device = lax.axis_index("ctx")
    own_skip = jnp.repeat(lax.dynamic_slice_in_dim(skip, device * OWN, OWN), SSM_DIM)[None]
    landed = exchange_in(queries, keys, values, saved, out_grad, doc_ids, inputs, bmat, cmat, step, alog[None])
    dx, gk, gv, decay = compute(*landed, own_skip)
    grad_x, grad_k, grad_v, grad_d = exchange_out(dx, gk, gv, decay)
    return (grad_k, grad_v, grad_x, grad_d)


def solution(mesh):
    return jax.shard_map(
        shards,
        mesh=mesh,
        in_specs=(
            P("dp", "ctx", None),
            P("dp", "ctx", None),
            P("dp", "ctx", None),
            P("dp", "ctx", None),
            P("dp", "ctx", None),
            P("dp", "ctx"),
            P("dp", "ctx", None),
            P("dp", "ctx", None),
            P("dp", "ctx", None),
            P("dp", "ctx", None),
            P(),
            P(),
        ),
        out_specs=(P("dp", "ctx", None), P("dp", "ctx", None), P("dp", "ctx", None), P()),
        check_vma=False,
    )
```

```python
import jax
import jax.numpy as jnp
from jax import lax
from jax.experimental import pallas as pl
from jax.experimental.pallas import tpu as pltpu
from jax.sharding import PartitionSpec as P

QHEADS = 32
KVHEADS = 4
HEAD_DIM = 128
SSM_HEADS = 128
SSM_DIM = 32
STATE = 128
SEQ = 2048
ROWS = 128
HALF = 64
CTX = 16
DP = 8
WIDTH = 256
OWN = 8
BLOCK = 256
SPAN = 5
SCALE = HEAD_DIM ** (-0.5)
FAR = -1e30

MESH = pl.DeviceIdType.MESH
HIGHEST = lax.Precision.HIGHEST
F32 = jnp.float32
BF16 = jnp.bfloat16


def dot(a, b, dims, precision=None):
    return lax.dot_general(a, b, (dims, ((), ())), precision=precision, preferred_element_type=F32)


NN = ((1,), (0,))
NT = ((1,), (1,))
TN = ((0,), (0,))


def three(a):
    high = a.astype(BF16)
    rest = a - high.astype(F32)
    mid = rest.astype(BF16)
    low = (rest - mid.astype(F32)).astype(BF16)
    return high, mid, low


def greet(axis, count):
    me = lax.axis_index(axis)
    barrier = pltpu.get_barrier_semaphore()

    def one(off, _):
        pl.semaphore_signal(barrier, inc=1, device_id={axis: lax.rem(me + off, count)}, device_id_type=MESH)
        return 0

    lax.fori_loop(1, count, one, 0)


def await_greetings(total):
    pl.semaphore_wait(pltpu.get_barrier_semaphore(), total)


def pack_small(out_grad, saved, ids, step, alog, small):
    ones = jnp.ones((8, HEAD_DIM), F32)
    sub = lax.broadcasted_iota(jnp.int32, (8, ROWS), 0)
    docs = jnp.broadcast_to(ids[...].astype(F32), (8, ROWS))
    rate = step[0] * -jnp.exp(alog[...])
    upto = lax.broadcasted_iota(jnp.int32, (ROWS, ROWS), 0) <= lax.broadcasted_iota(jnp.int32, (ROWS, ROWS), 1)
    totals = dot(rate, upto.astype(F32), TN, HIGHEST)
    steps = step[0].T
    for j in range(CTX):
        small[j, 0:8, :] = steps[8 * j : 8 * j + 8]
        small[j, 8:16, :] = totals[8 * j : 8 * j + 8]

    def one(j, _):
        deltas = []
        for h in range(2):
            cols = pl.ds(pl.multiple_of(WIDTH * j + HEAD_DIM * h, HEAD_DIM), HEAD_DIM)
            product = out_grad[0, :, cols].astype(F32) * saved[0, :, cols].astype(F32)
            deltas.append(dot(ones, product, NT, HIGHEST))
        small[j, 16:24, :] = jnp.where(sub == 0, deltas[0], jnp.where(sub == 1, deltas[1], docs))
        return 0

    lax.fori_loop(0, CTX, one, 0)


def in_moves(peer, place, arrays, landed):
    q, d, k, v, x, b, c, small = arrays
    lq, ld, lk, lv, lx, lb, lc, ls = landed
    wide = pl.ds(pl.multiple_of(peer * WIDTH, WIDTH), WIDTH)
    narrow = pl.ds(pl.multiple_of(peer // 4 * HEAD_DIM, HEAD_DIM), HEAD_DIM)
    early = pl.ds(pl.multiple_of(place * HALF, HALF), HALF)
    late = pl.ds(pl.multiple_of((2 * CTX - 1 - place) * HALF, HALF), HALF)
    here = pl.ds(pl.multiple_of(place * ROWS, ROWS), ROWS)
    first, second = pl.ds(0, HALF), pl.ds(HALF, HALF)
    moves = []
    for src, dst in ((k, lk), (v, lv)):
        moves.append((src.at[0, second, narrow], dst.at[late, :]))
        moves.append((src.at[0, first, narrow], dst.at[early, :]))
    for src, dst in ((q, lq), (d, ld)):
        moves.append((src.at[0, second, wide], dst.at[late, :]))
    for src, dst in ((q, lq), (d, ld)):
        moves.append((src.at[0, first, wide], dst.at[early, :]))
    for src, dst in ((b, lb), (c, lc)):
        moves.append((src.at[0, :, narrow], dst.at[here, :]))
    moves.append((x.at[0, :, wide], lx.at[here, :]))
    moves.append((small.at[peer], ls.at[place]))
    return moves


KV_KINDS = (0, 1, 2, 3)
LATE_KINDS = (4, 5)
EARLY_KINDS = (6, 7)
SSM_KINDS = (8, 9, 10)
SMALL_KIND = 11
KINDS = 12


def spread_columns(small, dcol, doccol):
    row = lax.broadcasted_iota(jnp.int32, (24, 3 * ROWS), 0) % 8
    lane = lax.broadcasted_iota(jnp.int32, (24, 3 * ROWS), 1) // ROWS
    pick = jnp.where(row == lane, 1.0, 0.0).astype(BF16)
    doccol[0:8, :] = jnp.full((8, ROWS), -1.0, F32)

    def one(src, _):
        parts = jnp.concatenate([p.astype(F32) for p in three(small[src, 16:24, :])], axis=0).astype(BF16)
        wide = dot(parts, pick, TN)
        early = pl.multiple_of(src * HALF, HALF)
        late = pl.multiple_of((2 * CTX - 1 - src) * HALF, HALF)
        dcol[pl.ds(early, HALF), :] = wide[:HALF, : 2 * ROWS]
        dcol[pl.ds(late, HALF), :] = wide[HALF:, : 2 * ROWS]
        doccol[pl.ds(pl.multiple_of(8 + src * ROWS, 8), ROWS), :] = wide[:, 2 * ROWS :]
        return 0

    lax.fori_loop(0, CTX, one, 0)


def attention_block(i, q, d, k, v, small, dcol, doccol, dk, dv, cot, q2, d2, s_ref, m_ref, l_ref, dq):
    base = pl.multiple_of(i * BLOCK, BLOCK)
    rows = pl.ds(base, BLOCK)
    q2[:BLOCK, :] = q[rows, :HEAD_DIM]
    q2[BLOCK:, :] = q[rows, HEAD_DIM:]
    d2[:BLOCK, :] = d[rows, :HEAD_DIM]
    d2[BLOCK:, :] = d[rows, HEAD_DIM:]
    m_ref[...] = jnp.full(m_ref.shape, FAR, F32)
    l_ref[...] = jnp.zeros(l_ref.shape, F32)
    dq[...] = jnp.zeros(dq.shape, F32)
    first = jnp.maximum(i - (SPAN - 1), 0)
    ahead = lax.broadcasted_iota(jnp.int32, (BLOCK, BLOCK), 0) - lax.broadcasted_iota(jnp.int32, (BLOCK, BLOCK), 1)

    def scores(j, _):
        keys = k[pl.ds(pl.multiple_of(j * BLOCK, BLOCK), BLOCK), :]
        own = doccol[pl.ds(pl.multiple_of(8 + base, 8), BLOCK), :]
        own = jnp.concatenate([own, own], axis=1)
        theirs = jnp.concatenate([small[2 * j, 18:19, :], small[2 * j + 1, 18:19, :]], axis=1)
        allowed = (own == theirs) & (ahead >= (j - i) * BLOCK)
        for h in range(2):
            part = pl.ds(h * BLOCK, BLOCK)
            s = jnp.where(allowed, dot(q2[part, :], keys, NT), FAR)
            s_ref[j - first, part, :] = s
            m_ref[part, :] = jnp.maximum(m_ref[part, :], jnp.maximum(s[:, :ROWS], s[:, ROWS:]))
        return 0

    lax.fori_loop(first, i + 1, scores, 0)
    m_ref[...] = jnp.broadcast_to(jnp.max(m_ref[...], axis=1, keepdims=True), m_ref.shape)

    def exps(j, _):
        for h in range(2):
            part = pl.ds(h * BLOCK, BLOCK)
            m = m_ref[part, :]
            e = jnp.exp((s_ref[j - first, part, :] - jnp.concatenate([m, m], axis=1)) * SCALE)
            s_ref[j - first, part, :] = e
            l_ref[part, :] += e[:, :ROWS] + e[:, ROWS:]
        return 0

    lax.fori_loop(first, i + 1, exps, 0)
    l_ref[...] = jnp.broadcast_to(1.0 / jnp.sum(l_ref[...], axis=1, keepdims=True), l_ref.shape)

    def grads(j, _):
        there = pl.ds(pl.multiple_of(j * BLOCK, BLOCK), BLOCK)
        keys, vals = k[there, :], v[there, :]
        probs, scaled = [], []
        for h in range(2):
            part = pl.ds(h * BLOCK, BLOCK)
            inv = l_ref[part, :]
            p = s_ref[j - first, part, :] * jnp.concatenate([inv, inv], axis=1)
            delta = dcol[rows, h * ROWS : (h + 1) * ROWS]
            dp = dot(d2[part, :], vals, NT) - jnp.concatenate([delta, delta], axis=1)
            ds = (p * dp * SCALE).astype(BF16)
            dq[part, :] += dot(ds, keys, NN)
            probs.append(p.astype(BF16))
            scaled.append(ds)
        dk[there, :] += dot(jnp.concatenate(scaled, axis=0), q2[...], TN)
        dv[there, :] += dot(jnp.concatenate(probs, axis=0), d2[...], TN)
        return 0

    lax.fori_loop(first, i + 1, grads, 0)
    cot[:, :HEAD_DIM] = dq[:BLOCK, :].astype(BF16)
    cot[:, HEAD_DIM:] = dq[BLOCK:, :].astype(BF16)


def spread_matrix(spread):
    row = lax.broadcasted_iota(jnp.int32, spread.shape, 0)
    lane = lax.broadcasted_iota(jnp.int32, spread.shape, 1)
    head = row % OWN
    a = (lane < 1024) & (row < 24) & (lane // ROWS == head)
    b = (lane >= 1024) & (lane < 1280) & (row < 24) & ((lane - 1024) // SSM_DIM == head)
    c = (lane >= 1280) & (row >= 24) & ((lane - 1280) // SSM_DIM == head)
    spread[...] = jnp.where(a | b | c, 1.0, 0.0).astype(BF16)


def ssm_chunk(c, at, x, b, cm, small, doccol, cot, skip, spread, gstate, gtimed, acc_a, acc_s, dx):
    base = pl.multiple_of(c * ROWS, ROWS)
    here = pl.ds(base, ROWS)
    bc, cc = b[here, :], cm[here, :]
    xc = x[here, :].astype(F32)
    dyb = cot[at : at + ROWS, :]
    dy = dyb.astype(F32)
    steps, totals = small[c, 0:8, :], small[c, 8:16, :]
    parts = jnp.concatenate([p.astype(F32) for p in three(totals) + three(steps)], axis=0).astype(BF16)
    wide = dot(parts, spread[...], TN)
    te, se = wide[:, 1024:1280], wide[:, 1280:1536]
    docs = doccol[pl.ds(pl.multiple_of(8 + base, 8), ROWS), :]
    before = doccol[pl.ds(7 + base, 1), :]
    last = doccol[pl.ds(7 + ROWS + base, 1), :]
    docrow = small[c, 18:19, :]
    sub = lax.broadcasted_iota(jnp.int32, (ROWS, ROWS), 0)
    lane = lax.broadcasted_iota(jnp.int32, (ROWS, ROWS), 1)
    inner = jnp.where((sub <= lane) & (docs == docrow), dot(bc, cc, NT), 0.0)

    plain, timed = [], []
    for half in range(2):
        dyh = dyb[:, half * 128 : half * 128 + 128]
        total = None
        for pair in range(2):
            tops, lows, rights = [], [], []
            for one in range(2):
                local = 2 * pair + one
                h = 4 * half + local
                gap = totals[h : h + 1, :] - wide[:, ROWS * h : ROWS * h + ROWS]
                w = inner * jnp.exp(gap)
                tops.append(w.astype(BF16))
                lows.append((w * gap).astype(BF16))
                rights.append(jnp.where(lane // SSM_DIM == local, dyh.astype(F32), 0.0).astype(BF16))
            left = jnp.concatenate([jnp.concatenate(tops, axis=1), jnp.concatenate(lows, axis=1)], axis=0)
            out = dot(left, jnp.concatenate(rights, axis=0), NN)
            total = out if total is None else total + out
        plain.append(total[:ROWS])
        timed.append(total[ROWS:])
    intra = jnp.concatenate(plain, axis=1)
    intra_t = jnp.concatenate(timed, axis=1)

    both = jnp.concatenate([gstate[...], gtimed[...]], axis=1).astype(BF16)
    inter = dot(bc, both, NN)
    te_last = te[ROWS - 1 : ROWS, :]
    docs2 = jnp.concatenate([docs, docs], axis=1)
    before2 = jnp.concatenate([before, before], axis=1)
    last2 = jnp.concatenate([last, last], axis=1)
    left_time = te_last - te
    leave = jnp.where(docs2 == last2, jnp.exp(left_time), 0.0)
    got = intra + leave * inter[:, :WIDTH]
    got_t = intra_t + leave * (left_time * inter[:, :WIDTH] + inter[:, WIDTH:])
    dx[here, :] = (se * got + skip[...] * dy).astype(BF16)
    acc_a[...] += se * xc * got_t
    acc_s[...] += dy * xc

    enter = jnp.where(docs2 == before2, jnp.exp(te), 0.0)
    dye = dy * enter
    fresh = dot(cc, jnp.concatenate([dye, dye * te], axis=1).astype(BF16), TN)
    whole = jnp.where(last2 == before2, jnp.exp(te_last), 0.0)
    old = gstate[...]
    gtimed[...] = whole * (gtimed[...] + te_last * old) + fresh[:, WIDTH:]
    gstate[...] = whole * old + fresh[:, :WIDTH]


def finish_decay(me, acc_a, acc_s):
    sums = jnp.concatenate(
        [jnp.sum(acc_a[...], axis=0, keepdims=True), jnp.sum(acc_s[...], axis=0, keepdims=True), jnp.zeros((6, WIDTH), F32)],
        axis=0,
    )
    lane = lax.broadcasted_iota(jnp.int32, (WIDTH, SSM_HEADS), 0)
    head = lax.broadcasted_iota(jnp.int32, (WIDTH, SSM_HEADS), 1)
    place = jnp.where(lane // SSM_DIM + me * OWN == head, 1.0, 0.0)
    return dot(sums, place, NN, HIGHEST)


def kernel(q, d, k, v, x, b, c, dvm, o, ids, step, alog, skip,
           grad_x, grad_k, grad_v, grad_d,
           lq, ld, lk, lv, lx, lb, lc, ls, small, send_sem, recv_sem, own_sem,
           dk, dv, cot, q2, d2, s_ref, m_ref, l_ref, dq, dcol, doccol, spread, gstate, gtimed, acc_a, acc_s,
           dx, stage, terms, kv_send, kv_recv, x_send, x_recv, kv_own, x_own,
           decay, ctx_decay, seq_decay, all_decay, ctx_send, ctx_recv, ctx_own, dp_send, dp_recv, dp_own):
    me = lax.axis_index("ctx")
    row = lax.axis_index("dp")
    arrays = (q, d, k, v, x, b, c, small)
    landed = (lq, ld, lk, lv, lx, lb, lc, ls)

    def in_copy(kind, to, frm, peer):
        src, dst = in_moves(to, frm, arrays, landed)[kind]
        return pltpu.make_async_remote_copy(
            src_ref=src, dst_ref=dst, send_sem=send_sem.at[kind, peer], recv_sem=recv_sem.at[kind, frm],
            device_id={"ctx": peer}, device_id_type=MESH,
        )

    def send(kinds):
        def one(off, _):
            to = lax.rem(me + off, CTX)
            for kind in kinds:
                in_copy(kind, to, me, to).start()
            return 0

        lax.fori_loop(1, CTX, one, 0)

    def own(kinds):
        for kind in kinds:
            src, dst = in_moves(me, me, arrays, landed)[kind]
            yield pltpu.make_async_copy(src, dst, own_sem.at[kind])

    def arrived(src, kinds):
        @pl.when(src != me)
        def _():
            for kind in kinds:
                in_copy(kind, me, src, src).wait_recv()

    greet("ctx", CTX)
    greet("dp", DP)
    await_greetings(CTX - 1 + DP - 1)
    send(KV_KINDS)
    for copy in own(range(KINDS - 1)):
        copy.start()
    pack_small(dvm, o, ids, step, alog, small)
    send((SMALL_KIND,))
    for copy in own((SMALL_KIND,)):
        copy.start()
    send(LATE_KINDS)

    @pl.when(me >= CTX // 2)
    def _():
        send(SSM_KINDS)

    send(EARLY_KINDS)

    @pl.when(me < CTX // 2)
    def _():
        send(SSM_KINDS)

    for ref in (dk, dv, gstate, gtimed, acc_a, acc_s):
        ref[...] = jnp.zeros(ref.shape, F32)
    spread_matrix(spread)
    for copy in own(range(KINDS)):
        copy.wait()

    def first(src, _):
        arrived(src, KV_KINDS + (SMALL_KIND,))
        return 0

    lax.fori_loop(0, CTX, first, 0)
    spread_columns(ls, dcol, doccol)

    def kv_place(late, owner):
        return pl.ds(pl.multiple_of((owner + late * (2 * CTX - 1 - 2 * owner)) * HALF, HALF), HALF)

    def kv_copy(which, late, owner, place, peer):
        return pltpu.make_async_remote_copy(
            src_ref=stage.at[which, kv_place(late, owner), :],
            dst_ref=terms.at[which, place, pl.ds(pl.multiple_of(late * HALF, HALF), HALF), :],
            send_sem=kv_send.at[which, late, peer], recv_sem=kv_recv.at[which, late, place],
            device_id={"ctx": peer}, device_id_type=MESH,
        )

    def kv_mine(which, late):
        return pltpu.make_async_copy(
            stage.at[which, kv_place(late, me), :],
            terms.at[which, me, pl.ds(pl.multiple_of(late * HALF, HALF), HALF), :],
            kv_own.at[which, late],
        )

    def x_copy(owner, place, peer):
        return pltpu.make_async_remote_copy(
            src_ref=dx.at[pl.ds(pl.multiple_of(owner * ROWS, ROWS), ROWS), :],
            dst_ref=grad_x.at[0, :, pl.ds(pl.multiple_of(place * WIDTH, WIDTH), WIDTH)],
            send_sem=x_send.at[peer], recv_sem=x_recv.at[place],
            device_id={"ctx": peer}, device_id_type=MESH,
        )

    def x_mine():
        return pltpu.make_async_copy(
            dx.at[pl.ds(pl.multiple_of(me * ROWS, ROWS), ROWS), :],
            grad_x.at[0, :, pl.ds(pl.multiple_of(me * WIDTH, WIDTH), WIDTH)],
            x_own,
        )

    def block(n, _):
        i = SEQ // BLOCK - 1 - n
        late = i // 4

        @pl.when(i >= 4)
        def _():
            for r in range(4):
                arrived(28 - 4 * i + r, LATE_KINDS)

        @pl.when(i < 4)
        def _():
            for r in range(4):
                arrived(4 * i + r, EARLY_KINDS)

        attention_block(i, lq, ld, lk, lv, ls, dcol, doccol, dk, dv, cot, q2, d2, s_ref, m_ref, l_ref, dq)
        rows = pl.ds(pl.multiple_of(i * BLOCK, BLOCK), BLOCK)
        stage[0, rows, :] = dk[rows, :].astype(BF16)
        stage[1, rows, :] = dv[rows, :].astype(BF16)
        for r in range(4):
            chunk = 4 * i + r
            owner = chunk + late * (2 * CTX - 1 - 2 * chunk)

            @pl.when(owner != me)
            def _():
                for which in range(2):
                    kv_copy(which, late, owner, me, owner).start()

            @pl.when(owner == me)
            def _():
                for which in range(2):
                    kv_mine(which, late).start()

        for sub in (1, 0):
            owner = 2 * i + sub
            arrived(owner, SSM_KINDS)
            ssm_chunk(owner, sub * ROWS, lx, lb, lc, ls, doccol, cot, skip, spread, gstate, gtimed, acc_a, acc_s, dx)

            @pl.when(owner != me)
            def _():
                x_copy(owner, me, owner).start()

            @pl.when(owner == me)
            def _():
                x_mine().start()

        return 0

    lax.fori_loop(0, SEQ // BLOCK, block, 0)

    decay[...] = finish_decay(me, acc_a, acc_s)

    def ctx_copy(frm, peer):
        return pltpu.make_async_remote_copy(
            src_ref=decay, dst_ref=ctx_decay.at[frm], send_sem=ctx_send.at[peer], recv_sem=ctx_recv.at[frm],
            device_id={"ctx": peer}, device_id_type=MESH,
        )

    def dp_copy(frm, peer):
        return pltpu.make_async_remote_copy(
            src_ref=seq_decay, dst_ref=all_decay.at[frm], send_sem=dp_send.at[peer], recv_sem=dp_recv.at[frm],
            device_id={"dp": peer}, device_id_type=MESH,
        )

    def start_ctx(off, _):
        to = lax.rem(me + off, CTX)
        ctx_copy(me, to).start()
        return 0

    lax.fori_loop(1, CTX, start_ctx, 0)
    ctx_mine = pltpu.make_async_copy(decay, ctx_decay.at[me], ctx_own)
    ctx_mine.start()

    def end_ctx(off, _):
        frm = lax.rem(me + CTX - off, CTX)
        ctx_copy(frm, frm).wait_recv()
        return 0

    lax.fori_loop(1, CTX, end_ctx, 0)
    ctx_mine.wait()
    seq_decay[...] = jnp.sum(ctx_decay[...], axis=0)

    def start_dp(off, _):
        to = lax.rem(row + off, DP)
        dp_copy(row, to).start()
        return 0

    lax.fori_loop(1, DP, start_dp, 0)
    dp_mine = pltpu.make_async_copy(seq_decay, all_decay.at[row], dp_own)
    dp_mine.start()

    def end_kv(off, _):
        frm = lax.rem(me + CTX - off, CTX)
        for which in range(2):
            for late in range(2):
                kv_copy(which, late, me, frm, frm).wait_recv()
        return 0

    lax.fori_loop(1, CTX, end_kv, 0)
    for which in range(2):
        for late in range(2):
            kv_mine(which, late).wait()
    for group in range(KVHEADS):
        cols = pl.ds(group * HEAD_DIM, HEAD_DIM)
        for which, dst in ((0, grad_k), (1, grad_v)):
            total = terms[which, 4 * group].astype(F32)
            for other in range(1, 4):
                total += terms[which, 4 * group + other].astype(F32)
            dst[0, :, cols] = total.astype(BF16)

    def end_dp(off, _):
        frm = lax.rem(row + DP - off, DP)
        dp_copy(frm, frm).wait_recv()
        return 0

    lax.fori_loop(1, DP, end_dp, 0)
    dp_mine.wait()
    total = all_decay[0]
    for other in range(1, DP):
        total += all_decay[other]
    grad_d[...] = total[:2]

    def end_x(off, _):
        frm = lax.rem(me + CTX - off, CTX)
        x_copy(me, frm, frm).wait_recv()
        return 0

    lax.fori_loop(1, CTX, end_x, 0)
    x_mine().wait()

    def sent(off, _):
        to = lax.rem(me + off, CTX)
        for kind in range(KINDS):
            in_copy(kind, to, me, to).wait_send()
        for which in range(2):
            for late in range(2):
                kv_copy(which, late, to, me, to).wait_send()
        x_copy(to, me, to).wait_send()
        ctx_copy(me, to).wait_send()
        return 0

    lax.fori_loop(1, CTX, sent, 0)

    def sent_dp(off, _):
        dp_copy(row, lax.rem(row + off, DP)).wait_send()
        return 0

    lax.fori_loop(1, DP, sent_dp, 0)


DMA = pltpu.SemaphoreType.DMA
SCRATCH = [
    pltpu.VMEM((SEQ, WIDTH), BF16),
    pltpu.VMEM((SEQ, WIDTH), BF16),
    pltpu.VMEM((SEQ, HEAD_DIM), BF16),
    pltpu.VMEM((SEQ, HEAD_DIM), BF16),
    pltpu.VMEM((SEQ, WIDTH), BF16),
    pltpu.VMEM((SEQ, STATE), BF16),
    pltpu.VMEM((SEQ, STATE), BF16),
    pltpu.VMEM((CTX, 24, ROWS), F32),
    pltpu.VMEM((CTX, 24, ROWS), F32),
    DMA((KINDS, CTX)),
    DMA((KINDS, CTX)),
    DMA((KINDS,)),
    pltpu.VMEM((SEQ, HEAD_DIM), F32),
    pltpu.VMEM((SEQ, HEAD_DIM), F32),
    pltpu.VMEM((BLOCK, WIDTH), BF16),
    pltpu.VMEM((2 * BLOCK, HEAD_DIM), BF16),
    pltpu.VMEM((2 * BLOCK, HEAD_DIM), BF16),
    pltpu.VMEM((SPAN, 2 * BLOCK, BLOCK), F32),
    pltpu.VMEM((2 * BLOCK, ROWS), F32),
    pltpu.VMEM((2 * BLOCK, ROWS), F32),
    pltpu.VMEM((2 * BLOCK, HEAD_DIM), F32),
    pltpu.VMEM((SEQ, 2 * ROWS), F32),
    pltpu.VMEM((SEQ + 8, ROWS), F32),
    pltpu.VMEM((48, 1536), BF16),
    pltpu.VMEM((STATE, WIDTH), F32),
    pltpu.VMEM((STATE, WIDTH), F32),
    pltpu.VMEM((ROWS, WIDTH), F32),
    pltpu.VMEM((ROWS, WIDTH), F32),
    pltpu.VMEM((SEQ, WIDTH), BF16),
    pltpu.VMEM((2, SEQ, HEAD_DIM), BF16),
    pltpu.VMEM((2, CTX, ROWS, HEAD_DIM), BF16),
    DMA((2, 2, CTX)),
    DMA((2, 2, CTX)),
    DMA((CTX,)),
    DMA((CTX,)),
    DMA((2, 2)),
    DMA,
    pltpu.VMEM((8, SSM_HEADS), F32),
    pltpu.VMEM((CTX, 8, SSM_HEADS), F32),
    pltpu.VMEM((8, SSM_HEADS), F32),
    pltpu.VMEM((DP, 8, SSM_HEADS), F32),
    DMA((CTX,)),
    DMA((CTX,)),
    DMA,
    DMA((DP,)),
    DMA((DP,)),
    DMA,
]


def gradients(q, k, v, o, d, ids, x, b, c, step, alog, skip):
    hbm = pl.BlockSpec(memory_space=pl.ANY)
    vmem = pl.BlockSpec(memory_space=pltpu.VMEM)
    return pl.pallas_call(
        kernel,
        out_shape=[
            jax.ShapeDtypeStruct((1, ROWS, SSM_HEADS * SSM_DIM), BF16),
            jax.ShapeDtypeStruct((1, ROWS, KVHEADS * HEAD_DIM), BF16),
            jax.ShapeDtypeStruct((1, ROWS, KVHEADS * HEAD_DIM), BF16),
            jax.ShapeDtypeStruct((2, SSM_HEADS), F32),
        ],
        in_specs=[hbm] * 7 + [vmem] * 6,
        out_specs=[hbm, vmem, vmem, vmem],
        scratch_shapes=SCRATCH,
        compiler_params=pltpu.CompilerParams(
            collective_id=0, has_side_effects=True, vmem_limit_bytes=60 * 2**20
        ),
        name="gradients",
    )(q, d, k, v, x, b, c, d, o, ids, step, alog, skip)


def shards(queries, keys, values, saved, out_grad, doc_ids, inputs, bmat, cmat, step, alog, skip):
    device = lax.axis_index("ctx")
    own_skip = jnp.repeat(lax.dynamic_slice_in_dim(skip, device * OWN, OWN), SSM_DIM)[None]
    grad_x, grad_k, grad_v, grad_d = gradients(
        queries, keys, values, saved, out_grad, doc_ids, inputs, bmat, cmat, step, alog[None], own_skip
    )
    return (grad_k, grad_v, grad_x, grad_d)


def solution(mesh):
    return jax.shard_map(
        shards,
        mesh=mesh,
        in_specs=(
            P("dp", "ctx", None),
            P("dp", "ctx", None),
            P("dp", "ctx", None),
            P("dp", "ctx", None),
            P("dp", "ctx", None),
            P("dp", "ctx"),
            P("dp", "ctx", None),
            P("dp", "ctx", None),
            P("dp", "ctx", None),
            P("dp", "ctx", None),
            P(),
            P(),
        ),
        out_specs=(P("dp", "ctx", None), P("dp", "ctx", None), P("dp", "ctx", None), P()),
        check_vma=False,
    )
```

```python
import jax
import jax.numpy as jnp
from jax import lax
from jax.experimental import pallas as pl
from jax.experimental.pallas import tpu as pltpu
from jax.sharding import PartitionSpec as P

QHEADS = 32
KVHEADS = 4
HEAD_DIM = 128
SSM_HEADS = 128
SSM_DIM = 32
STATE = 128
SEQ = 2048
ROWS = 128
HALF = 64
CTX = 16
DP = 8
WIDTH = 256
OWN = 8
QCOLS = 512
BLOCK = 256
SPAN = 5
SCALE = HEAD_DIM ** (-0.5)
FAR = -1e30

MESH = pl.DeviceIdType.MESH
HIGHEST = lax.Precision.HIGHEST
F32 = jnp.float32
BF16 = jnp.bfloat16


def dot(a, b, dims, precision=None):
    return lax.dot_general(a, b, (dims, ((), ())), precision=precision, preferred_element_type=F32)


NN = ((1,), (0,))
NT = ((1,), (1,))
TN = ((0,), (0,))


def three(a):
    high = a.astype(BF16)
    rest = a - high.astype(F32)
    mid = rest.astype(BF16)
    low = (rest - mid.astype(F32)).astype(BF16)
    return high, mid, low


def greet(axis, count):
    me = lax.axis_index(axis)
    barrier = pltpu.get_barrier_semaphore()

    def one(off, _):
        pl.semaphore_signal(barrier, inc=1, device_id={axis: lax.rem(me + off, count)}, device_id_type=MESH)
        return 0

    lax.fori_loop(1, count, one, 0)


def await_greetings(total):
    pl.semaphore_wait(pltpu.get_barrier_semaphore(), total)


def slot(device):
    return device // 4 * 4 + device % 2 * 2 + device // 2 % 2


def early_rows(device):
    return pl.ds(pl.multiple_of(device * HALF, HALF), HALF)


def late_rows(device):
    return pl.ds(pl.multiple_of((2 * CTX - 1 - device) * HALF, HALF), HALF)


def device_rows(device):
    return pl.ds(pl.multiple_of(device * ROWS, ROWS), ROWS)


def block_rows(i):
    return pl.ds(pl.multiple_of(i * BLOCK, BLOCK), BLOCK)


def columns(start, width):
    return pl.ds(pl.multiple_of(start * width, width), width)


def pack_small(out_grad, saved, ids, step, alog, small):
    ones = jnp.ones((8, HEAD_DIM), F32)
    sub = lax.broadcasted_iota(jnp.int32, (8, ROWS), 0)
    docs = jnp.broadcast_to(ids[...].astype(F32), (8, ROWS))
    rate = step[0] * -jnp.exp(alog[...])
    upto = lax.broadcasted_iota(jnp.int32, (ROWS, ROWS), 0) <= lax.broadcasted_iota(jnp.int32, (ROWS, ROWS), 1)
    totals = dot(rate, upto.astype(F32), TN, HIGHEST)
    steps = step[0].T
    for j in range(CTX):
        at = 8 * slot(j)
        small[j, 0:8, :] = steps[at : at + 8]
        small[j, 8:16, :] = totals[at : at + 8]

    def one(pair, _):
        tile = docs
        for e in range(4):
            cols = columns(4 * pair + e, HEAD_DIM)
            product = out_grad[0, :, cols].astype(F32) * saved[0, :, cols].astype(F32)
            tile = jnp.where(sub == e, dot(ones, product, NT, HIGHEST), tile)
        for z in range(2):
            small[pair // 2 * 4 + 2 * z + pair % 2, 16:24, :] = tile
        return 0

    lax.fori_loop(0, CTX // 2, one, 0)


def spread_columns(small, zz, dcol, doccol):
    row = lax.broadcasted_iota(jnp.int32, (24, 5 * ROWS), 0) % 8
    lane = lax.broadcasted_iota(jnp.int32, (24, 5 * ROWS), 1) // ROWS
    pick = jnp.where(row == lane, 1.0, 0.0).astype(BF16)
    doccol[0:8, :] = jnp.full((8, ROWS), -1.0, F32)

    def one(src, _):
        parts = jnp.concatenate([p.astype(F32) for p in three(small[src, 16:24, :])], axis=0).astype(BF16)
        wide = dot(parts, pick, TN)
        doccol[pl.ds(pl.multiple_of(8 + src * ROWS, 8), ROWS), :] = wide[:, 4 * ROWS :]

        @pl.when(src // 2 % 2 == zz)
        def _():
            dcol[query_rows(src, 0), :] = wide[:HALF, : 4 * ROWS]
            dcol[query_rows(src, 1), :] = wide[HALF:, : 4 * ROWS]

        return 0

    lax.fori_loop(0, CTX, one, 0)


def query_rows(src, late):
    block = src // 4 + late * (7 - 2 * (src // 4))
    second = src % 2 + late * (1 - 2 * (src % 2))
    return pl.ds(pl.multiple_of(block * ROWS + second * HALF, HALF), HALF)


def attention_block(i, off, q, d, kv, small, dcol, doccol, dkv, q2, d2, s_ref, m_ref, l_ref, dq):
    rows = device_rows(i)
    for h in range(4):
        part = pl.ds(h * ROWS, ROWS)
        q2[part, :] = q[rows, h * HEAD_DIM : (h + 1) * HEAD_DIM]
        d2[part, :] = d[rows, h * HEAD_DIM : (h + 1) * HEAD_DIM]
    m_ref[...] = jnp.full(m_ref.shape, FAR, F32)
    l_ref[...] = jnp.zeros(l_ref.shape, F32)
    dq[...] = jnp.zeros(dq.shape, F32)
    first = jnp.maximum(i - (SPAN - 1), 0)
    ahead = lax.broadcasted_iota(jnp.int32, (ROWS, BLOCK), 0) - lax.broadcasted_iota(jnp.int32, (ROWS, BLOCK), 1)

    def scores(j, _):
        keys = kv[0, block_rows(j), :]
        own = doccol[pl.ds(pl.multiple_of(8 + i * BLOCK + off, 8), ROWS), :]
        own = jnp.concatenate([own, own], axis=1)
        theirs = jnp.concatenate([small[2 * j, 20:21, :], small[2 * j + 1, 20:21, :]], axis=1)
        allowed = (own == theirs) & (ahead >= (j - i) * BLOCK - off)
        for h in range(4):
            part = pl.ds(h * ROWS, ROWS)
            s = jnp.where(allowed, dot(q2[part, :], keys, NT), FAR)
            s_ref[j - first, part, :] = s
            m_ref[part, :] = jnp.maximum(m_ref[part, :], jnp.maximum(s[:, :ROWS], s[:, ROWS:]))
        return 0

    lax.fori_loop(first, i + 1, scores, 0)
    m_ref[...] = jnp.broadcast_to(jnp.max(m_ref[...], axis=1, keepdims=True), m_ref.shape)

    def exps(j, _):
        for h in range(4):
            part = pl.ds(h * ROWS, ROWS)
            m = m_ref[part, :]
            e = jnp.exp((s_ref[j - first, part, :] - jnp.concatenate([m, m], axis=1)) * SCALE)
            s_ref[j - first, part, :] = e
            l_ref[part, :] += e[:, :ROWS] + e[:, ROWS:]
        return 0

    lax.fori_loop(first, i + 1, exps, 0)
    l_ref[...] = jnp.broadcast_to(1.0 / jnp.sum(l_ref[...], axis=1, keepdims=True), l_ref.shape)

    def grads(j, _):
        there = block_rows(j)
        keys, vals = kv[0, there, :], kv[1, there, :]
        probs, scaled = [], []
        for h in range(4):
            part = pl.ds(h * ROWS, ROWS)
            inv = l_ref[part, :]
            p = s_ref[j - first, part, :] * jnp.concatenate([inv, inv], axis=1)
            delta = dcol[rows, h * ROWS : (h + 1) * ROWS]
            dp = dot(d2[part, :], vals, NT) - jnp.concatenate([delta, delta], axis=1)
            ds = (p * dp * SCALE).astype(BF16)
            dq[part, :] += dot(ds, keys, NN)
            probs.append(p.astype(BF16))
            scaled.append(ds)
        dkv[0, there, :] += dot(jnp.concatenate(scaled, axis=0), q2[...], TN)
        dkv[1, there, :] += dot(jnp.concatenate(probs, axis=0), d2[...], TN)
        return 0

    lax.fori_loop(first, i + 1, grads, 0)


def spread_matrix(spread):
    row = lax.broadcasted_iota(jnp.int32, spread.shape, 0)
    lane = lax.broadcasted_iota(jnp.int32, spread.shape, 1)
    head = row % OWN
    a = (lane < 1024) & (row < 24) & (lane // ROWS == head)
    b = (lane >= 1024) & (lane < 1280) & (row < 24) & ((lane - 1024) // SSM_DIM == head)
    c = (lane >= 1280) & (row >= 24) & ((lane - 1280) // SSM_DIM == head)
    spread[...] = jnp.where(a | b | c, 1.0, 0.0).astype(BF16)


def ssm_chunk(c, x, bcm, small, doccol, cot, skip, spread, gstate, gtimed, acc_a, acc_s, dx):
    base = pl.multiple_of(c * ROWS, ROWS)
    here = pl.ds(base, ROWS)
    bc, cc = bcm[0, here, :], bcm[1, here, :]
    xc = x[here, :].astype(F32)
    dyb = cot[here, :]
    dy = dyb.astype(F32)
    steps, totals = small[c, 0:8, :], small[c, 8:16, :]
    parts = jnp.concatenate([p.astype(F32) for p in three(totals) + three(steps)], axis=0).astype(BF16)
    wide = dot(parts, spread[...], TN)
    te, se = wide[:, 1024:1280], wide[:, 1280:1536]
    docs = doccol[pl.ds(pl.multiple_of(8 + base, 8), ROWS), :]
    before = doccol[pl.ds(7 + base, 1), :]
    last = doccol[pl.ds(7 + ROWS + base, 1), :]
    docrow = small[c, 20:21, :]
    sub = lax.broadcasted_iota(jnp.int32, (ROWS, ROWS), 0)
    lane = lax.broadcasted_iota(jnp.int32, (ROWS, ROWS), 1)
    inner = jnp.where((sub <= lane) & (docs == docrow), dot(bc, cc, NT), 0.0)

    plain, timed = [], []
    for half in range(2):
        dyh = dyb[:, half * 128 : half * 128 + 128]
        total = None
        for pair in range(2):
            tops, lows, rights = [], [], []
            for one in range(2):
                local = 2 * pair + one
                h = 4 * half + local
                gap = totals[h : h + 1, :] - wide[:, ROWS * h : ROWS * h + ROWS]
                w = inner * jnp.exp(gap)
                tops.append(w.astype(BF16))
                lows.append((w * gap).astype(BF16))
                rights.append(jnp.where(lane // SSM_DIM == local, dyh.astype(F32), 0.0).astype(BF16))
            left = jnp.concatenate([jnp.concatenate(tops, axis=1), jnp.concatenate(lows, axis=1)], axis=0)
            out = dot(left, jnp.concatenate(rights, axis=0), NN)
            total = out if total is None else total + out
        plain.append(total[:ROWS])
        timed.append(total[ROWS:])
    intra = jnp.concatenate(plain, axis=1)
    intra_t = jnp.concatenate(timed, axis=1)

    both = jnp.concatenate([gstate[...], gtimed[...]], axis=1).astype(BF16)
    inter = dot(bc, both, NN)
    te_last = te[ROWS - 1 : ROWS, :]
    docs2 = jnp.concatenate([docs, docs], axis=1)
    before2 = jnp.concatenate([before, before], axis=1)
    last2 = jnp.concatenate([last, last], axis=1)
    left_time = te_last - te
    leave = jnp.where(docs2 == last2, jnp.exp(left_time), 0.0)
    got = intra + leave * inter[:, :WIDTH]
    got_t = intra_t + leave * (left_time * inter[:, :WIDTH] + inter[:, WIDTH:])
    dx[here, :] = (se * got + skip[0:1, :] * dy).astype(BF16)
    acc_a[...] += se * xc * got_t
    acc_s[...] += dy * xc

    enter = jnp.where(docs2 == before2, jnp.exp(te), 0.0)
    dye = dy * enter
    fresh = dot(cc, jnp.concatenate([dye, dye * te], axis=1).astype(BF16), TN)
    whole = jnp.where(last2 == before2, jnp.exp(te_last), 0.0)
    old = gstate[...]
    gtimed[...] = whole * (gtimed[...] + te_last * old) + fresh[:, WIDTH:]
    gstate[...] = whole * old + fresh[:, :WIDTH]


def own_heads(me):
    row = lax.broadcasted_iota(jnp.int32, (SSM_HEADS, WIDTH), 0)
    lane = lax.broadcasted_iota(jnp.int32, (SSM_HEADS, WIDTH), 1)
    return jnp.where(lane // SSM_DIM + slot(me) * OWN == row, 1.0, 0.0)


def finish_decay(me, acc_a, acc_s):
    sums = jnp.concatenate(
        [jnp.sum(acc_a[...], axis=0, keepdims=True), jnp.sum(acc_s[...], axis=0, keepdims=True), jnp.zeros((6, WIDTH), F32)],
        axis=0,
    )
    return dot(sums, own_heads(me), NT, HIGHEST)


BLOCKS = SEQ // BLOCK
KV_EARLY, KV_LATE, BC = range(3)


def kernel(q, d, k, v, x, b, c, dvm, o, ids, step, alog, skip_in,
           grad_x, grad_kv, grad_d,
           lq, ld, lkv, lbc, lx, ls, small,
           x_in_send, x_in_recv, small_send, small_recv, first_send, first_recv,
           z_send, core_send, relay_send, fwd_recv, q_send, q_recv, own_sem,
           dkv, q2, d2, s_ref, m_ref, l_ref, dq, dcol, doccol, spread, gstate, gtimed, acc_a, acc_s, skip,
           dx, x_send, x_recv, x_own,
           cot, cot_out, cot_send, cot_recv,
           pair_in, pair_send, pair_recv, half_out, half_in, half_send, half_recv,
           done, done_send, done_recv, done_own,
           decay, ctx_decay, seq_decay, all_decay, ctx_send, ctx_recv, ctx_own, dp_send, dp_recv, dp_own):
    me = lax.axis_index("ctx")
    row = lax.axis_index("dp")
    xx, zz, cc, zc = me // 4, me // 2 % 2, me % 2, me % 4
    core_peer = me + 1 - 2 * cc
    z_peer = me + 2 - 4 * zz
    first, second = pl.ds(0, HALF), pl.ds(HALF, HALF)

    def remote(src, dst, send_sem, recv_sem, peer):
        return pltpu.make_async_remote_copy(
            src_ref=src, dst_ref=dst, send_sem=send_sem, recv_sem=recv_sem,
            device_id={"ctx": peer}, device_id_type=MESH,
        )

    def group_moves(plane, frm):
        cols = columns(plane, HEAD_DIM)
        return [
            (k.at[0, first, cols], lkv.at[0, early_rows(frm), :]),
            (v.at[0, first, cols], lkv.at[1, early_rows(frm), :]),
            (k.at[0, second, cols], lkv.at[0, late_rows(frm), :]),
            (v.at[0, second, cols], lkv.at[1, late_rows(frm), :]),
            (b.at[0, :, cols], lbc.at[0, device_rows(frm), :]),
            (c.at[0, :, cols], lbc.at[1, device_rows(frm), :]),
        ]

    def first_copy(kind, to, frm, peer):
        src, dst = group_moves(to // 4, frm)[kind]
        return remote(src, dst, first_send.at[kind, peer // 4], first_recv.at[kind, frm], peer)

    def landed(kind, src):
        return (
            lkv.at[:, early_rows(src), :],
            lkv.at[:, late_rows(src), :],
            lbc.at[:, device_rows(src), :],
        )[kind]

    def forward(kind, src, sems, peer):
        ref = landed(kind, src)
        return remote(ref, ref, sems.at[kind, src // 4], fwd_recv.at[kind, src], peer)

    def others_x(body):
        def one(n, _):
            body(lax.rem(xx + n, 4) * 4 + zc)
            return 0

        lax.fori_loop(1, 4, one, 0)

    def each_x(body):
        def one(n, _):
            body(lax.rem(xx + n, 4) * 4 + zc)
            return 0

        lax.fori_loop(0, 4, one, 0)

    def send_first(kinds):
        others_x(lambda to: [first_copy(kind, to, me, to).start() for kind in kinds])

    def q_copy(array, late, to, frm, peer):
        src = ((q, d)[array]).at[0, pl.ds(late * HALF, HALF), columns(to // 4 * 2 + to % 2, QCOLS)]
        dst = ((lq, ld)[array]).at[query_rows(frm, late), :]
        return remote(src, dst, q_send.at[2 * array + late, peer], q_recv.at[2 * array + late, frm], peer)

    def send_q(late):
        def one(n, _):
            to = lax.rem(xx + n // 2, 4) * 4 + 2 * zz + lax.rem(cc + n, 2)
            for array in range(2):
                q_copy(array, late, to, me, to).start()
            return 0

        lax.fori_loop(1, 8, one, 0)

    def q_arrived(src, late):
        @pl.when(src != me)
        def _():
            for array in range(2):
                q_copy(array, late, me, src, src).wait_recv()

    def x_in_copy(to, frm, peer):
        return remote(x.at[0, :, columns(slot(to), WIDTH)], lx.at[device_rows(frm), :],
                      x_in_send.at[peer], x_in_recv.at[frm], peer)

    def small_copy(to, frm, peer):
        return remote(small.at[to], ls.at[frm], small_send.at[peer], small_recv.at[frm], peer)

    def to_all(body):
        def one(n, _):
            body(lax.rem(me + n, CTX))
            return 0

        lax.fori_loop(1, CTX, one, 0)

    def own_copies():
        moves = group_moves(xx, me)
        for array in range(2):
            for late in range(2):
                moves.append((((q, d)[array]).at[0, pl.ds(late * HALF, HALF), columns(xx * 2 + cc, QCOLS)],
                              ((lq, ld)[array]).at[query_rows(me, late), :]))
        moves.append((x.at[0, :, columns(slot(me), WIDTH)], lx.at[device_rows(me), :]))
        moves.append((small.at[me], ls.at[me]))
        return [pltpu.make_async_copy(src, dst, own_sem.at[n]) for n, (src, dst) in enumerate(moves)]

    greet("ctx", CTX)
    greet("dp", DP)
    await_greetings(CTX - 1 + DP - 1)
    send_first((0, 1, 2, 3))
    own = own_copies()
    for copy in own[:-1]:
        copy.start()
    send_q(1)
    send_first((4, 5))
    pack_small(dvm, o, ids, step, alog, small)
    to_all(lambda to: small_copy(to, me, to).start())
    own[-1].start()
    for copy in own:
        copy.wait()

    def pass_on(kinds, parts):
        def one(src):
            @pl.when(src != me)
            def _():
                for kind in kinds:
                    first_copy(kind, me, src, src).wait_recv()

            for part in parts:
                forward(part, src, z_send, z_peer).start()
                forward(part, src, core_send, core_peer).start()

        each_x(one)

    def relay(parts):
        def one(src):
            src = src + 2 - 4 * zz
            for part in parts:
                forward(part, src, z_send, z_peer).wait_recv()
                forward(part, src, relay_send, core_peer).start()

        each_x(one)

    pass_on((0, 1, 2, 3), (KV_EARLY, KV_LATE))

    @pl.when(me >= CTX // 2)
    def _():
        to_all(lambda to: x_in_copy(to, me, to).start())

    send_q(0)

    @pl.when(me < CTX // 2)
    def _():
        to_all(lambda to: x_in_copy(to, me, to).start())

    pass_on((4, 5), (BC,))
    relay((KV_EARLY, KV_LATE))

    for ref in (dkv, gstate, gtimed, acc_a, acc_s):
        ref[...] = jnp.zeros(ref.shape, F32)
    skip[...] = dot(jnp.broadcast_to(skip_in[...], (8, SSM_HEADS)), own_heads(me), NN, HIGHEST)
    spread_matrix(spread)

    to_all(lambda src: small_copy(me, src, src).wait_recv())
    spread_columns(ls, zz, dcol, doccol)

    def from_core(parts):
        def one(src):
            for flip in (0, 1):
                at = src + 1 - 2 * cc + flip * (2 - 4 * zz)
                for part in parts:
                    forward(part, at, core_send, core_peer).wait_recv()

        each_x(one)

    from_core((KV_EARLY, KV_LATE))
    relay((BC,))

    def x_copy(to, frm, peer):
        return remote(dx.at[device_rows(to), :], grad_x.at[0, :, columns(slot(frm), WIDTH)],
                      x_send.at[peer], x_recv.at[frm], peer)

    def x_mine():
        return pltpu.make_async_copy(dx.at[device_rows(me), :], grad_x.at[0, :, columns(slot(me), WIDTH)], x_own)

    def own_off(i):
        late = i // 4
        return (zz + late - 2 * zz * late) * ROWS

    def cot_copy(i, off):
        return remote(cot_out.at[i], cot.at[pl.ds(pl.multiple_of(i * BLOCK + off, ROWS), ROWS), :],
                      cot_send.at[i], cot_recv.at[i], z_peer)

    def pair_copy(i, which):
        return remote(dkv.at[which, block_rows(i), :], pair_in.at[i], pair_send.at[i], pair_recv.at[i], core_peer)

    def half_copy(i):
        return remote(half_out.at[i], half_in.at[i], half_send.at[i], half_recv.at[i], z_peer)

    def done_owner(i, r):
        late = i // 4
        chunk = 4 * i + own_off(i) // HALF + r
        return chunk + late * (2 * CTX - 1 - 2 * chunk)

    def done_copy(i, r, core, plane, late, peer):
        return remote(done.at[i, pl.ds(r * HALF, HALF), :],
                      grad_kv.at[core, pl.ds(pl.multiple_of(late * HALF, HALF), HALF), columns(plane, HEAD_DIM)],
                      done_send.at[i, r], done_recv.at[core, late, plane], peer)

    def done_mine(i, r):
        late = i // 4
        return pltpu.make_async_copy(
            done.at[i, pl.ds(r * HALF, HALF), :],
            grad_kv.at[cc, pl.ds(pl.multiple_of(late * HALF, HALF), HALF), columns(xx, HEAD_DIM)],
            done_own.at[late],
        )

    def sum_pair(i):
        pair_copy(i, 1 - cc).wait_recv()
        off = ROWS - own_off(i)
        there = pl.ds(pl.multiple_of(i * BLOCK + off, ROWS), ROWS)
        half_out[i] = (dkv[cc, there, :] + pair_in[i, pl.ds(pl.multiple_of(off, ROWS), ROWS), :]).astype(BF16)
        half_copy(i).start()

    def sum_half(i):
        half_copy(i).wait_recv()
        off = own_off(i)
        there = pl.ds(pl.multiple_of(i * BLOCK + off, ROWS), ROWS)
        mine = dkv[cc, there, :] + pair_in[i, pl.ds(pl.multiple_of(off, ROWS), ROWS), :]
        done[i] = (mine + half_in[i].astype(F32)).astype(BF16)
        for r in range(2):
            owner = done_owner(i, r)

            @pl.when(owner != me)
            def _():
                done_copy(i, r, cc, xx, i // 4, owner).start()

            @pl.when(owner == me)
            def _():
                done_mine(i, r).start()

    def block(n, _):
        @pl.when(n < BLOCKS)
        def _():
            i = BLOCKS - 1 - n
            off = own_off(i)

            @pl.when(i >= 4)
            def _():
                for r in range(2):
                    q_arrived(4 * (7 - i) + 2 * zz + r, 1)

            @pl.when(i < 4)
            def _():
                for r in range(2):
                    q_arrived(4 * i + 2 * zz + r, 0)

            attention_block(i, off, lq, ld, lkv, ls, dcol, doccol, dkv, q2, d2, s_ref, m_ref, l_ref, dq)
            pair_copy(i, 1 - cc).start()
            here = pl.ds(pl.multiple_of(i * BLOCK + off, ROWS), ROWS)
            for e in range(2):
                cols = slice(e * HEAD_DIM, (e + 1) * HEAD_DIM)
                mine = pl.ds(pl.multiple_of((2 * zz + e) * ROWS, ROWS), ROWS)
                theirs = pl.ds(pl.multiple_of((2 - 2 * zz + e) * ROWS, ROWS), ROWS)
                cot[here, cols] = dq[mine, :].astype(BF16)
                cot_out[i, :, cols] = dq[theirs, :].astype(BF16)
            cot_copy(i, off).start()

        @pl.when(n == 0)
        def _():
            from_core((BC,))

        @pl.when(n >= 1)
        def _():
            sum_pair(BLOCKS - n)

        @pl.when(n >= 2)
        def _():
            sum_half(BLOCKS + 1 - n)

        @pl.when(n >= 1)
        def _():
            i = BLOCKS - n
            cot_copy(i, ROWS - own_off(i)).wait_recv()
            for sub in (1, 0):
                owner = 2 * i + sub

                @pl.when(owner != me)
                def _():
                    x_in_copy(me, owner, owner).wait_recv()

                ssm_chunk(owner, lx, lbc, ls, doccol, cot, skip, spread, gstate, gtimed, acc_a, acc_s, dx)

                @pl.when(owner != me)
                def _():
                    x_copy(owner, me, owner).start()

                @pl.when(owner == me)
                def _():
                    x_mine().start()

        return 0

    lax.fori_loop(0, BLOCKS + 1, block, 0)

    decay[...] = finish_decay(me, acc_a, acc_s)

    def ctx_copy(frm, peer):
        return remote(decay, ctx_decay.at[frm], ctx_send.at[peer], ctx_recv.at[frm], peer)

    def dp_copy(frm, peer):
        return pltpu.make_async_remote_copy(
            src_ref=seq_decay, dst_ref=all_decay.at[frm], send_sem=dp_send.at[peer], recv_sem=dp_recv.at[frm],
            device_id={"dp": peer}, device_id_type=MESH,
        )

    to_all(lambda to: ctx_copy(me, to).start())
    ctx_mine = pltpu.make_async_copy(decay, ctx_decay.at[me], ctx_own)
    ctx_mine.start()
    sum_half(0)
    to_all(lambda frm: ctx_copy(frm, frm).wait_recv())
    ctx_mine.wait()
    seq_decay[...] = jnp.sum(ctx_decay[...], axis=0)

    def start_dp(off, _):
        dp_copy(row, lax.rem(row + off, DP)).start()
        return 0

    lax.fori_loop(1, DP, start_dp, 0)
    dp_mine = pltpu.make_async_copy(seq_decay, all_decay.at[row], dp_own)
    dp_mine.start()

    def sent(to):
        small_copy(to, me, to).wait_send()
        x_in_copy(to, me, to).wait_send()
        x_copy(to, me, to).wait_send()
        ctx_copy(me, to).wait_send()

    to_all(sent)
    others_x(lambda to: [first_copy(kind, to, me, to).wait_send() for kind in range(6)])

    def forwarded(src):
        other = src + 2 - 4 * zz
        for part in range(3):
            forward(part, src, z_send, z_peer).wait_send()
            forward(part, src, core_send, core_peer).wait_send()
            forward(part, other, relay_send, core_peer).wait_send()

    each_x(forwarded)

    def sent_q(n, _):
        to = lax.rem(xx + n // 2, 4) * 4 + 2 * zz + lax.rem(cc + n, 2)
        for array in range(2):
            for late in range(2):
                q_copy(array, late, to, me, to).wait_send()
        return 0

    lax.fori_loop(1, 8, sent_q, 0)

    def sent_blocks(i, _):
        cot_copy(i, own_off(i)).wait_send()
        pair_copy(i, 1 - cc).wait_send()
        half_copy(i).wait_send()
        for r in range(2):
            owner = done_owner(i, r)

            @pl.when(owner != me)
            def _():
                done_copy(i, r, cc, xx, i // 4, owner).wait_send()

            @pl.when(owner == me)
            def _():
                done_mine(i, r).wait()

        return 0

    lax.fori_loop(0, BLOCKS, sent_blocks, 0)

    for core in range(2):
        for late in range(2):
            for plane in range(4):
                @pl.when(plane * 4 + 2 * zz + core != me)
                def _():
                    done_copy(0, 0, core, plane, late, core_peer).wait_recv()

    def end_dp(off, _):
        frm = lax.rem(row + DP - off, DP)
        dp_copy(frm, frm).wait_recv()
        dp_copy(row, frm).wait_send()
        return 0

    lax.fori_loop(1, DP, end_dp, 0)
    dp_mine.wait()
    total = all_decay[0]
    for other in range(1, DP):
        total += all_decay[other]
    grad_d[...] = total[:2]
    to_all(lambda frm: x_copy(me, frm, frm).wait_recv())
    x_mine().wait()


DMA = pltpu.SemaphoreType.DMA
SCRATCH = [
    pltpu.VMEM((SEQ // 2, QCOLS), BF16),
    pltpu.VMEM((SEQ // 2, QCOLS), BF16),
    pltpu.VMEM((2, SEQ, HEAD_DIM), BF16),
    pltpu.VMEM((2, SEQ, STATE), BF16),
    pltpu.VMEM((SEQ, WIDTH), BF16),
    pltpu.VMEM((CTX, 24, ROWS), F32),
    pltpu.VMEM((CTX, 24, ROWS), F32),
    DMA((CTX,)),
    DMA((CTX,)),
    DMA((CTX,)),
    DMA((CTX,)),
    DMA((6, 4)),
    DMA((6, CTX)),
    DMA((3, 4)),
    DMA((3, 4)),
    DMA((3, 4)),
    DMA((3, CTX)),
    DMA((4, CTX)),
    DMA((4, CTX)),
    DMA((12,)),
    pltpu.VMEM((2, SEQ, HEAD_DIM), F32),
    pltpu.VMEM((4 * ROWS, HEAD_DIM), BF16),
    pltpu.VMEM((4 * ROWS, HEAD_DIM), BF16),
    pltpu.VMEM((SPAN, 4 * ROWS, BLOCK), F32),
    pltpu.VMEM((4 * ROWS, ROWS), F32),
    pltpu.VMEM((4 * ROWS, ROWS), F32),
    pltpu.VMEM((4 * ROWS, HEAD_DIM), F32),
    pltpu.VMEM((SEQ // 2, 4 * ROWS), F32),
    pltpu.VMEM((SEQ + 8, ROWS), F32),
    pltpu.VMEM((48, 1536), BF16),
    pltpu.VMEM((STATE, WIDTH), F32),
    pltpu.VMEM((STATE, WIDTH), F32),
    pltpu.VMEM((ROWS, WIDTH), F32),
    pltpu.VMEM((ROWS, WIDTH), F32),
    pltpu.VMEM((8, WIDTH), F32),
    pltpu.VMEM((SEQ, WIDTH), BF16),
    DMA((CTX,)),
    DMA((CTX,)),
    DMA,
    pltpu.VMEM((SEQ, WIDTH), BF16),
    pltpu.VMEM((BLOCKS, ROWS, WIDTH), BF16),
    DMA((BLOCKS,)),
    DMA((BLOCKS,)),
    pltpu.VMEM((BLOCKS, BLOCK, HEAD_DIM), F32),
    DMA((BLOCKS,)),
    DMA((BLOCKS,)),
    pltpu.VMEM((BLOCKS, ROWS, HEAD_DIM), BF16),
    pltpu.VMEM((BLOCKS, ROWS, HEAD_DIM), BF16),
    DMA((BLOCKS,)),
    DMA((BLOCKS,)),
    pltpu.VMEM((BLOCKS, ROWS, HEAD_DIM), BF16),
    DMA((BLOCKS, 2)),
    DMA((2, 2, 4)),
    DMA((2,)),
    pltpu.VMEM((8, SSM_HEADS), F32),
    pltpu.VMEM((CTX, 8, SSM_HEADS), F32),
    pltpu.VMEM((8, SSM_HEADS), F32),
    pltpu.VMEM((DP, 8, SSM_HEADS), F32),
    DMA((CTX,)),
    DMA((CTX,)),
    DMA,
    DMA((DP,)),
    DMA((DP,)),
    DMA,
]


def gradients(q, k, v, o, d, ids, x, b, c, step, alog, skip):
    hbm = pl.BlockSpec(memory_space=pl.ANY)
    vmem = pl.BlockSpec(memory_space=pltpu.VMEM)
    return pl.pallas_call(
        kernel,
        out_shape=[
            jax.ShapeDtypeStruct((1, ROWS, SSM_HEADS * SSM_DIM), BF16),
            jax.ShapeDtypeStruct((2, ROWS, KVHEADS * HEAD_DIM), BF16),
            jax.ShapeDtypeStruct((2, SSM_HEADS), F32),
        ],
        in_specs=[hbm] * 7 + [vmem] * 6,
        out_specs=[hbm, hbm, vmem],
        scratch_shapes=SCRATCH,
        compiler_params=pltpu.CompilerParams(
            collective_id=0, has_side_effects=True, vmem_limit_bytes=60 * 2**20
        ),
        name="gradients",
    )(q, d, k, v, x, b, c, d, o, ids, step, alog, skip)


def settle_kernel(x, kv, dec, grad_k, grad_v, grad_x, grad_d):
    grad_x[...] = x[...]
    grad_k[0] = kv[0]
    grad_v[0] = kv[1]
    grad_d[...] = dec[...]


def settle(x, kv, dec):
    vmem = pl.BlockSpec(memory_space=pltpu.VMEM)
    narrow = jax.ShapeDtypeStruct((1, ROWS, KVHEADS * HEAD_DIM), BF16)
    return pl.pallas_call(
        settle_kernel,
        out_shape=[narrow, narrow, jax.ShapeDtypeStruct(x.shape, BF16), jax.ShapeDtypeStruct(dec.shape, F32)],
        in_specs=[vmem] * 3,
        out_specs=[vmem] * 4,
        compiler_params=pltpu.CompilerParams(vmem_limit_bytes=60 * 2**20),
        name="settle",
    )(x, kv, dec)


def shards(queries, keys, values, saved, out_grad, doc_ids, inputs, bmat, cmat, step, alog, skip):
    return tuple(settle(*gradients(
        queries, keys, values, saved, out_grad, doc_ids, inputs, bmat, cmat, step, alog[None], skip[None]
    )))


def solution(mesh):
    return jax.shard_map(
        shards,
        mesh=mesh,
        in_specs=(
            P("dp", "ctx", None),
            P("dp", "ctx", None),
            P("dp", "ctx", None),
            P("dp", "ctx", None),
            P("dp", "ctx", None),
            P("dp", "ctx"),
            P("dp", "ctx", None),
            P("dp", "ctx", None),
            P("dp", "ctx", None),
            P("dp", "ctx", None),
            P(),
            P(),
        ),
        out_specs=(P("dp", "ctx", None), P("dp", "ctx", None), P("dp", "ctx", None), P()),
        check_vma=False,
    )
```

```python
import jax
import jax.numpy as jnp
from jax import lax
from jax.experimental import pallas as pl
from jax.experimental.pallas import tpu as pltpu
from jax.sharding import PartitionSpec as P

QHEADS = 32
KVHEADS = 4
HEAD_DIM = 128
SSM_HEADS = 128
SSM_DIM = 32
STATE = 128
SEQ = 2048
ROWS = 128
HALF = 64
CTX = 16
DP = 8
WIDTH = 256
OWN = 8
QCOLS = 512
BLOCK = 256
SPAN = 5
SCALE = HEAD_DIM ** (-0.5)
FAR = -1e30

MESH = pl.DeviceIdType.MESH
HIGHEST = lax.Precision.HIGHEST
F32 = jnp.float32
BF16 = jnp.bfloat16


def dot(a, b, dims, precision=None):
    return lax.dot_general(a, b, (dims, ((), ())), precision=precision, preferred_element_type=F32)


NN = ((1,), (0,))
NT = ((1,), (1,))
TN = ((0,), (0,))


def three(a):
    high = a.astype(BF16)
    rest = a - high.astype(F32)
    mid = rest.astype(BF16)
    low = (rest - mid.astype(F32)).astype(BF16)
    return high, mid, low


def greet(axis, count):
    me = lax.axis_index(axis)
    barrier = pltpu.get_barrier_semaphore()

    def one(off, _):
        pl.semaphore_signal(barrier, inc=1, device_id={axis: lax.rem(me + off, count)}, device_id_type=MESH)
        return 0

    lax.fori_loop(1, count, one, 0)


def await_greetings(total):
    pl.semaphore_wait(pltpu.get_barrier_semaphore(), total)


def slot(device):
    return device // 4 * 4 + device % 2 * 2 + device // 2 % 2


def early_rows(device):
    return pl.ds(pl.multiple_of(device * HALF, HALF), HALF)


def late_rows(device):
    return pl.ds(pl.multiple_of((2 * CTX - 1 - device) * HALF, HALF), HALF)


def device_rows(device):
    return pl.ds(pl.multiple_of(device * ROWS, ROWS), ROWS)


def block_rows(i):
    return pl.ds(pl.multiple_of(i * BLOCK, BLOCK), BLOCK)


def columns(start, width):
    return pl.ds(pl.multiple_of(start * width, width), width)


def pack_small(out_grad, saved, ids, step, alog, small):
    docs = jnp.broadcast_to(ids[...].astype(F32), (4, ROWS))
    rate = step[0] * -jnp.exp(alog[...])
    upto = lax.broadcasted_iota(jnp.int32, (ROWS, ROWS), 0) <= lax.broadcasted_iota(jnp.int32, (ROWS, ROWS), 1)
    totals = dot(rate, upto.astype(F32), TN, HIGHEST)
    steps = step[0].T
    lane = lax.broadcasted_iota(jnp.int32, (ROWS, ROWS), 1)
    deltas = jnp.zeros((ROWS, ROWS), F32)
    for h in range(QHEADS):
        cols = slice(h * HEAD_DIM, (h + 1) * HEAD_DIM)
        product = out_grad[0, :, cols].astype(F32) * saved[0, :, cols].astype(F32)
        deltas = jnp.where(lane == h, jnp.sum(product, axis=1, keepdims=True), deltas)
    deltas = deltas.T
    for j in range(CTX):
        at = 8 * slot(j)
        small[j, 0:8, :] = steps[at : at + 8]
        small[j, 8:16, :] = totals[at : at + 8]
        pair = 4 * (j // 4 * 2 + j % 2)
        small[j, 16:20, :] = deltas[pair : pair + 4]
        small[j, 20:24, :] = docs


def spread_columns(small, doccol):
    doccol[0:8, :] = jnp.full((8, ROWS), -1.0, F32)
    row = lax.broadcasted_iota(jnp.int32, (8, ROWS), 0)
    pick = jnp.where(row == 4, 1.0, 0.0).astype(BF16)

    def one(src, _):
        docs = jnp.where(row == 4, small[src, 16:24, :], 0.0).astype(BF16)
        doccol[pl.ds(pl.multiple_of(8 + src * ROWS, 8), ROWS), :] = dot(docs, pick, TN)
        return 0

    lax.fori_loop(0, CTX, one, 0)


def query_rows(src, late):
    block = src // 4 + late * (7 - 2 * (src // 4))
    second = src % 2 + late * (1 - 2 * (src % 2))
    return pl.ds(pl.multiple_of(block * ROWS + second * HALF, HALF), HALF)


def transpose_keys(kv, kt):
    def one(n, _):
        rows = device_rows(n)
        kt[:, rows] = kv[0, rows, :].T
        return 0

    lax.fori_loop(0, CTX, one, 0)


def attention_block(i, off, zz, q, d, kv, kt, small, doccol, dkv, q2, d2, qt, dt, s_ref, dq, whole):
    rows = device_rows(i)
    for h in range(4):
        part = pl.ds(h * ROWS, ROWS)
        q2[part, :] = q[rows, h * HEAD_DIM : (h + 1) * HEAD_DIM]
        d2[part, :] = d[rows, h * HEAD_DIM : (h + 1) * HEAD_DIM]
        qt[:, part] = q[rows, h * HEAD_DIM : (h + 1) * HEAD_DIM].T
        dt[:, part] = d[rows, h * HEAD_DIM : (h + 1) * HEAD_DIM].T
    dq[...] = jnp.zeros(dq.shape, F32)
    first = jnp.maximum(i - (SPAN - 1), 0)

    def each(body, carry):
        if not whole:
            return lax.fori_loop(0, i + 1 - first, body, carry)
        for n in range(SPAN):
            carry = body(n, carry)
        return carry

    ahead = lax.broadcasted_iota(jnp.int32, (BLOCK, ROWS), 1) - lax.broadcasted_iota(jnp.int32, (BLOCK, ROWS), 0)
    own = small[2 * i + off // ROWS, 20:21, :]
    late = i // 4
    plane = i + late * (7 - 2 * i)
    base = 4 * plane + 2 * zz
    lo, hi = small[base + late, 16:24, :], small[base + 1 - late, 16:24, :]
    left = lax.broadcasted_iota(jnp.int32, (8, ROWS), 1) < HALF
    early_tile = jnp.where(left, lo, jnp.roll(hi, HALF, 1))
    late_tile = jnp.where(left, jnp.roll(lo, HALF, 1), hi)
    tile = jnp.where(late == 1, late_tile, early_tile)
    delta = jnp.concatenate([tile[h : h + 1, :] for h in range(4)], axis=1)

    def scores(n, m):
        j = first + n
        keys = kv[0, block_rows(j), :]
        theirs = doccol[pl.ds(pl.multiple_of(8 + j * BLOCK, 8), BLOCK), :]
        allowed = (own == theirs) & (ahead >= (j - i) * BLOCK - off)
        parts = []
        for half in range(2):
            s = dot(keys, qt[:, pl.ds(half * BLOCK, BLOCK)], NN)
            s = jnp.where(jnp.concatenate([allowed, allowed], axis=1), s, FAR)
            s_ref[n, :, pl.ds(half * BLOCK, BLOCK)] = s
            parts.append(jnp.max(s.reshape(BLOCK // 8, 8, BLOCK), axis=0))
        return jnp.maximum(m, jnp.concatenate(parts, axis=1))

    m = each(scores, jnp.full((8, 4 * ROWS), FAR, F32))
    m = jnp.max(m, axis=0, keepdims=True)

    def exps(n, total):
        parts = []
        for half in range(2):
            cols = pl.ds(half * BLOCK, BLOCK)
            e = jnp.exp((s_ref[n, :, cols] - m[:, half * BLOCK : (half + 1) * BLOCK]) * SCALE)
            s_ref[n, :, cols] = e
            parts.append(jnp.sum(e.reshape(BLOCK // 8, 8, BLOCK), axis=0))
        return total + jnp.concatenate(parts, axis=1)

    total = each(exps, jnp.zeros((8, 4 * ROWS), F32))
    inv = 1.0 / jnp.sum(total, axis=0, keepdims=True)

    def grads(n, _):
        j = first + n
        there = block_rows(j)
        vals, keys_t = kv[1, there, :], kt[:, there]
        probs, scaled = [], []
        for half in range(4):
            cols = slice(half * ROWS, (half + 1) * ROWS)
            p = s_ref[n, :, pl.ds(half * ROWS, ROWS)] * inv[:, cols]
            dp = dot(vals, dt[:, pl.ds(half * ROWS, ROWS)], NN) - delta[:, cols]
            ds = (p * dp * SCALE).astype(BF16)
            dq[:, cols] += dot(keys_t, ds, NN)
            probs.append(p.astype(BF16))
            scaled.append(ds)
        dkv[0, there, :] += dot(jnp.concatenate(scaled, axis=1), q2[...], NN)
        dkv[1, there, :] += dot(jnp.concatenate(probs, axis=1), d2[...], NN)
        return 0

    each(grads, 0)


def spread_matrix(spread):
    row = lax.broadcasted_iota(jnp.int32, spread.shape, 0)
    lane = lax.broadcasted_iota(jnp.int32, spread.shape, 1)
    head = row % OWN
    a = (lane < 1024) & (row < 24) & (lane // ROWS == head)
    b = (lane >= 1024) & (lane < 1280) & (row < 24) & ((lane - 1024) // SSM_DIM == head)
    c = (lane >= 1280) & (row >= 24) & ((lane - 1280) // SSM_DIM == head)
    spread[...] = jnp.where(a | b | c, 1.0, 0.0).astype(BF16)


def ssm_chunk(c, x, bcm, small, doccol, cot, skip, spread, gstate, gtimed, acc_a, acc_s, dx):
    base = pl.multiple_of(c * ROWS, ROWS)
    here = pl.ds(base, ROWS)
    bc, cc = bcm[0, here, :], bcm[1, here, :]
    xc = x[here, :].astype(F32)
    dyb = cot[here, :]
    dy = dyb.astype(F32)
    steps, totals = small[c, 0:8, :], small[c, 8:16, :]
    parts = jnp.concatenate([p.astype(F32) for p in three(totals) + three(steps)], axis=0).astype(BF16)
    wide = dot(parts, spread[...], TN)
    te, se = wide[:, 1024:1280], wide[:, 1280:1536]
    docs = doccol[pl.ds(pl.multiple_of(8 + base, 8), ROWS), :]
    before = doccol[pl.ds(7 + base, 1), :]
    last = doccol[pl.ds(7 + ROWS + base, 1), :]
    docrow = small[c, 20:21, :]
    sub = lax.broadcasted_iota(jnp.int32, (ROWS, ROWS), 0)
    lane = lax.broadcasted_iota(jnp.int32, (ROWS, ROWS), 1)
    inner = jnp.where((sub <= lane) & (docs == docrow), dot(bc, cc, NT), 0.0)

    plain, timed = [], []
    for half in range(2):
        dyh = dyb[:, half * 128 : half * 128 + 128]
        total = None
        for pair in range(2):
            tops, lows, rights = [], [], []
            for one in range(2):
                local = 2 * pair + one
                h = 4 * half + local
                gap = totals[h : h + 1, :] - wide[:, ROWS * h : ROWS * h + ROWS]
                w = inner * jnp.exp(gap)
                tops.append(w.astype(BF16))
                lows.append((w * gap).astype(BF16))
                rights.append(jnp.where(lane // SSM_DIM == local, dyh.astype(F32), 0.0).astype(BF16))
            left = jnp.concatenate([jnp.concatenate(tops, axis=1), jnp.concatenate(lows, axis=1)], axis=0)
            out = dot(left, jnp.concatenate(rights, axis=0), NN)
            total = out if total is None else total + out
        plain.append(total[:ROWS])
        timed.append(total[ROWS:])
    intra = jnp.concatenate(plain, axis=1)
    intra_t = jnp.concatenate(timed, axis=1)

    both = jnp.concatenate([gstate[...], gtimed[...]], axis=1).astype(BF16)
    inter = dot(bc, both, NN)
    te_last = te[ROWS - 1 : ROWS, :]
    docs2 = jnp.concatenate([docs, docs], axis=1)
    before2 = jnp.concatenate([before, before], axis=1)
    last2 = jnp.concatenate([last, last], axis=1)
    left_time = te_last - te
    leave = jnp.where(docs2 == last2, jnp.exp(left_time), 0.0)
    got = intra + leave * inter[:, :WIDTH]
    got_t = intra_t + leave * (left_time * inter[:, :WIDTH] + inter[:, WIDTH:])
    dx[here, :] = (se * got + skip[0:1, :] * dy).astype(BF16)
    acc_a[...] += se * xc * got_t
    acc_s[...] += dy * xc

    enter = jnp.where(docs2 == before2, jnp.exp(te), 0.0)
    dye = dy * enter
    fresh = dot(cc, jnp.concatenate([dye, dye * te], axis=1).astype(BF16), TN)
    whole = jnp.where(last2 == before2, jnp.exp(te_last), 0.0)
    old = gstate[...]
    gtimed[...] = whole * (gtimed[...] + te_last * old) + fresh[:, WIDTH:]
    gstate[...] = whole * old + fresh[:, :WIDTH]


def own_heads(me):
    row = lax.broadcasted_iota(jnp.int32, (SSM_HEADS, WIDTH), 0)
    lane = lax.broadcasted_iota(jnp.int32, (SSM_HEADS, WIDTH), 1)
    return jnp.where(lane // SSM_DIM + slot(me) * OWN == row, 1.0, 0.0)


def finish_decay(me, acc_a, acc_s):
    sums = jnp.concatenate(
        [jnp.sum(acc_a[...], axis=0, keepdims=True), jnp.sum(acc_s[...], axis=0, keepdims=True), jnp.zeros((6, WIDTH), F32)],
        axis=0,
    )
    return dot(sums, own_heads(me), NT, HIGHEST)


BLOCKS = SEQ // BLOCK
KV_EARLY, KV_LATE, BC = range(3)


def kernel(q, d, k, v, x, b, c, dvm, o, ids, step, alog, skip_in,
           grad_x, grad_kv, grad_d,
           lq, ld, lkv, lbc, lx, ls, small,
           x_in_send, x_in_recv, small_send, small_recv, first_send, first_recv,
           z_send, core_send, relay_send, fwd_recv, q_send, q_recv, own_sem,
           dkv, q2, d2, qt, dt, kt, s_ref, dq, doccol, spread, gstate, gtimed, acc_a, acc_s, skip,
           dx, x_send, x_recv, x_own,
           cot, cot_out, cot_send, cot_recv,
           pair_in, pair_send, pair_recv, half_out, half_in, half_send, half_recv,
           done, done_send, done_recv, done_own,
           decay, ctx_decay, seq_decay, all_decay, ctx_send, ctx_recv, ctx_own, dp_send, dp_recv, dp_own):
    me = lax.axis_index("ctx")
    row = lax.axis_index("dp")
    xx, zz, cc, zc = me // 4, me // 2 % 2, me % 2, me % 4
    core_peer = me + 1 - 2 * cc
    z_peer = me + 2 - 4 * zz
    first, second = pl.ds(0, HALF), pl.ds(HALF, HALF)

    def remote(src, dst, send_sem, recv_sem, peer):
        return pltpu.make_async_remote_copy(
            src_ref=src, dst_ref=dst, send_sem=send_sem, recv_sem=recv_sem,
            device_id={"ctx": peer}, device_id_type=MESH,
        )

    def group_moves(plane, frm):
        cols = columns(plane, HEAD_DIM)
        return [
            (k.at[0, first, cols], lkv.at[0, early_rows(frm), :]),
            (v.at[0, first, cols], lkv.at[1, early_rows(frm), :]),
            (k.at[0, second, cols], lkv.at[0, late_rows(frm), :]),
            (v.at[0, second, cols], lkv.at[1, late_rows(frm), :]),
            (b.at[0, :, cols], lbc.at[0, device_rows(frm), :]),
            (c.at[0, :, cols], lbc.at[1, device_rows(frm), :]),
        ]

    def first_copy(kind, to, frm, peer):
        src, dst = group_moves(to // 4, frm)[kind]
        return remote(src, dst, first_send.at[kind, peer // 4], first_recv.at[kind, frm], peer)

    def landed(kind, src):
        return (
            lkv.at[:, early_rows(src), :],
            lkv.at[:, late_rows(src), :],
            lbc.at[:, device_rows(src), :],
        )[kind]

    def forward(kind, src, sems, peer):
        ref = landed(kind, src)
        return remote(ref, ref, sems.at[kind, src // 4], fwd_recv.at[kind, src], peer)

    def others_x(body):
        def one(n, _):
            body(lax.rem(xx + n, 4) * 4 + zc)
            return 0

        lax.fori_loop(1, 4, one, 0)

    def each_x(body):
        def one(n, _):
            body(lax.rem(xx + n, 4) * 4 + zc)
            return 0

        lax.fori_loop(0, 4, one, 0)

    def send_first(kinds):
        others_x(lambda to: [first_copy(kind, to, me, to).start() for kind in kinds])

    def q_copy(array, late, to, frm, peer):
        src = ((q, d)[array]).at[0, pl.ds(late * HALF, HALF), columns(to // 4 * 2 + to % 2, QCOLS)]
        dst = ((lq, ld)[array]).at[query_rows(frm, late), :]
        return remote(src, dst, q_send.at[2 * array + late, peer], q_recv.at[2 * array + late, frm], peer)

    def send_q(late):
        def one(n, _):
            to = lax.rem(xx + n // 2, 4) * 4 + 2 * zz + lax.rem(cc + n, 2)
            for array in range(2):
                q_copy(array, late, to, me, to).start()
            return 0

        lax.fori_loop(1, 8, one, 0)

    def q_arrived(src, late):
        @pl.when(src != me)
        def _():
            for array in range(2):
                q_copy(array, late, me, src, src).wait_recv()

    def x_in_copy(to, frm, peer):
        return remote(x.at[0, :, columns(slot(to), WIDTH)], lx.at[device_rows(frm), :],
                      x_in_send.at[peer], x_in_recv.at[frm], peer)

    def small_copy(to, frm, peer):
        return remote(small.at[to], ls.at[frm], small_send.at[peer], small_recv.at[frm], peer)

    def to_all(body):
        def one(n, _):
            body(lax.rem(me + n, CTX))
            return 0

        lax.fori_loop(1, CTX, one, 0)

    def own_copies():
        moves = group_moves(xx, me)
        for array in range(2):
            for late in range(2):
                moves.append((((q, d)[array]).at[0, pl.ds(late * HALF, HALF), columns(xx * 2 + cc, QCOLS)],
                              ((lq, ld)[array]).at[query_rows(me, late), :]))
        moves.append((x.at[0, :, columns(slot(me), WIDTH)], lx.at[device_rows(me), :]))
        moves.append((small.at[me], ls.at[me]))
        return [pltpu.make_async_copy(src, dst, own_sem.at[n]) for n, (src, dst) in enumerate(moves)]

    greet("ctx", CTX)
    greet("dp", DP)
    await_greetings(CTX - 1 + DP - 1)
    send_first((0, 1, 2, 3))
    own = own_copies()
    for copy in own[:-1]:
        copy.start()
    send_first((4, 5))
    send_q(1)
    pack_small(dvm, o, ids, step, alog, small)
    to_all(lambda to: small_copy(to, me, to).start())
    own[-1].start()

    @pl.when(me >= CTX // 2)
    def _():
        to_all(lambda to: x_in_copy(to, me, to).start())

    for copy in own:
        copy.wait()

    def pass_on(kinds, parts):
        def one(src):
            @pl.when(src != me)
            def _():
                for kind in kinds:
                    first_copy(kind, me, src, src).wait_recv()

            for part in parts:
                forward(part, src, z_send, z_peer).start()
                forward(part, src, core_send, core_peer).start()

        each_x(one)

    def relay(parts):
        def one(src):
            src = src + 2 - 4 * zz
            for part in parts:
                forward(part, src, z_send, z_peer).wait_recv()
                forward(part, src, relay_send, core_peer).start()

        each_x(one)

    pass_on((0, 1, 2, 3), (KV_EARLY, KV_LATE))
    pass_on((4, 5), (BC,))
    relay((KV_EARLY, KV_LATE))
    send_q(0)

    @pl.when(me < CTX // 2)
    def _():
        to_all(lambda to: x_in_copy(to, me, to).start())

    for ref in (dkv, gstate, gtimed, acc_a, acc_s):
        ref[...] = jnp.zeros(ref.shape, F32)
    skip[...] = dot(jnp.broadcast_to(skip_in[...], (8, SSM_HEADS)), own_heads(me), NN, HIGHEST)
    spread_matrix(spread)

    to_all(lambda src: small_copy(me, src, src).wait_recv())
    spread_columns(ls, doccol)

    def from_core(parts):
        def one(src):
            for flip in (0, 1):
                at = src + 1 - 2 * cc + flip * (2 - 4 * zz)
                for part in parts:
                    forward(part, at, core_send, core_peer).wait_recv()

        each_x(one)

    from_core((KV_EARLY, KV_LATE))
    relay((BC,))
    transpose_keys(lkv, kt)

    def x_copy(to, frm, peer):
        return remote(dx.at[device_rows(to), :], grad_x.at[0, :, columns(slot(frm), WIDTH)],
                      x_send.at[peer], x_recv.at[frm], peer)

    def x_mine():
        return pltpu.make_async_copy(dx.at[device_rows(me), :], grad_x.at[0, :, columns(slot(me), WIDTH)], x_own)

    def own_off(i):
        late = i // 4
        return (zz + late - 2 * zz * late) * ROWS

    def cot_copy(i, off):
        return remote(cot_out.at[i], cot.at[pl.ds(pl.multiple_of(i * BLOCK + off, ROWS), ROWS), :],
                      cot_send.at[i], cot_recv.at[i], z_peer)

    def pair_copy(i, which):
        return remote(dkv.at[which, block_rows(i), :], pair_in.at[i], pair_send.at[i], pair_recv.at[i], core_peer)

    def half_copy(i):
        return remote(half_out.at[i], half_in.at[i], half_send.at[i], half_recv.at[i], z_peer)

    def done_owner(i, r):
        late = i // 4
        chunk = 4 * i + own_off(i) // HALF + r
        return chunk + late * (2 * CTX - 1 - 2 * chunk)

    def done_copy(i, r, core, plane, late, peer):
        return remote(done.at[i, pl.ds(r * HALF, HALF), :],
                      grad_kv.at[core, pl.ds(pl.multiple_of(late * HALF, HALF), HALF), columns(plane, HEAD_DIM)],
                      done_send.at[i, r], done_recv.at[core, late, plane], peer)

    def done_mine(i, r):
        late = i // 4
        return pltpu.make_async_copy(
            done.at[i, pl.ds(r * HALF, HALF), :],
            grad_kv.at[cc, pl.ds(pl.multiple_of(late * HALF, HALF), HALF), columns(xx, HEAD_DIM)],
            done_own.at[late],
        )

    def sum_pair(i):
        pair_copy(i, 1 - cc).wait_recv()
        off = ROWS - own_off(i)
        there = pl.ds(pl.multiple_of(i * BLOCK + off, ROWS), ROWS)
        half_out[i] = (dkv[cc, there, :] + pair_in[i, pl.ds(pl.multiple_of(off, ROWS), ROWS), :]).astype(BF16)
        half_copy(i).start()

    def sum_half(i):
        half_copy(i).wait_recv()
        off = own_off(i)
        there = pl.ds(pl.multiple_of(i * BLOCK + off, ROWS), ROWS)
        mine = dkv[cc, there, :] + pair_in[i, pl.ds(pl.multiple_of(off, ROWS), ROWS), :]
        done[i] = (mine + half_in[i].astype(F32)).astype(BF16)
        for r in range(2):
            owner = done_owner(i, r)

            @pl.when(owner != me)
            def _():
                done_copy(i, r, cc, xx, i // 4, owner).start()

            @pl.when(owner == me)
            def _():
                done_mine(i, r).start()

    def block(n, _):
        @pl.when(n < BLOCKS)
        def _():
            i = BLOCKS - 1 - n
            off = own_off(i)

            @pl.when(i >= 4)
            def _():
                for r in range(2):
                    q_arrived(4 * (7 - i) + 2 * zz + r, 1)

            @pl.when(i < 4)
            def _():
                for r in range(2):
                    q_arrived(4 * i + 2 * zz + r, 0)

            for whole in (True, False):
                @pl.when((i >= SPAN - 1) == whole)
                def _():
                    attention_block(i, off, zz, lq, ld, lkv, kt, ls, doccol, dkv, q2, d2, qt, dt, s_ref, dq, whole)

            pair_copy(i, 1 - cc).start()
            here = pl.ds(pl.multiple_of(i * BLOCK + off, ROWS), ROWS)
            for e in range(2):
                cols = slice(e * HEAD_DIM, (e + 1) * HEAD_DIM)
                cot[here, cols] = dq[:, columns(2 * zz + e, ROWS)].T.astype(BF16)
                cot_out[i, :, cols] = dq[:, columns(2 - 2 * zz + e, ROWS)].T.astype(BF16)
            cot_copy(i, off).start()

        @pl.when(n == 1)
        def _():
            from_core((BC,))

        @pl.when(n >= 1)
        def _():
            sum_pair(BLOCKS - n)

        @pl.when(n >= 2)
        def _():
            sum_half(BLOCKS + 1 - n)

        @pl.when(n >= 1)
        def _():
            i = BLOCKS - n
            cot_copy(i, ROWS - own_off(i)).wait_recv()
            for sub in (1, 0):
                owner = 2 * i + sub

                @pl.when(owner != me)
                def _():
                    x_in_copy(me, owner, owner).wait_recv()

                ssm_chunk(owner, lx, lbc, ls, doccol, cot, skip, spread, gstate, gtimed, acc_a, acc_s, dx)

                @pl.when(owner != me)
                def _():
                    x_copy(owner, me, owner).start()

                @pl.when(owner == me)
                def _():
                    x_mine().start()

        return 0

    lax.fori_loop(0, BLOCKS + 1, block, 0)

    decay[...] = finish_decay(me, acc_a, acc_s)

    def ctx_copy(frm, peer):
        return remote(decay, ctx_decay.at[frm], ctx_send.at[peer], ctx_recv.at[frm], peer)

    def dp_copy(frm, peer):
        return pltpu.make_async_remote_copy(
            src_ref=seq_decay, dst_ref=all_decay.at[frm], send_sem=dp_send.at[peer], recv_sem=dp_recv.at[frm],
            device_id={"dp": peer}, device_id_type=MESH,
        )

    to_all(lambda to: ctx_copy(me, to).start())
    ctx_mine = pltpu.make_async_copy(decay, ctx_decay.at[me], ctx_own)
    ctx_mine.start()
    sum_half(0)
    to_all(lambda frm: ctx_copy(frm, frm).wait_recv())
    ctx_mine.wait()
    seq_decay[...] = jnp.sum(ctx_decay[...], axis=0)

    def start_dp(off, _):
        dp_copy(row, lax.rem(row + off, DP)).start()
        return 0

    lax.fori_loop(1, DP, start_dp, 0)
    dp_mine = pltpu.make_async_copy(seq_decay, all_decay.at[row], dp_own)
    dp_mine.start()

    def sent(to):
        small_copy(to, me, to).wait_send()
        x_in_copy(to, me, to).wait_send()
        x_copy(to, me, to).wait_send()
        ctx_copy(me, to).wait_send()

    to_all(sent)
    others_x(lambda to: [first_copy(kind, to, me, to).wait_send() for kind in range(6)])

    def forwarded(src):
        other = src + 2 - 4 * zz
        for part in range(3):
            forward(part, src, z_send, z_peer).wait_send()
            forward(part, src, core_send, core_peer).wait_send()
            forward(part, other, relay_send, core_peer).wait_send()

    each_x(forwarded)

    def sent_q(n, _):
        to = lax.rem(xx + n // 2, 4) * 4 + 2 * zz + lax.rem(cc + n, 2)
        for array in range(2):
            for late in range(2):
                q_copy(array, late, to, me, to).wait_send()
        return 0

    lax.fori_loop(1, 8, sent_q, 0)

    def sent_blocks(i, _):
        cot_copy(i, own_off(i)).wait_send()
        pair_copy(i, 1 - cc).wait_send()
        half_copy(i).wait_send()
        for r in range(2):
            owner = done_owner(i, r)

            @pl.when(owner != me)
            def _():
                done_copy(i, r, cc, xx, i // 4, owner).wait_send()

            @pl.when(owner == me)
            def _():
                done_mine(i, r).wait()

        return 0

    lax.fori_loop(0, BLOCKS, sent_blocks, 0)

    for core in range(2):
        for late in range(2):
            for plane in range(4):
                @pl.when(plane * 4 + 2 * zz + core != me)
                def _():
                    done_copy(0, 0, core, plane, late, core_peer).wait_recv()

    def end_dp(off, _):
        frm = lax.rem(row + DP - off, DP)
        dp_copy(frm, frm).wait_recv()
        dp_copy(row, frm).wait_send()
        return 0

    lax.fori_loop(1, DP, end_dp, 0)
    dp_mine.wait()
    total = all_decay[0]
    for other in range(1, DP):
        total += all_decay[other]
    grad_d[...] = total[:2]
    to_all(lambda frm: x_copy(me, frm, frm).wait_recv())
    x_mine().wait()


DMA = pltpu.SemaphoreType.DMA
SCRATCH = [
    pltpu.VMEM((SEQ // 2, QCOLS), BF16),
    pltpu.VMEM((SEQ // 2, QCOLS), BF16),
    pltpu.VMEM((2, SEQ, HEAD_DIM), BF16),
    pltpu.VMEM((2, SEQ, STATE), BF16),
    pltpu.VMEM((SEQ, WIDTH), BF16),
    pltpu.VMEM((CTX, 24, ROWS), F32),
    pltpu.VMEM((CTX, 24, ROWS), F32),
    DMA((CTX,)),
    DMA((CTX,)),
    DMA((CTX,)),
    DMA((CTX,)),
    DMA((6, 4)),
    DMA((6, CTX)),
    DMA((3, 4)),
    DMA((3, 4)),
    DMA((3, 4)),
    DMA((3, CTX)),
    DMA((4, CTX)),
    DMA((4, CTX)),
    DMA((12,)),
    pltpu.VMEM((2, SEQ, HEAD_DIM), F32),
    pltpu.VMEM((4 * ROWS, HEAD_DIM), BF16),
    pltpu.VMEM((4 * ROWS, HEAD_DIM), BF16),
    pltpu.VMEM((HEAD_DIM, 4 * ROWS), BF16),
    pltpu.VMEM((HEAD_DIM, 4 * ROWS), BF16),
    pltpu.VMEM((HEAD_DIM, SEQ), BF16),
    pltpu.VMEM((SPAN, BLOCK, 4 * ROWS), F32),
    pltpu.VMEM((HEAD_DIM, 4 * ROWS), F32),
    pltpu.VMEM((SEQ + 8, ROWS), F32),
    pltpu.VMEM((48, 1536), BF16),
    pltpu.VMEM((STATE, WIDTH), F32),
    pltpu.VMEM((STATE, WIDTH), F32),
    pltpu.VMEM((ROWS, WIDTH), F32),
    pltpu.VMEM((ROWS, WIDTH), F32),
    pltpu.VMEM((8, WIDTH), F32),
    pltpu.VMEM((SEQ, WIDTH), BF16),
    DMA((CTX,)),
    DMA((CTX,)),
    DMA,
    pltpu.VMEM((SEQ, WIDTH), BF16),
    pltpu.VMEM((BLOCKS, ROWS, WIDTH), BF16),
    DMA((BLOCKS,)),
    DMA((BLOCKS,)),
    pltpu.VMEM((BLOCKS, BLOCK, HEAD_DIM), F32),
    DMA((BLOCKS,)),
    DMA((BLOCKS,)),
    pltpu.VMEM((BLOCKS, ROWS, HEAD_DIM), BF16),
    pltpu.VMEM((BLOCKS, ROWS, HEAD_DIM), BF16),
    DMA((BLOCKS,)),
    DMA((BLOCKS,)),
    pltpu.VMEM((BLOCKS, ROWS, HEAD_DIM), BF16),
    DMA((BLOCKS, 2)),
    DMA((2, 2, 4)),
    DMA((2,)),
    pltpu.VMEM((8, SSM_HEADS), F32),
    pltpu.VMEM((CTX, 8, SSM_HEADS), F32),
    pltpu.VMEM((8, SSM_HEADS), F32),
    pltpu.VMEM((DP, 8, SSM_HEADS), F32),
    DMA((CTX,)),
    DMA((CTX,)),
    DMA,
    DMA((DP,)),
    DMA((DP,)),
    DMA,
]


def gradients(q, k, v, o, d, ids, x, b, c, step, alog, skip):
    hbm = pl.BlockSpec(memory_space=pl.ANY)
    vmem = pl.BlockSpec(memory_space=pltpu.VMEM)
    return pl.pallas_call(
        kernel,
        out_shape=[
            jax.ShapeDtypeStruct((1, ROWS, SSM_HEADS * SSM_DIM), BF16),
            jax.ShapeDtypeStruct((2, ROWS, KVHEADS * HEAD_DIM), BF16),
            jax.ShapeDtypeStruct((2, SSM_HEADS), F32),
        ],
        in_specs=[hbm] * 7 + [vmem] * 6,
        out_specs=[hbm, hbm, vmem],
        scratch_shapes=SCRATCH,
        compiler_params=pltpu.CompilerParams(
            collective_id=0, has_side_effects=True, vmem_limit_bytes=60 * 2**20
        ),
        name="gradients",
    )(q, d, k, v, x, b, c, d, o, ids, step, alog, skip)


def settle_kernel(x, kv, dec, grad_k, grad_v, grad_x, grad_d):
    grad_x[...] = x[...]
    grad_k[0] = kv[0]
    grad_v[0] = kv[1]
    grad_d[...] = dec[...]


def settle(x, kv, dec):
    vmem = pl.BlockSpec(memory_space=pltpu.VMEM)
    narrow = jax.ShapeDtypeStruct((1, ROWS, KVHEADS * HEAD_DIM), BF16)
    return pl.pallas_call(
        settle_kernel,
        out_shape=[narrow, narrow, jax.ShapeDtypeStruct(x.shape, BF16), jax.ShapeDtypeStruct(dec.shape, F32)],
        in_specs=[vmem] * 3,
        out_specs=[vmem] * 4,
        compiler_params=pltpu.CompilerParams(vmem_limit_bytes=60 * 2**20),
        name="settle",
    )(x, kv, dec)


def shards(queries, keys, values, saved, out_grad, doc_ids, inputs, bmat, cmat, step, alog, skip):
    return tuple(settle(*gradients(
        queries, keys, values, saved, out_grad, doc_ids, inputs, bmat, cmat, step, alog[None], skip[None]
    )))


def solution(mesh):
    return jax.shard_map(
        shards,
        mesh=mesh,
        in_specs=(
            P("dp", "ctx", None),
            P("dp", "ctx", None),
            P("dp", "ctx", None),
            P("dp", "ctx", None),
            P("dp", "ctx", None),
            P("dp", "ctx"),
            P("dp", "ctx", None),
            P("dp", "ctx", None),
            P("dp", "ctx", None),
            P("dp", "ctx", None),
            P(),
            P(),
        ),
        out_specs=(P("dp", "ctx", None), P("dp", "ctx", None), P("dp", "ctx", None), P()),
        check_vma=False,
    )
```

```python
import jax
import jax.numpy as jnp
from jax import lax
from jax.experimental import pallas as pl
from jax.experimental.pallas import tpu as pltpu
from jax.sharding import PartitionSpec as P

QHEADS = 32
KVHEADS = 4
HEAD_DIM = 128
SSM_HEADS = 128
SSM_DIM = 32
STATE = 128
SEQ = 2048
ROWS = 128
HALF = 64
CTX = 16
DP = 8
WIDTH = 256
OWN = 8
QCOLS = 512
BLOCK = 256
SPAN = 5
SCALE = HEAD_DIM ** (-0.5)
FAR = -1e30

MESH = pl.DeviceIdType.MESH
HIGHEST = lax.Precision.HIGHEST
F32 = jnp.float32
BF16 = jnp.bfloat16


def dot(a, b, dims, precision=None):
    return lax.dot_general(a, b, (dims, ((), ())), precision=precision, preferred_element_type=F32)


NN = ((1,), (0,))
NT = ((1,), (1,))
TN = ((0,), (0,))


def three(a):
    high = a.astype(BF16)
    rest = a - high.astype(F32)
    mid = rest.astype(BF16)
    low = (rest - mid.astype(F32)).astype(BF16)
    return high, mid, low


def greet(axis, count):
    me = lax.axis_index(axis)
    barrier = pltpu.get_barrier_semaphore()

    def one(off, _):
        pl.semaphore_signal(barrier, inc=1, device_id={axis: lax.rem(me + off, count)}, device_id_type=MESH)
        return 0

    lax.fori_loop(1, count, one, 0)


def await_greetings(total):
    pl.semaphore_wait(pltpu.get_barrier_semaphore(), total)


def slot(device):
    return device // 4 * 4 + device % 2 * 2 + device // 2 % 2


def early_rows(device):
    return pl.ds(pl.multiple_of(device * HALF, HALF), HALF)


def late_rows(device):
    return pl.ds(pl.multiple_of((2 * CTX - 1 - device) * HALF, HALF), HALF)


def device_rows(device):
    return pl.ds(pl.multiple_of(device * ROWS, ROWS), ROWS)


def block_rows(i):
    return pl.ds(pl.multiple_of(i * BLOCK, BLOCK), BLOCK)


def columns(start, width):
    return pl.ds(pl.multiple_of(start * width, width), width)


def pack_small(out_grad, saved, ids, step, alog, small):
    docs = jnp.broadcast_to(ids[...].astype(F32), (4, ROWS))
    rate = step[0] * -jnp.exp(alog[...])
    upto = lax.broadcasted_iota(jnp.int32, (ROWS, ROWS), 0) <= lax.broadcasted_iota(jnp.int32, (ROWS, ROWS), 1)
    totals = dot(rate, upto.astype(F32), TN, HIGHEST)
    steps = step[0].T
    lane = lax.broadcasted_iota(jnp.int32, (ROWS, ROWS), 1)
    deltas = jnp.zeros((ROWS, ROWS), F32)
    for h in range(QHEADS):
        cols = slice(h * HEAD_DIM, (h + 1) * HEAD_DIM)
        product = out_grad[0, :, cols].astype(F32) * saved[0, :, cols].astype(F32)
        deltas = jnp.where(lane == h, jnp.sum(product, axis=1, keepdims=True), deltas)
    deltas = deltas.T
    for j in range(CTX):
        at = 8 * slot(j)
        small[j, 0:8, :] = steps[at : at + 8]
        small[j, 8:16, :] = totals[at : at + 8]
        pair = 4 * (j // 4 * 2 + j % 2)
        small[j, 16:20, :] = deltas[pair : pair + 4]
        small[j, 20:24, :] = docs


def spread_columns(small, doccol):
    doccol[0:8, :] = jnp.full((8, ROWS), -1.0, F32)
    row = lax.broadcasted_iota(jnp.int32, (8, ROWS), 0)
    pick = jnp.where(row == 4, 1.0, 0.0).astype(BF16)

    def one(src, _):
        docs = jnp.where(row == 4, small[src, 16:24, :], 0.0).astype(BF16)
        doccol[pl.ds(pl.multiple_of(8 + src * ROWS, 8), ROWS), :] = dot(docs, pick, TN)
        return 0

    lax.fori_loop(0, CTX, one, 0)


def query_rows(src, late):
    block = src // 4 + late * (7 - 2 * (src // 4))
    second = src % 2 + late * (1 - 2 * (src % 2))
    return pl.ds(pl.multiple_of(block * ROWS + second * HALF, HALF), HALF)


def transpose_keys(kv, kt):
    def one(n, _):
        rows = device_rows(n)
        kt[:, rows] = kv[0, rows, :].T
        return 0

    lax.fori_loop(0, CTX, one, 0)


def attention_block(i, off, zz, q, d, kv, kt, small, doccol, dkv, q2, d2, qt, dt, s_ref, dq, whole):
    rows = device_rows(i)
    for h in range(4):
        part = pl.ds(h * ROWS, ROWS)
        q2[part, :] = q[rows, h * HEAD_DIM : (h + 1) * HEAD_DIM]
        d2[part, :] = d[rows, h * HEAD_DIM : (h + 1) * HEAD_DIM]
        qt[:, part] = q[rows, h * HEAD_DIM : (h + 1) * HEAD_DIM].T
        dt[:, part] = d[rows, h * HEAD_DIM : (h + 1) * HEAD_DIM].T
    dq[...] = jnp.zeros(dq.shape, F32)
    first = jnp.maximum(i - (SPAN - 1), 0)

    def each(body, carry):
        if not whole:
            return lax.fori_loop(0, i + 1 - first, body, carry)
        for n in range(SPAN):
            carry = body(n, carry)
        return carry

    ahead = lax.broadcasted_iota(jnp.int32, (BLOCK, ROWS), 1) - lax.broadcasted_iota(jnp.int32, (BLOCK, ROWS), 0)
    own = small[2 * i + off // ROWS, 20:21, :]
    late = i // 4
    plane = i + late * (7 - 2 * i)
    base = 4 * plane + 2 * zz
    lo, hi = small[base + late, 16:24, :], small[base + 1 - late, 16:24, :]
    left = lax.broadcasted_iota(jnp.int32, (8, ROWS), 1) < HALF
    early_tile = jnp.where(left, lo, jnp.roll(hi, HALF, 1))
    late_tile = jnp.where(left, jnp.roll(lo, HALF, 1), hi)
    tile = jnp.where(late == 1, late_tile, early_tile)
    delta = jnp.concatenate([tile[h : h + 1, :] for h in range(4)], axis=1)

    def scores(n, m):
        j = first + n
        keys = kv[0, block_rows(j), :]
        theirs = doccol[pl.ds(pl.multiple_of(8 + j * BLOCK, 8), BLOCK), :]
        allowed = (own == theirs) & (ahead >= (j - i) * BLOCK - off)
        parts = []
        for half in range(2):
            s = dot(keys, qt[:, pl.ds(half * BLOCK, BLOCK)], NN)
            s = jnp.where(jnp.concatenate([allowed, allowed], axis=1), s, FAR)
            s_ref[n, :, pl.ds(half * BLOCK, BLOCK)] = s
            parts.append(jnp.max(s.reshape(BLOCK // 8, 8, BLOCK), axis=0))
        return jnp.maximum(m, jnp.concatenate(parts, axis=1))

    m = each(scores, jnp.full((8, 4 * ROWS), FAR, F32))
    m = jnp.max(m, axis=0, keepdims=True)

    def exps(n, total):
        parts = []
        for half in range(2):
            cols = pl.ds(half * BLOCK, BLOCK)
            e = jnp.exp((s_ref[n, :, cols] - m[:, half * BLOCK : (half + 1) * BLOCK]) * SCALE)
            s_ref[n, :, cols] = e
            parts.append(jnp.sum(e.reshape(BLOCK // 8, 8, BLOCK), axis=0))
        return total + jnp.concatenate(parts, axis=1)

    total = each(exps, jnp.zeros((8, 4 * ROWS), F32))
    inv = 1.0 / jnp.sum(total, axis=0, keepdims=True)

    def grads(n, _):
        j = first + n
        there = block_rows(j)
        vals, keys_t = kv[1, there, :], kt[:, there]
        probs, scaled = [], []
        for half in range(4):
            cols = slice(half * ROWS, (half + 1) * ROWS)
            p = s_ref[n, :, pl.ds(half * ROWS, ROWS)] * inv[:, cols]
            dp = dot(vals, dt[:, pl.ds(half * ROWS, ROWS)], NN) - delta[:, cols]
            ds = (p * dp * SCALE).astype(BF16)
            dq[:, cols] += dot(keys_t, ds, NN)
            probs.append(p.astype(BF16))
            scaled.append(ds)
        dkv[0, there, :] += dot(jnp.concatenate(scaled, axis=1), q2[...], NN)
        dkv[1, there, :] += dot(jnp.concatenate(probs, axis=1), d2[...], NN)
        return 0

    each(grads, 0)


def spread_matrix(spread):
    row = lax.broadcasted_iota(jnp.int32, spread.shape, 0)
    lane = lax.broadcasted_iota(jnp.int32, spread.shape, 1)
    head = row % OWN
    a = (lane < 1024) & (row < 24) & (lane // ROWS == head)
    b = (lane >= 1024) & (lane < 1280) & (row < 24) & ((lane - 1024) // SSM_DIM == head)
    c = (lane >= 1280) & (row >= 24) & ((lane - 1280) // SSM_DIM == head)
    spread[...] = jnp.where(a | b | c, 1.0, 0.0).astype(BF16)


def ssm_chunk(c, bcm, small, doccol, cot, skip, spread, gstate, gtimed, timed_out, dx):
    base = pl.multiple_of(c * ROWS, ROWS)
    here = pl.ds(base, ROWS)
    bc, cc = bcm[0, here, :], bcm[1, here, :]
    dyb = cot[here, :]
    dy = dyb.astype(F32)
    steps, totals = small[c, 0:8, :], small[c, 8:16, :]
    parts = jnp.concatenate([p.astype(F32) for p in three(totals) + three(steps)], axis=0).astype(BF16)
    wide = dot(parts, spread[...], TN)
    te, se = wide[:, 1024:1280], wide[:, 1280:1536]
    docs = doccol[pl.ds(pl.multiple_of(8 + base, 8), ROWS), :]
    before = doccol[pl.ds(7 + base, 1), :]
    last = doccol[pl.ds(7 + ROWS + base, 1), :]
    docrow = small[c, 20:21, :]
    sub = lax.broadcasted_iota(jnp.int32, (ROWS, ROWS), 0)
    lane = lax.broadcasted_iota(jnp.int32, (ROWS, ROWS), 1)
    inner = jnp.where((sub <= lane) & (docs == docrow), dot(bc, cc, NT), 0.0)

    plain, timed = [], []
    for half in range(2):
        dyh = dyb[:, half * 128 : half * 128 + 128]
        total = None
        for pair in range(2):
            tops, lows, rights = [], [], []
            for one in range(2):
                local = 2 * pair + one
                h = 4 * half + local
                gap = totals[h : h + 1, :] - wide[:, ROWS * h : ROWS * h + ROWS]
                w = inner * jnp.exp(gap)
                tops.append(w.astype(BF16))
                lows.append((w * gap).astype(BF16))
                rights.append(jnp.where(lane // SSM_DIM == local, dyh.astype(F32), 0.0).astype(BF16))
            left = jnp.concatenate([jnp.concatenate(tops, axis=1), jnp.concatenate(lows, axis=1)], axis=0)
            out = dot(left, jnp.concatenate(rights, axis=0), NN)
            total = out if total is None else total + out
        plain.append(total[:ROWS])
        timed.append(total[ROWS:])
    intra = jnp.concatenate(plain, axis=1)
    intra_t = jnp.concatenate(timed, axis=1)

    both = jnp.concatenate([gstate[...], gtimed[...]], axis=1).astype(BF16)
    inter = dot(bc, both, NN)
    te_last = te[ROWS - 1 : ROWS, :]
    docs2 = jnp.concatenate([docs, docs], axis=1)
    before2 = jnp.concatenate([before, before], axis=1)
    last2 = jnp.concatenate([last, last], axis=1)
    left_time = te_last - te
    leave = jnp.where(docs2 == last2, jnp.exp(left_time), 0.0)
    got = intra + leave * inter[:, :WIDTH]
    got_t = intra_t + leave * (left_time * inter[:, :WIDTH] + inter[:, WIDTH:])
    dx[here, :] = (se * got + skip[0:1, :] * dy).astype(BF16)
    timed_out[here, :] = se * got_t

    enter = jnp.where(docs2 == before2, jnp.exp(te), 0.0)
    dye = dy * enter
    fresh = dot(cc, jnp.concatenate([dye, dye * te], axis=1).astype(BF16), TN)
    whole = jnp.where(last2 == before2, jnp.exp(te_last), 0.0)
    old = gstate[...]
    gtimed[...] = whole * (gtimed[...] + te_last * old) + fresh[:, WIDTH:]
    gstate[...] = whole * old + fresh[:, :WIDTH]


def own_heads(me):
    row = lax.broadcasted_iota(jnp.int32, (SSM_HEADS, WIDTH), 0)
    lane = lax.broadcasted_iota(jnp.int32, (SSM_HEADS, WIDTH), 1)
    return jnp.where(lane // SSM_DIM + slot(me) * OWN == row, 1.0, 0.0)


def finish_decay(me, acc_a, acc_s):
    sums = jnp.concatenate(
        [jnp.sum(acc_a[...], axis=0, keepdims=True), jnp.sum(acc_s[...], axis=0, keepdims=True), jnp.zeros((6, WIDTH), F32)],
        axis=0,
    )
    return dot(sums, own_heads(me), NT, HIGHEST)


BLOCKS = SEQ // BLOCK
LAG = 1
KV_EARLY, KV_LATE, BC = range(3)


def kernel(q, d, k, v, x, b, c, dvm, o, ids, step, alog, skip_in,
           grad_x, grad_kv, grad_d, lx, hop, pass_x,
           lq, ld, lkv, lbc, xv, xv_sem, ls, small,
           x_in_send, x_in_recv, hop_send, hop_recv, hop_on_send, small_send, small_recv, first_send, first_recv,
           z_send, core_send, relay_send, fwd_recv, q_send, q_recv, own_sem,
           dkv, q2, d2, qt, dt, kt, s_ref, dq, doccol, spread, gstate, gtimed, timed, acc_a, acc_s, skip,
           dx, x_send, x_recv, x_own, pass_send, pass_recv, pass_on_send,
           cot, cot_out, cot_send, cot_recv,
           pair_in, pair_send, pair_recv, half_out, half_in, half_send, half_recv,
           done, done_send, done_recv, done_own,
           decay, ctx_decay, seq_decay, all_decay, ctx_send, ctx_recv, ctx_own, dp_send, dp_recv, dp_own):
    me = lax.axis_index("ctx")
    row = lax.axis_index("dp")
    xx, zz, cc, zc = me // 4, me // 2 % 2, me % 2, me % 4
    core_peer = me + 1 - 2 * cc
    z_peer = me + 2 - 4 * zz
    first, second = pl.ds(0, HALF), pl.ds(HALF, HALF)

    def remote(src, dst, send_sem, recv_sem, peer):
        return pltpu.make_async_remote_copy(
            src_ref=src, dst_ref=dst, send_sem=send_sem, recv_sem=recv_sem,
            device_id={"ctx": peer}, device_id_type=MESH,
        )

    def group_moves(plane, frm):
        cols = columns(plane, HEAD_DIM)
        return [
            (k.at[0, first, cols], lkv.at[0, early_rows(frm), :]),
            (v.at[0, first, cols], lkv.at[1, early_rows(frm), :]),
            (k.at[0, second, cols], lkv.at[0, late_rows(frm), :]),
            (v.at[0, second, cols], lkv.at[1, late_rows(frm), :]),
            (b.at[0, :, cols], lbc.at[0, device_rows(frm), :]),
            (c.at[0, :, cols], lbc.at[1, device_rows(frm), :]),
        ]

    def first_copy(kind, to, frm, peer):
        src, dst = group_moves(to // 4, frm)[kind]
        return remote(src, dst, first_send.at[kind, peer // 4], first_recv.at[kind, frm], peer)

    def landed(kind, src):
        return (
            lkv.at[:, early_rows(src), :],
            lkv.at[:, late_rows(src), :],
            lbc.at[:, device_rows(src), :],
        )[kind]

    def forward(kind, src, sems, peer):
        ref = landed(kind, src)
        return remote(ref, ref, sems.at[kind, src // 4], fwd_recv.at[kind, src], peer)

    def others_x(body):
        def one(n, _):
            body(lax.rem(xx + n, 4) * 4 + zc)
            return 0

        lax.fori_loop(1, 4, one, 0)

    def each_x(body):
        def one(n, _):
            body(lax.rem(xx + n, 4) * 4 + zc)
            return 0

        lax.fori_loop(0, 4, one, 0)

    def send_first(kinds):
        others_x(lambda to: [first_copy(kind, to, me, to).start() for kind in kinds])

    def q_copy(array, late, to, frm, peer):
        src = ((q, d)[array]).at[0, pl.ds(late * HALF, HALF), columns(to // 4 * 2 + to % 2, QCOLS)]
        dst = ((lq, ld)[array]).at[query_rows(frm, late), :]
        return remote(src, dst, q_send.at[2 * array + late, peer], q_recv.at[2 * array + late, frm], peer)

    def send_q(late):
        def one(n, _):
            to = lax.rem(xx + n // 2, 4) * 4 + 2 * zz + lax.rem(cc + n, 2)
            for array in range(2):
                q_copy(array, late, to, me, to).start()
            return 0

        lax.fori_loop(1, 8, one, 0)

    def q_arrived(src, late):
        @pl.when(src != me)
        def _():
            for array in range(2):
                q_copy(array, late, me, src, src).wait_recv()

    def x_in_copy(to, frm, peer):
        return remote(x.at[0, :, columns(slot(to), WIDTH)], lx.at[device_rows(frm), :],
                      x_in_send.at[peer], x_in_recv.at[frm], peer)

    def small_copy(to, frm, peer):
        return remote(small.at[to], ls.at[frm], small_send.at[peer], small_recv.at[frm], peer)

    def to_all(body):
        def one(n, _):
            body(lax.rem(me + n, CTX))
            return 0

        lax.fori_loop(1, CTX, one, 0)

    def own_copies():
        moves = group_moves(xx, me)
        for array in range(2):
            for late in range(2):
                moves.append((((q, d)[array]).at[0, pl.ds(late * HALF, HALF), columns(xx * 2 + cc, QCOLS)],
                              ((lq, ld)[array]).at[query_rows(me, late), :]))
        moves.append((x.at[0, :, columns(slot(me), WIDTH)], xv.at[device_rows(me), :]))
        moves.append((small.at[me], ls.at[me]))
        return [pltpu.make_async_copy(src, dst, own_sem.at[n]) for n, (src, dst) in enumerate(moves)]

    greet("ctx", CTX)
    greet("dp", DP)
    await_greetings(CTX - 1 + DP - 1)
    send_first((0, 1, 2, 3))
    own = own_copies()
    for copy in own[:-1]:
        copy.start()

    def direct_x_in(over, flip_z, flip_c):
        to = lax.rem(xx + over, 4) * 4 + 2 * lax.rem(zz + flip_z, 2) + lax.rem(cc + flip_c, 2)
        return x_in_copy(to, me, to)

    def hop_copy(over, core):
        to = lax.rem(xx + over, 4) * 4 + 2 - 2 * zz + core
        return remote(x.at[0, :, columns(slot(to), WIDTH)], hop.at[over - 1, core],
                      hop_send.at[over - 1, core], hop_recv.at[over - 1, core], z_peer)

    def hop_on(over, core):
        to = lax.rem(xx + over, 4) * 4 + 2 * zz + core
        return remote(hop.at[over - 1, core], lx.at[device_rows(z_peer), :],
                      hop_on_send.at[over - 1, core], x_in_recv.at[z_peer], to)

    direct_x_in(0, 1, 0).start()
    direct_x_in(0, 1, 1).start()

    @pl.when(xx >= 2)
    def _():
        send_first((4, 5))

    pack_small(dvm, o, ids, step, alog, small)
    to_all(lambda to: small_copy(to, me, to).start())
    own[-1].start()
    send_q(1)

    @pl.when(xx < 2)
    def _():
        send_first((4, 5))

    for copy in own:
        copy.wait()

    def planes(first, count, body):
        def one(n, _):
            body(n * 4 + zc)
            return 0

        lax.fori_loop(first, first + count, one, 0)

    def pass_on(kinds, parts, first, count):
        def one(src):
            @pl.when(src != me)
            def _():
                for kind in kinds:
                    first_copy(kind, me, src, src).wait_recv()

            for part in parts:
                forward(part, src, z_send, z_peer).start()
                forward(part, src, core_send, core_peer).start()

        planes(first, count, one)

    def relay(parts, first, count):
        def one(src):
            src = src + 2 - 4 * zz
            for part in parts:
                forward(part, src, z_send, z_peer).wait_recv()
                forward(part, src, relay_send, core_peer).start()

        planes(first, count, one)

    def from_core(parts, first, count):
        def one(src):
            for flip in (0, 1):
                at = src + 1 - 2 * cc + flip * (2 - 4 * zz)
                for part in parts:
                    forward(part, at, core_send, core_peer).wait_recv()

        planes(first, count, one)

    pass_on((0, 1, 2, 3), (KV_EARLY, KV_LATE), 0, 4)
    pass_on((4, 5), (BC,), 2, 2)
    send_q(0)
    for over in range(1, 4):
        for core in range(2):
            hop_copy(over, core).start()

    for ref in (dkv, gstate, gtimed, acc_a, acc_s):
        ref[...] = jnp.zeros(ref.shape, F32)
    skip[...] = dot(jnp.broadcast_to(skip_in[...], (8, SSM_HEADS)), own_heads(me), NN, HIGHEST)
    spread_matrix(spread)
    relay((KV_EARLY, KV_LATE), 0, 4)
    to_all(lambda src: small_copy(me, src, src).wait_recv())
    spread_columns(ls, doccol)
    from_core((KV_EARLY, KV_LATE), 0, 4)
    transpose_keys(lkv, kt)
    relay((BC,), 2, 2)

    def x_copy(to, frm, peer):
        return remote(dx.at[device_rows(to), :], grad_x.at[0, :, columns(slot(frm), WIDTH)],
                      x_send.at[peer], x_recv.at[frm], peer)

    def x_mine():
        return pltpu.make_async_copy(dx.at[device_rows(me), :], grad_x.at[0, :, columns(slot(me), WIDTH)], x_own)

    def pass_copy(i):
        return remote(dx.at[block_rows(i), :], pass_x.at[i // 2], pass_send.at[i // 2], pass_recv.at[i // 2], z_peer)

    def passed_copy(i, sub):
        owner = 2 * i + sub
        return remote(pass_x.at[i // 2, pl.ds(sub * ROWS, ROWS), :], grad_x.at[0, :, columns(slot(z_peer), WIDTH)],
                      pass_on_send.at[i // 2, sub], x_recv.at[z_peer], owner)

    def passes(i):
        return (i % 2 != zz) & (i // 2 != xx) & (i >= 2)

    def passed(i):
        return (i % 2 == zz) & (i // 2 != xx) & (i >= 2)

    def own_off(i):
        late = i // 4
        return (zz + late - 2 * zz * late) * ROWS

    def cot_copy(i, off):
        return remote(cot_out.at[i], cot.at[pl.ds(pl.multiple_of(i * BLOCK + off, ROWS), ROWS), :],
                      cot_send.at[i], cot_recv.at[i], z_peer)

    def pair_copy(i, which):
        return remote(dkv.at[which, block_rows(i), :], pair_in.at[i], pair_send.at[i], pair_recv.at[i], core_peer)

    def half_copy(i):
        return remote(half_out.at[i], half_in.at[i], half_send.at[i], half_recv.at[i], z_peer)

    def done_owner(i, r):
        late = i // 4
        chunk = 4 * i + own_off(i) // HALF + r
        return chunk + late * (2 * CTX - 1 - 2 * chunk)

    def done_copy(i, r, core, plane, late, peer):
        return remote(done.at[i, pl.ds(r * HALF, HALF), :],
                      grad_kv.at[core, pl.ds(pl.multiple_of(late * HALF, HALF), HALF), columns(plane, HEAD_DIM)],
                      done_send.at[i, r], done_recv.at[core, late, plane], peer)

    def done_mine(i, r):
        late = i // 4
        return pltpu.make_async_copy(
            done.at[i, pl.ds(r * HALF, HALF), :],
            grad_kv.at[cc, pl.ds(pl.multiple_of(late * HALF, HALF), HALF), columns(xx, HEAD_DIM)],
            done_own.at[late],
        )

    def sum_pair(i):
        pair_copy(i, 1 - cc).wait_recv()
        off = ROWS - own_off(i)
        there = pl.ds(pl.multiple_of(i * BLOCK + off, ROWS), ROWS)
        half_out[i] = (dkv[cc, there, :] + pair_in[i, pl.ds(pl.multiple_of(off, ROWS), ROWS), :]).astype(BF16)
        half_copy(i).start()

    def sum_half(i):
        half_copy(i).wait_recv()
        off = own_off(i)
        there = pl.ds(pl.multiple_of(i * BLOCK + off, ROWS), ROWS)
        mine = dkv[cc, there, :] + pair_in[i, pl.ds(pl.multiple_of(off, ROWS), ROWS), :]
        done[i] = (mine + half_in[i].astype(F32)).astype(BF16)
        for r in range(2):
            owner = done_owner(i, r)

            @pl.when(owner != me)
            def _():
                done_copy(i, r, cc, xx, i // 4, owner).start()

            @pl.when(owner == me)
            def _():
                done_mine(i, r).start()

    def block(n, _):
        @pl.when(n < BLOCKS)
        def _():
            i = BLOCKS - 1 - n
            off = own_off(i)

            @pl.when(i >= 4)
            def _():
                for r in range(2):
                    q_arrived(4 * (7 - i) + 2 * zz + r, 1)

            @pl.when(i < 4)
            def _():
                for r in range(2):
                    q_arrived(4 * i + 2 * zz + r, 0)

            for whole in (True, False):
                @pl.when((i >= SPAN - 1) == whole)
                def _():
                    attention_block(i, off, zz, lq, ld, lkv, kt, ls, doccol, dkv, q2, d2, qt, dt, s_ref, dq, whole)

            pair_copy(i, 1 - cc).start()
            here = pl.ds(pl.multiple_of(i * BLOCK + off, ROWS), ROWS)
            for e in range(2):
                cols = slice(e * HEAD_DIM, (e + 1) * HEAD_DIM)
                cot[here, cols] = dq[:, columns(2 * zz + e, ROWS)].T.astype(BF16)
                cot_out[i, :, cols] = dq[:, columns(2 - 2 * zz + e, ROWS)].T.astype(BF16)
            cot_copy(i, off).start()

        @pl.when(n == 0)
        def _():
            pass_on((4, 5), (BC,), 0, 2)
            direct_x_in(0, 0, 1).start()

        @pl.when((n >= 1) & (n < 4))
        def _():
            direct_x_in(n, 0, 0).start()
            direct_x_in(n, 0, 1).start()

        @pl.when((n >= 4) & (n < 7))
        def _():
            for core in range(2):
                hop_copy(n - 3, core).wait_recv()
                hop_on(n - 3, core).start()

        @pl.when((n >= 2) & passed(BLOCKS + 1 - n))
        def _():
            i = BLOCKS + 1 - n
            pass_copy(i).wait_recv()
            for sub in range(2):
                passed_copy(i, sub).start()

        @pl.when(n == 1)
        def _():
            from_core((BC,), 2, 2)

        @pl.when(n == 2)
        def _():
            relay((BC,), 0, 2)

        @pl.when(n == 4)
        def _():
            from_core((BC,), 0, 2)

        @pl.when((n >= 1) & (n <= BLOCKS))
        def _():
            sum_pair(BLOCKS - n)

        @pl.when(n >= 2)
        def _():
            sum_half(BLOCKS + 1 - n)

        @pl.when(n >= LAG)
        def _():
            i = BLOCKS - 1 + LAG - n
            cot_copy(i, ROWS - own_off(i)).wait_recv()
            for sub in (1, 0):
                owner = 2 * i + sub

                ssm_chunk(owner, lbc, ls, doccol, cot, skip, spread, gstate, gtimed, timed, dx)

                @pl.when((owner != me) & jnp.logical_not(passes(i)))
                def _():
                    x_copy(owner, me, owner).start()

                @pl.when(owner == me)
                def _():
                    x_mine().start()

            @pl.when(passes(i))
            def _():
                pass_copy(i).start()

        return 0

    lax.fori_loop(0, BLOCKS + LAG, block, 0)

    def take_in(src):
        return pltpu.make_async_copy(lx.at[device_rows(src), :], xv.at[device_rows(src), :], xv_sem.at[src])

    def landed_x(src):
        x_in_copy(me, src, src).wait_recv()
        take_in(src).start()

    to_all(landed_x)
    to_all(lambda src: take_in(src).wait())

    def gather(c, _):
        here = device_rows(c)
        xc = xv[here, :].astype(F32)
        acc_a[...] += xc * timed[here, :]
        acc_s[...] += xc * cot[here, :].astype(F32)
        return 0

    lax.fori_loop(0, CTX, gather, 0)
    decay[...] = finish_decay(me, acc_a, acc_s)

    def ctx_copy(frm, peer):
        return remote(decay, ctx_decay.at[frm], ctx_send.at[peer], ctx_recv.at[frm], peer)

    def dp_copy(frm, peer):
        return pltpu.make_async_remote_copy(
            src_ref=seq_decay, dst_ref=all_decay.at[frm], send_sem=dp_send.at[peer], recv_sem=dp_recv.at[frm],
            device_id={"dp": peer}, device_id_type=MESH,
        )

    to_all(lambda to: ctx_copy(me, to).start())
    ctx_mine = pltpu.make_async_copy(decay, ctx_decay.at[me], ctx_own)
    ctx_mine.start()
    sum_half(0)
    to_all(lambda frm: ctx_copy(frm, frm).wait_recv())
    ctx_mine.wait()
    seq_decay[...] = jnp.sum(ctx_decay[...], axis=0)

    def start_dp(off, _):
        dp_copy(row, lax.rem(row + off, DP)).start()
        return 0

    lax.fori_loop(1, DP, start_dp, 0)
    dp_mine = pltpu.make_async_copy(seq_decay, all_decay.at[row], dp_own)
    dp_mine.start()

    def sent(to):
        small_copy(to, me, to).wait_send()

        @pl.when(jnp.logical_not(passes(to // 2)))
        def _():
            x_copy(to, me, to).wait_send()

        ctx_copy(me, to).wait_send()

    to_all(sent)
    for over in range(4):
        for core in range(2):
            if over:
                hop_copy(over, core).wait_send()
                hop_on(over, core).wait_send()
            else:
                direct_x_in(0, 1, core).wait_send()
            if over or core:
                direct_x_in(over, 0, core).wait_send()
    others_x(lambda to: [first_copy(kind, to, me, to).wait_send() for kind in range(6)])

    def forwarded(src):
        other = src + 2 - 4 * zz
        for part in range(3):
            forward(part, src, z_send, z_peer).wait_send()
            forward(part, src, core_send, core_peer).wait_send()
            forward(part, other, relay_send, core_peer).wait_send()

    each_x(forwarded)

    def sent_q(n, _):
        to = lax.rem(xx + n // 2, 4) * 4 + 2 * zz + lax.rem(cc + n, 2)
        for array in range(2):
            for late in range(2):
                q_copy(array, late, to, me, to).wait_send()
        return 0

    lax.fori_loop(1, 8, sent_q, 0)

    def sent_blocks(i, _):
        @pl.when(passes(i))
        def _():
            pass_copy(i).wait_send()

        @pl.when(passed(i))
        def _():
            for sub in range(2):
                passed_copy(i, sub).wait_send()

        cot_copy(i, own_off(i)).wait_send()
        pair_copy(i, 1 - cc).wait_send()
        half_copy(i).wait_send()
        for r in range(2):
            owner = done_owner(i, r)

            @pl.when(owner != me)
            def _():
                done_copy(i, r, cc, xx, i // 4, owner).wait_send()

            @pl.when(owner == me)
            def _():
                done_mine(i, r).wait()

        return 0

    lax.fori_loop(0, BLOCKS, sent_blocks, 0)

    for core in range(2):
        for late in range(2):
            for plane in range(4):
                @pl.when(plane * 4 + 2 * zz + core != me)
                def _():
                    done_copy(0, 0, core, plane, late, core_peer).wait_recv()

    def end_dp(off, _):
        frm = lax.rem(row + DP - off, DP)
        dp_copy(frm, frm).wait_recv()
        dp_copy(row, frm).wait_send()
        return 0

    lax.fori_loop(1, DP, end_dp, 0)
    dp_mine.wait()
    total = all_decay[0]
    for other in range(1, DP):
        total += all_decay[other]
    grad_d[...] = total[:2]
    to_all(lambda frm: x_copy(me, frm, frm).wait_recv())
    x_mine().wait()


DMA = pltpu.SemaphoreType.DMA
SCRATCH = [
    pltpu.VMEM((SEQ // 2, QCOLS), BF16),
    pltpu.VMEM((SEQ // 2, QCOLS), BF16),
    pltpu.VMEM((2, SEQ, HEAD_DIM), BF16),
    pltpu.VMEM((2, SEQ, STATE), BF16),
    pltpu.VMEM((SEQ, WIDTH), BF16),
    DMA((CTX,)),
    pltpu.VMEM((CTX, 24, ROWS), F32),
    pltpu.VMEM((CTX, 24, ROWS), F32),
    DMA((CTX,)),
    DMA((CTX,)),
    DMA((3, 2)),
    DMA((3, 2)),
    DMA((3, 2)),
    DMA((CTX,)),
    DMA((CTX,)),
    DMA((6, 4)),
    DMA((6, CTX)),
    DMA((3, 4)),
    DMA((3, 4)),
    DMA((3, 4)),
    DMA((3, CTX)),
    DMA((4, CTX)),
    DMA((4, CTX)),
    DMA((12,)),
    pltpu.VMEM((2, SEQ, HEAD_DIM), F32),
    pltpu.VMEM((4 * ROWS, HEAD_DIM), BF16),
    pltpu.VMEM((4 * ROWS, HEAD_DIM), BF16),
    pltpu.VMEM((HEAD_DIM, 4 * ROWS), BF16),
    pltpu.VMEM((HEAD_DIM, 4 * ROWS), BF16),
    pltpu.VMEM((HEAD_DIM, SEQ), BF16),
    pltpu.VMEM((SPAN, BLOCK, 4 * ROWS), F32),
    pltpu.VMEM((HEAD_DIM, 4 * ROWS), F32),
    pltpu.VMEM((SEQ + 8, ROWS), F32),
    pltpu.VMEM((48, 1536), BF16),
    pltpu.VMEM((STATE, WIDTH), F32),
    pltpu.VMEM((STATE, WIDTH), F32),
    pltpu.VMEM((SEQ, WIDTH), F32),
    pltpu.VMEM((ROWS, WIDTH), F32),
    pltpu.VMEM((ROWS, WIDTH), F32),
    pltpu.VMEM((8, WIDTH), F32),
    pltpu.VMEM((SEQ, WIDTH), BF16),
    DMA((CTX,)),
    DMA((CTX,)),
    DMA,
    DMA((4,)),
    DMA((4,)),
    DMA((4, 2)),
    pltpu.VMEM((SEQ, WIDTH), BF16),
    pltpu.VMEM((BLOCKS, ROWS, WIDTH), BF16),
    DMA((BLOCKS,)),
    DMA((BLOCKS,)),
    pltpu.VMEM((BLOCKS, BLOCK, HEAD_DIM), F32),
    DMA((BLOCKS,)),
    DMA((BLOCKS,)),
    pltpu.VMEM((BLOCKS, ROWS, HEAD_DIM), BF16),
    pltpu.VMEM((BLOCKS, ROWS, HEAD_DIM), BF16),
    DMA((BLOCKS,)),
    DMA((BLOCKS,)),
    pltpu.VMEM((BLOCKS, ROWS, HEAD_DIM), BF16),
    DMA((BLOCKS, 2)),
    DMA((2, 2, 4)),
    DMA((2,)),
    pltpu.VMEM((8, SSM_HEADS), F32),
    pltpu.VMEM((CTX, 8, SSM_HEADS), F32),
    pltpu.VMEM((8, SSM_HEADS), F32),
    pltpu.VMEM((DP, 8, SSM_HEADS), F32),
    DMA((CTX,)),
    DMA((CTX,)),
    DMA,
    DMA((DP,)),
    DMA((DP,)),
    DMA,
]


def gradients(q, k, v, o, d, ids, x, b, c, step, alog, skip):
    hbm = pl.BlockSpec(memory_space=pl.ANY)
    vmem = pl.BlockSpec(memory_space=pltpu.VMEM)
    return pl.pallas_call(
        kernel,
        out_shape=[
            jax.ShapeDtypeStruct((1, ROWS, SSM_HEADS * SSM_DIM), BF16),
            jax.ShapeDtypeStruct((2, ROWS, KVHEADS * HEAD_DIM), BF16),
            jax.ShapeDtypeStruct((2, SSM_HEADS), F32),
            jax.ShapeDtypeStruct((SEQ, WIDTH), BF16),
            jax.ShapeDtypeStruct((3, 2, ROWS, WIDTH), BF16),
            jax.ShapeDtypeStruct((4, BLOCK, WIDTH), BF16),
        ],
        in_specs=[hbm] * 7 + [vmem] * 6,
        out_specs=[hbm, hbm, vmem, hbm, hbm, hbm],
        scratch_shapes=SCRATCH,
        compiler_params=pltpu.CompilerParams(
            collective_id=0, has_side_effects=True, vmem_limit_bytes=60 * 2**20
        ),
        name="gradients",
    )(q, d, k, v, x, b, c, d, o, ids, step, alog, skip)[:3]


def settle_kernel(x, kv, dec, grad_k, grad_v, grad_x, grad_d):
    grad_x[...] = x[...]
    grad_k[0] = kv[0]
    grad_v[0] = kv[1]
    grad_d[...] = dec[...]


def settle(x, kv, dec):
    vmem = pl.BlockSpec(memory_space=pltpu.VMEM)
    narrow = jax.ShapeDtypeStruct((1, ROWS, KVHEADS * HEAD_DIM), BF16)
    return pl.pallas_call(
        settle_kernel,
        out_shape=[narrow, narrow, jax.ShapeDtypeStruct(x.shape, BF16), jax.ShapeDtypeStruct(dec.shape, F32)],
        in_specs=[vmem] * 3,
        out_specs=[vmem] * 4,
        compiler_params=pltpu.CompilerParams(vmem_limit_bytes=60 * 2**20),
        name="settle",
    )(x, kv, dec)


def shards(queries, keys, values, saved, out_grad, doc_ids, inputs, bmat, cmat, step, alog, skip):
    return tuple(settle(*gradients(
        queries, keys, values, saved, out_grad, doc_ids, inputs, bmat, cmat, step, alog[None], skip[None]
    )))


def solution(mesh):
    return jax.shard_map(
        shards,
        mesh=mesh,
        in_specs=(
            P("dp", "ctx", None),
            P("dp", "ctx", None),
            P("dp", "ctx", None),
            P("dp", "ctx", None),
            P("dp", "ctx", None),
            P("dp", "ctx"),
            P("dp", "ctx", None),
            P("dp", "ctx", None),
            P("dp", "ctx", None),
            P("dp", "ctx", None),
            P(),
            P(),
        ),
        out_specs=(P("dp", "ctx", None), P("dp", "ctx", None), P("dp", "ctx", None), P()),
        check_vma=False,
    )
```

```python
import jax
import jax.numpy as jnp
from jax import lax
from jax.experimental import pallas as pl
from jax.experimental.pallas import tpu as pltpu
from jax.sharding import PartitionSpec as P

QHEADS = 32
KVHEADS = 4
HEAD_DIM = 128
SSM_HEADS = 128
SSM_DIM = 32
STATE = 128
SEQ = 2048
ROWS = 128
HALF = 64
CTX = 16
DP = 8
WIDTH = 256
OWN = 8
QCOLS = 512
BLOCK = 256
SPAN = 5
SCALE = HEAD_DIM ** (-0.5)
FAR = -1e30

MESH = pl.DeviceIdType.MESH
HIGHEST = lax.Precision.HIGHEST
F32 = jnp.float32
BF16 = jnp.bfloat16


def dot(a, b, dims, precision=None):
    return lax.dot_general(a, b, (dims, ((), ())), precision=precision, preferred_element_type=F32)


NN = ((1,), (0,))
NT = ((1,), (1,))
TN = ((0,), (0,))


def three(a):
    high = a.astype(BF16)
    rest = a - high.astype(F32)
    mid = rest.astype(BF16)
    low = (rest - mid.astype(F32)).astype(BF16)
    return high, mid, low


def greet(axis, count):
    me = lax.axis_index(axis)
    barrier = pltpu.get_barrier_semaphore()

    def one(off, _):
        pl.semaphore_signal(barrier, inc=1, device_id={axis: lax.rem(me + off, count)}, device_id_type=MESH)
        return 0

    lax.fori_loop(1, count, one, 0)


def await_greetings(total):
    pl.semaphore_wait(pltpu.get_barrier_semaphore(), total)


def slot(device):
    return device // 4 * 4 + device % 2 * 2 + device // 2 % 2


def early_rows(device):
    return pl.ds(pl.multiple_of(device * HALF, HALF), HALF)


def late_rows(device):
    return pl.ds(pl.multiple_of((2 * CTX - 1 - device) * HALF, HALF), HALF)


def device_rows(device):
    return pl.ds(pl.multiple_of(device * ROWS, ROWS), ROWS)


def block_rows(i):
    return pl.ds(pl.multiple_of(i * BLOCK, BLOCK), BLOCK)


def columns(start, width):
    return pl.ds(pl.multiple_of(start * width, width), width)


def pack_small(out_grad, saved, ids, step, alog, small):
    docs = jnp.broadcast_to(ids[...].astype(F32), (4, ROWS))
    rate = step[0] * -jnp.exp(alog[...])
    upto = lax.broadcasted_iota(jnp.int32, (ROWS, ROWS), 0) <= lax.broadcasted_iota(jnp.int32, (ROWS, ROWS), 1)
    totals = dot(rate, upto.astype(F32), TN, HIGHEST)
    steps = step[0].T
    lane = lax.broadcasted_iota(jnp.int32, (ROWS, ROWS), 1)
    deltas = jnp.zeros((ROWS, ROWS), F32)
    for h in range(QHEADS):
        cols = slice(h * HEAD_DIM, (h + 1) * HEAD_DIM)
        product = out_grad[0, :, cols].astype(F32) * saved[0, :, cols].astype(F32)
        deltas = jnp.where(lane == h, jnp.sum(product, axis=1, keepdims=True), deltas)
    deltas = deltas.T
    for j in range(CTX):
        at = 8 * slot(j)
        small[j, 0:8, :] = steps[at : at + 8]
        small[j, 8:16, :] = totals[at : at + 8]
        pair = 4 * (j // 4 * 2 + j % 2)
        small[j, 16:20, :] = deltas[pair : pair + 4]
        small[j, 20:24, :] = docs


def spread_columns(small, doccol):
    doccol[0:8, :] = jnp.full((8, ROWS), -1.0, F32)
    row = lax.broadcasted_iota(jnp.int32, (8, ROWS), 0)
    pick = jnp.where(row == 4, 1.0, 0.0).astype(BF16)

    def one(src, _):
        docs = jnp.where(row == 4, small[src, 16:24, :], 0.0).astype(BF16)
        doccol[pl.ds(pl.multiple_of(8 + src * ROWS, 8), ROWS), :] = dot(docs, pick, TN)
        return 0

    lax.fori_loop(0, CTX, one, 0)


def query_rows(src, late):
    block = src // 4 + late * (7 - 2 * (src // 4))
    second = src % 2 + late * (1 - 2 * (src % 2))
    return pl.ds(pl.multiple_of(block * ROWS + second * HALF, HALF), HALF)


def transpose_keys(kv, kt):
    def one(n, _):
        rows = device_rows(n)
        kt[:, rows] = kv[0, rows, :].T
        return 0

    lax.fori_loop(0, CTX, one, 0)


def attention_block(i, off, zz, q, d, kv, kt, small, doccol, dkv, q2, d2, qt, dt, s_ref, dq, whole):
    rows = device_rows(i)
    for h in range(4):
        part = pl.ds(h * ROWS, ROWS)
        q2[part, :] = q[rows, h * HEAD_DIM : (h + 1) * HEAD_DIM]
        d2[part, :] = d[rows, h * HEAD_DIM : (h + 1) * HEAD_DIM]
        qt[:, part] = q[rows, h * HEAD_DIM : (h + 1) * HEAD_DIM].T
        dt[:, part] = d[rows, h * HEAD_DIM : (h + 1) * HEAD_DIM].T
    dq[...] = jnp.zeros(dq.shape, F32)
    first = jnp.maximum(i - (SPAN - 1), 0)

    def each(body, carry):
        if not whole:
            return lax.fori_loop(0, i + 1 - first, body, carry)
        for n in range(SPAN):
            carry = body(n, carry)
        return carry

    ahead = lax.broadcasted_iota(jnp.int32, (BLOCK, ROWS), 1) - lax.broadcasted_iota(jnp.int32, (BLOCK, ROWS), 0)
    own = small[2 * i + off // ROWS, 20:21, :]
    late = i // 4
    plane = i + late * (7 - 2 * i)
    base = 4 * plane + 2 * zz
    lo, hi = small[base + late, 16:24, :], small[base + 1 - late, 16:24, :]
    left = lax.broadcasted_iota(jnp.int32, (8, ROWS), 1) < HALF
    early_tile = jnp.where(left, lo, jnp.roll(hi, HALF, 1))
    late_tile = jnp.where(left, jnp.roll(lo, HALF, 1), hi)
    tile = jnp.where(late == 1, late_tile, early_tile)
    delta = jnp.concatenate([tile[h : h + 1, :] for h in range(4)], axis=1)

    def scores(n, m):
        j = first + n
        keys = kv[0, block_rows(j), :]
        theirs = doccol[pl.ds(pl.multiple_of(8 + j * BLOCK, 8), BLOCK), :]
        allowed = (own == theirs) & (ahead >= (j - i) * BLOCK - off)
        parts = []
        for half in range(2):
            s = dot(keys, qt[:, pl.ds(half * BLOCK, BLOCK)], NN)
            s = jnp.where(jnp.concatenate([allowed, allowed], axis=1), s, FAR)
            s_ref[n, :, pl.ds(half * BLOCK, BLOCK)] = s
            parts.append(jnp.max(s.reshape(BLOCK // 8, 8, BLOCK), axis=0))
        return jnp.maximum(m, jnp.concatenate(parts, axis=1))

    m = each(scores, jnp.full((8, 4 * ROWS), FAR, F32))
    m = jnp.max(m, axis=0, keepdims=True)

    def exps(n, total):
        parts = []
        for half in range(2):
            cols = pl.ds(half * BLOCK, BLOCK)
            e = jnp.exp((s_ref[n, :, cols] - m[:, half * BLOCK : (half + 1) * BLOCK]) * SCALE)
            s_ref[n, :, cols] = e
            parts.append(jnp.sum(e.reshape(BLOCK // 8, 8, BLOCK), axis=0))
        return total + jnp.concatenate(parts, axis=1)

    total = each(exps, jnp.zeros((8, 4 * ROWS), F32))
    inv = 1.0 / jnp.sum(total, axis=0, keepdims=True)

    def grads(n, _):
        j = first + n
        there = block_rows(j)
        vals, keys_t = kv[1, there, :], kt[:, there]
        probs, scaled = [], []
        for half in range(4):
            cols = slice(half * ROWS, (half + 1) * ROWS)
            p = s_ref[n, :, pl.ds(half * ROWS, ROWS)] * inv[:, cols]
            dp = dot(vals, dt[:, pl.ds(half * ROWS, ROWS)], NN) - delta[:, cols]
            ds = (p * dp * SCALE).astype(BF16)
            dq[:, cols] += dot(keys_t, ds, NN)
            probs.append(p.astype(BF16))
            scaled.append(ds)
        dkv[0, there, :] += dot(jnp.concatenate(scaled, axis=1), q2[...], NN)
        dkv[1, there, :] += dot(jnp.concatenate(probs, axis=1), d2[...], NN)
        return 0

    each(grads, 0)


def spread_matrix(spread):
    row = lax.broadcasted_iota(jnp.int32, spread.shape, 0)
    lane = lax.broadcasted_iota(jnp.int32, spread.shape, 1)
    head = row % OWN
    a = (lane < 1024) & (row < 24) & (lane // ROWS == head)
    b = (lane >= 1024) & (lane < 1280) & (row < 24) & ((lane - 1024) // SSM_DIM == head)
    c = (lane >= 1280) & (row >= 24) & ((lane - 1280) // SSM_DIM == head)
    spread[...] = jnp.where(a | b | c, 1.0, 0.0).astype(BF16)


def ssm_chunk(c, bcm, small, doccol, cot, skip, spread, gstate, gtimed, timed_out, dx):
    base = pl.multiple_of(c * ROWS, ROWS)
    here = pl.ds(base, ROWS)
    bc, cc = bcm[0, here, :], bcm[1, here, :]
    dyb = cot[here, :]
    dy = dyb.astype(F32)
    steps, totals = small[c, 0:8, :], small[c, 8:16, :]
    parts = jnp.concatenate([p.astype(F32) for p in three(totals) + three(steps)], axis=0).astype(BF16)
    wide = dot(parts, spread[...], TN)
    te, se = wide[:, 1024:1280], wide[:, 1280:1536]
    docs = doccol[pl.ds(pl.multiple_of(8 + base, 8), ROWS), :]
    before = doccol[pl.ds(7 + base, 1), :]
    last = doccol[pl.ds(7 + ROWS + base, 1), :]
    docrow = small[c, 20:21, :]
    sub = lax.broadcasted_iota(jnp.int32, (ROWS, ROWS), 0)
    lane = lax.broadcasted_iota(jnp.int32, (ROWS, ROWS), 1)
    inner = jnp.where((sub <= lane) & (docs == docrow), dot(bc, cc, NT), 0.0)

    plain, timed = [], []
    for half in range(2):
        dyh = dyb[:, half * 128 : half * 128 + 128]
        total = None
        for pair in range(2):
            tops, lows, rights = [], [], []
            for one in range(2):
                local = 2 * pair + one
                h = 4 * half + local
                gap = totals[h : h + 1, :] - wide[:, ROWS * h : ROWS * h + ROWS]
                w = inner * jnp.exp(gap)
                tops.append(w.astype(BF16))
                lows.append((w * gap).astype(BF16))
                rights.append(jnp.where(lane // SSM_DIM == local, dyh.astype(F32), 0.0).astype(BF16))
            left = jnp.concatenate([jnp.concatenate(tops, axis=1), jnp.concatenate(lows, axis=1)], axis=0)
            out = dot(left, jnp.concatenate(rights, axis=0), NN)
            total = out if total is None else total + out
        plain.append(total[:ROWS])
        timed.append(total[ROWS:])
    intra = jnp.concatenate(plain, axis=1)
    intra_t = jnp.concatenate(timed, axis=1)

    both = jnp.concatenate([gstate[...], gtimed[...]], axis=1).astype(BF16)
    inter = dot(bc, both, NN)
    te_last = te[ROWS - 1 : ROWS, :]
    docs2 = jnp.concatenate([docs, docs], axis=1)
    before2 = jnp.concatenate([before, before], axis=1)
    last2 = jnp.concatenate([last, last], axis=1)
    left_time = te_last - te
    leave = jnp.where(docs2 == last2, jnp.exp(left_time), 0.0)
    got = intra + leave * inter[:, :WIDTH]
    got_t = intra_t + leave * (left_time * inter[:, :WIDTH] + inter[:, WIDTH:])
    dx[here, :] = (se * got + skip[0:1, :] * dy).astype(BF16)
    timed_out[here, :] = se * got_t

    enter = jnp.where(docs2 == before2, jnp.exp(te), 0.0)
    dye = dy * enter
    fresh = dot(cc, jnp.concatenate([dye, dye * te], axis=1).astype(BF16), TN)
    whole = jnp.where(last2 == before2, jnp.exp(te_last), 0.0)
    old = gstate[...]
    gtimed[...] = whole * (gtimed[...] + te_last * old) + fresh[:, WIDTH:]
    gstate[...] = whole * old + fresh[:, :WIDTH]


def own_heads(me):
    row = lax.broadcasted_iota(jnp.int32, (SSM_HEADS, WIDTH), 0)
    lane = lax.broadcasted_iota(jnp.int32, (SSM_HEADS, WIDTH), 1)
    return jnp.where(lane // SSM_DIM + slot(me) * OWN == row, 1.0, 0.0)


def finish_decay(me, acc_a, acc_s):
    sums = jnp.concatenate(
        [jnp.sum(acc_a[...], axis=0, keepdims=True), jnp.sum(acc_s[...], axis=0, keepdims=True), jnp.zeros((6, WIDTH), F32)],
        axis=0,
    )
    return dot(sums, own_heads(me), NT, HIGHEST)


BLOCKS = SEQ // BLOCK
LAG = 1
KV_EARLY, KV_LATE, BC = range(3)


def kernel(q, d, k, v, x, b, c, dvm, o, ids, step, alog, skip_in,
           grad_x, grad_kv, grad_d, lx, hop, pass_x,
           lq, ld, lkv, lbc, xv, xv_sem, ls, small,
           x_in_send, x_in_recv, hop_send, hop_recv, hop_on_send, small_send, small_recv, first_send, first_recv,
           z_send, core_send, relay_send, fwd_recv, q_send, q_recv, own_sem,
           dkv, q2, d2, qt, dt, kt, s_ref, dq, doccol, spread, gstate, gtimed, timed, acc_a, acc_s, skip,
           dx, x_send, x_recv, x_own, pass_send, pass_recv, pass_on_send,
           cot, cot_out, cot_send, cot_recv,
           pair_in, pair_send, pair_recv, half_out, half_in, half_send, half_recv,
           done, done_send, done_recv, done_own,
           decay, ctx_decay, seq_decay, all_decay, ctx_send, ctx_recv, ctx_own, dp_send, dp_recv, dp_own):
    me = lax.axis_index("ctx")
    row = lax.axis_index("dp")
    xx, zz, cc, zc = me // 4, me // 2 % 2, me % 2, me % 4
    core_peer = me + 1 - 2 * cc
    z_peer = me + 2 - 4 * zz
    first, second = pl.ds(0, HALF), pl.ds(HALF, HALF)

    def remote(src, dst, send_sem, recv_sem, peer):
        return pltpu.make_async_remote_copy(
            src_ref=src, dst_ref=dst, send_sem=send_sem, recv_sem=recv_sem,
            device_id={"ctx": peer}, device_id_type=MESH,
        )

    def group_moves(plane, frm):
        cols = columns(plane, HEAD_DIM)
        return [
            (k.at[0, first, cols], lkv.at[0, early_rows(frm), :]),
            (v.at[0, first, cols], lkv.at[1, early_rows(frm), :]),
            (k.at[0, second, cols], lkv.at[0, late_rows(frm), :]),
            (v.at[0, second, cols], lkv.at[1, late_rows(frm), :]),
            (b.at[0, :, cols], lbc.at[0, device_rows(frm), :]),
            (c.at[0, :, cols], lbc.at[1, device_rows(frm), :]),
        ]

    def first_copy(kind, to, frm, peer):
        src, dst = group_moves(to // 4, frm)[kind]
        return remote(src, dst, first_send.at[kind, peer // 4], first_recv.at[kind, frm], peer)

    def landed(kind, src):
        return (
            lkv.at[:, early_rows(src), :],
            lkv.at[:, late_rows(src), :],
            lbc.at[:, device_rows(src), :],
        )[kind]

    def forward(kind, src, sems, peer):
        ref = landed(kind, src)
        return remote(ref, ref, sems.at[kind, src // 4], fwd_recv.at[kind, src], peer)

    def others_x(body):
        def one(n, _):
            body(lax.rem(xx + n, 4) * 4 + zc)
            return 0

        lax.fori_loop(1, 4, one, 0)

    def each_x(body):
        def one(n, _):
            body(lax.rem(xx + n, 4) * 4 + zc)
            return 0

        lax.fori_loop(0, 4, one, 0)

    def send_first(kinds):
        others_x(lambda to: [first_copy(kind, to, me, to).start() for kind in kinds])

    def q_copy(array, late, to, frm, peer):
        src = ((q, d)[array]).at[0, pl.ds(late * HALF, HALF), columns(to // 4 * 2 + to % 2, QCOLS)]
        dst = ((lq, ld)[array]).at[query_rows(frm, late), :]
        return remote(src, dst, q_send.at[2 * array + late, peer], q_recv.at[2 * array + late, frm], peer)

    def send_q(late):
        def one(n, _):
            to = lax.rem(xx + n // 2, 4) * 4 + 2 * zz + lax.rem(cc + n, 2)
            for array in range(2):
                q_copy(array, late, to, me, to).start()
            return 0

        lax.fori_loop(1, 8, one, 0)

    def q_arrived(src, late):
        @pl.when(src != me)
        def _():
            for array in range(2):
                q_copy(array, late, me, src, src).wait_recv()

    def x_in_copy(to, frm, peer):
        return remote(x.at[0, :, columns(slot(to), WIDTH)], lx.at[device_rows(frm), :],
                      x_in_send.at[peer], x_in_recv.at[frm], peer)

    def small_copy(to, frm, peer):
        return remote(small.at[to], ls.at[frm], small_send.at[peer], small_recv.at[frm], peer)

    def to_all(body):
        def one(n, _):
            body(lax.rem(me + n, CTX))
            return 0

        lax.fori_loop(1, CTX, one, 0)

    def own_copies():
        moves = group_moves(xx, me)
        for array in range(2):
            for late in range(2):
                moves.append((((q, d)[array]).at[0, pl.ds(late * HALF, HALF), columns(xx * 2 + cc, QCOLS)],
                              ((lq, ld)[array]).at[query_rows(me, late), :]))
        moves.append((x.at[0, :, columns(slot(me), WIDTH)], xv.at[device_rows(me), :]))
        moves.append((small.at[me], ls.at[me]))
        return [pltpu.make_async_copy(src, dst, own_sem.at[n]) for n, (src, dst) in enumerate(moves)]

    greet("ctx", CTX)
    greet("dp", DP)
    await_greetings(CTX - 1 + DP - 1)
    send_first((0, 1, 2, 3))
    own = own_copies()
    for copy in own[:-1]:
        copy.start()

    def direct_x_in(over, flip_z, flip_c):
        to = lax.rem(xx + over, 4) * 4 + 2 * lax.rem(zz + flip_z, 2) + lax.rem(cc + flip_c, 2)
        return x_in_copy(to, me, to)

    def hop_copy(over, core):
        to = lax.rem(xx + over, 4) * 4 + 2 - 2 * zz + core
        return remote(x.at[0, :, columns(slot(to), WIDTH)], hop.at[over - 1, core],
                      hop_send.at[over - 1, core], hop_recv.at[over - 1, core], z_peer)

    def hop_on(over, core):
        to = lax.rem(xx + over, 4) * 4 + 2 * zz + core
        return remote(hop.at[over - 1, core], lx.at[device_rows(z_peer), :],
                      hop_on_send.at[over - 1, core], x_in_recv.at[z_peer], to)

    direct_x_in(0, 1, 0).start()
    direct_x_in(0, 1, 1).start()

    @pl.when(xx >= 2)
    def _():
        send_first((4, 5))

    pack_small(dvm, o, ids, step, alog, small)
    to_all(lambda to: small_copy(to, me, to).start())
    own[-1].start()
    send_q(1)

    @pl.when(xx < 2)
    def _():
        send_first((4, 5))

    for copy in own:
        copy.wait()

    def planes(first, count, body):
        def one(n, _):
            body(n * 4 + zc)
            return 0

        lax.fori_loop(first, first + count, one, 0)

    def pass_on(kinds, parts, first, count):
        def one(src):
            @pl.when(src != me)
            def _():
                for kind in kinds:
                    first_copy(kind, me, src, src).wait_recv()

            for part in parts:
                forward(part, src, z_send, z_peer).start()
                forward(part, src, core_send, core_peer).start()

        planes(first, count, one)

    def relay(parts, first, count):
        def one(src):
            src = src + 2 - 4 * zz
            for part in parts:
                forward(part, src, z_send, z_peer).wait_recv()
                forward(part, src, relay_send, core_peer).start()

        planes(first, count, one)

    def from_core(parts, first, count):
        def one(src):
            for flip in (0, 1):
                at = src + 1 - 2 * cc + flip * (2 - 4 * zz)
                for part in parts:
                    forward(part, at, core_send, core_peer).wait_recv()

        planes(first, count, one)

    pass_on((0, 1, 2, 3), (KV_EARLY, KV_LATE), 0, 4)
    pass_on((4, 5), (BC,), 2, 2)
    send_q(0)
    for over in range(1, 4):
        for core in range(2):
            hop_copy(over, core).start()

    for ref in (dkv, gstate, gtimed, acc_a, acc_s):
        ref[...] = jnp.zeros(ref.shape, F32)
    skip[...] = dot(jnp.broadcast_to(skip_in[...], (8, SSM_HEADS)), own_heads(me), NN, HIGHEST)
    spread_matrix(spread)
    relay((KV_EARLY, KV_LATE), 0, 4)
    to_all(lambda src: small_copy(me, src, src).wait_recv())
    spread_columns(ls, doccol)
    from_core((KV_EARLY, KV_LATE), 0, 4)
    transpose_keys(lkv, kt)
    relay((BC,), 2, 2)

    def x_copy(to, frm, peer):
        return remote(dx.at[device_rows(to), :], grad_x.at[0, :, columns(slot(frm), WIDTH)],
                      x_send.at[peer], x_recv.at[frm], peer)

    def x_mine():
        return pltpu.make_async_copy(dx.at[device_rows(me), :], grad_x.at[0, :, columns(slot(me), WIDTH)], x_own)

    def pass_copy(i):
        return remote(dx.at[block_rows(i), :], pass_x.at[i // 2], pass_send.at[i // 2], pass_recv.at[i // 2], z_peer)

    def passed_copy(i, sub):
        owner = 2 * i + sub
        return remote(pass_x.at[i // 2, pl.ds(sub * ROWS, ROWS), :], grad_x.at[0, :, columns(slot(z_peer), WIDTH)],
                      pass_on_send.at[i // 2, sub], x_recv.at[z_peer], owner)

    def passes(i):
        return (i % 2 != zz) & (i // 2 != xx) & (i >= 2)

    def passed(i):
        return (i % 2 == zz) & (i // 2 != xx) & (i >= 2)

    def own_off(i):
        late = i // 4
        return (zz + late - 2 * zz * late) * ROWS

    def cot_copy(i, off):
        return remote(cot_out.at[i], cot.at[pl.ds(pl.multiple_of(i * BLOCK + off, ROWS), ROWS), :],
                      cot_send.at[i], cot_recv.at[i], z_peer)

    def pair_copy(i, which):
        return remote(dkv.at[which, block_rows(i), :], pair_in.at[i], pair_send.at[i], pair_recv.at[i], core_peer)

    def half_copy(i):
        return remote(half_out.at[i], half_in.at[i], half_send.at[i], half_recv.at[i], z_peer)

    def done_owner(i, r):
        late = i // 4
        chunk = 4 * i + own_off(i) // HALF + r
        return chunk + late * (2 * CTX - 1 - 2 * chunk)

    def done_copy(i, r, core, plane, late, peer):
        return remote(done.at[i, pl.ds(r * HALF, HALF), :],
                      grad_kv.at[core, pl.ds(pl.multiple_of(late * HALF, HALF), HALF), columns(plane, HEAD_DIM)],
                      done_send.at[i, r], done_recv.at[core, late, plane], peer)

    def done_mine(i, r):
        late = i // 4
        return pltpu.make_async_copy(
            done.at[i, pl.ds(r * HALF, HALF), :],
            grad_kv.at[cc, pl.ds(pl.multiple_of(late * HALF, HALF), HALF), columns(xx, HEAD_DIM)],
            done_own.at[late],
        )

    def sum_pair(i):
        pair_copy(i, 1 - cc).wait_recv()
        off = ROWS - own_off(i)
        there = pl.ds(pl.multiple_of(i * BLOCK + off, ROWS), ROWS)
        half_out[i] = (dkv[cc, there, :] + pair_in[i, pl.ds(pl.multiple_of(off, ROWS), ROWS), :]).astype(BF16)
        half_copy(i).start()

    def sum_half(i):
        half_copy(i).wait_recv()
        off = own_off(i)
        there = pl.ds(pl.multiple_of(i * BLOCK + off, ROWS), ROWS)
        mine = dkv[cc, there, :] + pair_in[i, pl.ds(pl.multiple_of(off, ROWS), ROWS), :]
        done[i] = (mine + half_in[i].astype(F32)).astype(BF16)
        for r in range(2):
            owner = done_owner(i, r)

            @pl.when(owner != me)
            def _():
                done_copy(i, r, cc, xx, i // 4, owner).start()

            @pl.when(owner == me)
            def _():
                done_mine(i, r).start()

    def take_in(src):
        return pltpu.make_async_copy(lx.at[device_rows(src), :], xv.at[device_rows(src), :], xv_sem.at[src])

    def landed_x(src):
        x_in_copy(me, src, src).wait_recv()
        take_in(src).start()

    def block(n, _):
        @pl.when(n < BLOCKS)
        def _():
            i = BLOCKS - 1 - n
            off = own_off(i)

            @pl.when(i >= 4)
            def _():
                for r in range(2):
                    q_arrived(4 * (7 - i) + 2 * zz + r, 1)

            @pl.when(i < 4)
            def _():
                for r in range(2):
                    q_arrived(4 * i + 2 * zz + r, 0)

            for whole in (True, False):
                @pl.when((i >= SPAN - 1) == whole)
                def _():
                    attention_block(i, off, zz, lq, ld, lkv, kt, ls, doccol, dkv, q2, d2, qt, dt, s_ref, dq, whole)

            pair_copy(i, 1 - cc).start()
            here = pl.ds(pl.multiple_of(i * BLOCK + off, ROWS), ROWS)
            for e in range(2):
                cols = slice(e * HEAD_DIM, (e + 1) * HEAD_DIM)
                cot[here, cols] = dq[:, columns(2 * zz + e, ROWS)].T.astype(BF16)
                cot_out[i, :, cols] = dq[:, columns(2 - 2 * zz + e, ROWS)].T.astype(BF16)
            cot_copy(i, off).start()

        @pl.when(n == 0)
        def _():
            pass_on((4, 5), (BC,), 0, 2)
            direct_x_in(0, 0, 1).start()

        @pl.when(n < 3)
        def _():
            direct_x_in(n + 1, 0, 0).start()
            direct_x_in(n + 1, 0, 1).start()

        @pl.when((n >= 2) & (n < 5))
        def _():
            for core in range(2):
                hop_copy(n - 1, core).wait_recv()
                hop_on(n - 1, core).start()

        @pl.when((n >= 2) & passed(BLOCKS + 1 - n))
        def _():
            i = BLOCKS + 1 - n
            pass_copy(i).wait_recv()
            for sub in range(2):
                passed_copy(i, sub).start()

        @pl.when(n == 1)
        def _():
            from_core((BC,), 2, 2)

        @pl.when(n == 2)
        def _():
            relay((BC,), 0, 2)

        @pl.when(n == 4)
        def _():
            from_core((BC,), 0, 2)

        @pl.when((n >= 1) & (n <= BLOCKS))
        def _():
            sum_pair(BLOCKS - n)

        @pl.when(n >= 2)
        def _():
            sum_half(BLOCKS + 1 - n)

        @pl.when(n == BLOCKS)
        def _():
            to_all(landed_x)

        @pl.when(n >= LAG)
        def _():
            i = BLOCKS - 1 + LAG - n
            cot_copy(i, ROWS - own_off(i)).wait_recv()
            for sub in (1, 0):
                owner = 2 * i + sub

                ssm_chunk(owner, lbc, ls, doccol, cot, skip, spread, gstate, gtimed, timed, dx)

                @pl.when((owner != me) & jnp.logical_not(passes(i)))
                def _():
                    x_copy(owner, me, owner).start()

                @pl.when(owner == me)
                def _():
                    x_mine().start()

            @pl.when(passes(i))
            def _():
                pass_copy(i).start()

        return 0

    lax.fori_loop(0, BLOCKS + LAG, block, 0)

    to_all(lambda src: take_in(src).wait())

    def gather(c, _):
        here = device_rows(c)
        xc = xv[here, :].astype(F32)
        acc_a[...] += xc * timed[here, :]
        acc_s[...] += xc * cot[here, :].astype(F32)
        return 0

    lax.fori_loop(0, CTX, gather, 0)
    decay[...] = finish_decay(me, acc_a, acc_s)

    def ctx_copy(frm, peer):
        return remote(decay, ctx_decay.at[frm], ctx_send.at[peer], ctx_recv.at[frm], peer)

    def dp_copy(frm, peer):
        return pltpu.make_async_remote_copy(
            src_ref=seq_decay, dst_ref=all_decay.at[frm], send_sem=dp_send.at[peer], recv_sem=dp_recv.at[frm],
            device_id={"dp": peer}, device_id_type=MESH,
        )

    to_all(lambda to: ctx_copy(me, to).start())
    ctx_mine = pltpu.make_async_copy(decay, ctx_decay.at[me], ctx_own)
    ctx_mine.start()
    sum_half(0)
    to_all(lambda frm: ctx_copy(frm, frm).wait_recv())
    ctx_mine.wait()
    seq_decay[...] = jnp.sum(ctx_decay[...], axis=0)

    def start_dp(off, _):
        dp_copy(row, lax.rem(row + off, DP)).start()
        return 0

    lax.fori_loop(1, DP, start_dp, 0)
    dp_mine = pltpu.make_async_copy(seq_decay, all_decay.at[row], dp_own)
    dp_mine.start()

    def sent(to):
        small_copy(to, me, to).wait_send()

        @pl.when(jnp.logical_not(passes(to // 2)))
        def _():
            x_copy(to, me, to).wait_send()

        ctx_copy(me, to).wait_send()

    to_all(sent)
    for over in range(4):
        for core in range(2):
            if over:
                hop_copy(over, core).wait_send()
                hop_on(over, core).wait_send()
            else:
                direct_x_in(0, 1, core).wait_send()
            if over or core:
                direct_x_in(over, 0, core).wait_send()
    others_x(lambda to: [first_copy(kind, to, me, to).wait_send() for kind in range(6)])

    def forwarded(src):
        other = src + 2 - 4 * zz
        for part in range(3):
            forward(part, src, z_send, z_peer).wait_send()
            forward(part, src, core_send, core_peer).wait_send()
            forward(part, other, relay_send, core_peer).wait_send()

    each_x(forwarded)

    def sent_q(n, _):
        to = lax.rem(xx + n // 2, 4) * 4 + 2 * zz + lax.rem(cc + n, 2)
        for array in range(2):
            for late in range(2):
                q_copy(array, late, to, me, to).wait_send()
        return 0

    lax.fori_loop(1, 8, sent_q, 0)

    def sent_blocks(i, _):
        @pl.when(passes(i))
        def _():
            pass_copy(i).wait_send()

        @pl.when(passed(i))
        def _():
            for sub in range(2):
                passed_copy(i, sub).wait_send()

        cot_copy(i, own_off(i)).wait_send()
        pair_copy(i, 1 - cc).wait_send()
        half_copy(i).wait_send()
        for r in range(2):
            owner = done_owner(i, r)

            @pl.when(owner != me)
            def _():
                done_copy(i, r, cc, xx, i // 4, owner).wait_send()

            @pl.when(owner == me)
            def _():
                done_mine(i, r).wait()

        return 0

    lax.fori_loop(0, BLOCKS, sent_blocks, 0)

    for core in range(2):
        for late in range(2):
            for plane in range(4):
                @pl.when(plane * 4 + 2 * zz + core != me)
                def _():
                    done_copy(0, 0, core, plane, late, core_peer).wait_recv()

    def end_dp(off, _):
        frm = lax.rem(row + DP - off, DP)
        dp_copy(frm, frm).wait_recv()
        dp_copy(row, frm).wait_send()
        return 0

    lax.fori_loop(1, DP, end_dp, 0)
    dp_mine.wait()
    total = all_decay[0]
    for other in range(1, DP):
        total += all_decay[other]
    grad_d[...] = total[:2]
    to_all(lambda frm: x_copy(me, frm, frm).wait_recv())
    x_mine().wait()


DMA = pltpu.SemaphoreType.DMA
SCRATCH = [
    pltpu.VMEM((SEQ // 2, QCOLS), BF16),
    pltpu.VMEM((SEQ // 2, QCOLS), BF16),
    pltpu.VMEM((2, SEQ, HEAD_DIM), BF16),
    pltpu.VMEM((2, SEQ, STATE), BF16),
    pltpu.VMEM((SEQ, WIDTH), BF16),
    DMA((CTX,)),
    pltpu.VMEM((CTX, 24, ROWS), F32),
    pltpu.VMEM((CTX, 24, ROWS), F32),
    DMA((CTX,)),
    DMA((CTX,)),
    DMA((3, 2)),
    DMA((3, 2)),
    DMA((3, 2)),
    DMA((CTX,)),
    DMA((CTX,)),
    DMA((6, 4)),
    DMA((6, CTX)),
    DMA((3, 4)),
    DMA((3, 4)),
    DMA((3, 4)),
    DMA((3, CTX)),
    DMA((4, CTX)),
    DMA((4, CTX)),
    DMA((12,)),
    pltpu.VMEM((2, SEQ, HEAD_DIM), F32),
    pltpu.VMEM((4 * ROWS, HEAD_DIM), BF16),
    pltpu.VMEM((4 * ROWS, HEAD_DIM), BF16),
    pltpu.VMEM((HEAD_DIM, 4 * ROWS), BF16),
    pltpu.VMEM((HEAD_DIM, 4 * ROWS), BF16),
    pltpu.VMEM((HEAD_DIM, SEQ), BF16),
    pltpu.VMEM((SPAN, BLOCK, 4 * ROWS), F32),
    pltpu.VMEM((HEAD_DIM, 4 * ROWS), F32),
    pltpu.VMEM((SEQ + 8, ROWS), F32),
    pltpu.VMEM((48, 1536), BF16),
    pltpu.VMEM((STATE, WIDTH), F32),
    pltpu.VMEM((STATE, WIDTH), F32),
    pltpu.VMEM((SEQ, WIDTH), F32),
    pltpu.VMEM((ROWS, WIDTH), F32),
    pltpu.VMEM((ROWS, WIDTH), F32),
    pltpu.VMEM((8, WIDTH), F32),
    pltpu.VMEM((SEQ, WIDTH), BF16),
    DMA((CTX,)),
    DMA((CTX,)),
    DMA,
    DMA((4,)),
    DMA((4,)),
    DMA((4, 2)),
    pltpu.VMEM((SEQ, WIDTH), BF16),
    pltpu.VMEM((BLOCKS, ROWS, WIDTH), BF16),
    DMA((BLOCKS,)),
    DMA((BLOCKS,)),
    pltpu.VMEM((BLOCKS, BLOCK, HEAD_DIM), F32),
    DMA((BLOCKS,)),
    DMA((BLOCKS,)),
    pltpu.VMEM((BLOCKS, ROWS, HEAD_DIM), BF16),
    pltpu.VMEM((BLOCKS, ROWS, HEAD_DIM), BF16),
    DMA((BLOCKS,)),
    DMA((BLOCKS,)),
    pltpu.VMEM((BLOCKS, ROWS, HEAD_DIM), BF16),
    DMA((BLOCKS, 2)),
    DMA((2, 2, 4)),
    DMA((2,)),
    pltpu.VMEM((8, SSM_HEADS), F32),
    pltpu.VMEM((CTX, 8, SSM_HEADS), F32),
    pltpu.VMEM((8, SSM_HEADS), F32),
    pltpu.VMEM((DP, 8, SSM_HEADS), F32),
    DMA((CTX,)),
    DMA((CTX,)),
    DMA,
    DMA((DP,)),
    DMA((DP,)),
    DMA,
]


def gradients(q, k, v, o, d, ids, x, b, c, step, alog, skip):
    hbm = pl.BlockSpec(memory_space=pl.ANY)
    vmem = pl.BlockSpec(memory_space=pltpu.VMEM)
    return pl.pallas_call(
        kernel,
        out_shape=[
            jax.ShapeDtypeStruct((1, ROWS, SSM_HEADS * SSM_DIM), BF16),
            jax.ShapeDtypeStruct((2, ROWS, KVHEADS * HEAD_DIM), BF16),
            jax.ShapeDtypeStruct((2, SSM_HEADS), F32),
            jax.ShapeDtypeStruct((SEQ, WIDTH), BF16),
            jax.ShapeDtypeStruct((3, 2, ROWS, WIDTH), BF16),
            jax.ShapeDtypeStruct((4, BLOCK, WIDTH), BF16),
        ],
        in_specs=[hbm] * 7 + [vmem] * 6,
        out_specs=[hbm, hbm, vmem, hbm, hbm, hbm],
        scratch_shapes=SCRATCH,
        compiler_params=pltpu.CompilerParams(
            collective_id=0, has_side_effects=True, vmem_limit_bytes=60 * 2**20
        ),
        name="gradients",
    )(q, d, k, v, x, b, c, d, o, ids, step, alog, skip)[:3]


def settle_kernel(x, kv, dec, grad_k, grad_v, grad_x, grad_d):
    grad_x[...] = x[...]
    grad_k[0] = kv[0]
    grad_v[0] = kv[1]
    grad_d[...] = dec[...]


def settle(x, kv, dec):
    vmem = pl.BlockSpec(memory_space=pltpu.VMEM)
    narrow = jax.ShapeDtypeStruct((1, ROWS, KVHEADS * HEAD_DIM), BF16)
    return pl.pallas_call(
        settle_kernel,
        out_shape=[narrow, narrow, jax.ShapeDtypeStruct(x.shape, BF16), jax.ShapeDtypeStruct(dec.shape, F32)],
        in_specs=[vmem] * 3,
        out_specs=[vmem] * 4,
        compiler_params=pltpu.CompilerParams(vmem_limit_bytes=60 * 2**20),
        name="settle",
    )(x, kv, dec)


def shards(queries, keys, values, saved, out_grad, doc_ids, inputs, bmat, cmat, step, alog, skip):
    return tuple(settle(*gradients(
        queries, keys, values, saved, out_grad, doc_ids, inputs, bmat, cmat, step, alog[None], skip[None]
    )))


def solution(mesh):
    return jax.shard_map(
        shards,
        mesh=mesh,
        in_specs=(
            P("dp", "ctx", None),
            P("dp", "ctx", None),
            P("dp", "ctx", None),
            P("dp", "ctx", None),
            P("dp", "ctx", None),
            P("dp", "ctx"),
            P("dp", "ctx", None),
            P("dp", "ctx", None),
            P("dp", "ctx", None),
            P("dp", "ctx", None),
            P(),
            P(),
        ),
        out_specs=(P("dp", "ctx", None), P("dp", "ctx", None), P("dp", "ctx", None), P()),
        check_vma=False,
    )
```

```python
import jax
import jax.numpy as jnp
from jax import lax
from jax.experimental import pallas as pl
from jax.experimental.pallas import tpu as pltpu
from jax.sharding import PartitionSpec as P

QHEADS = 32
KVHEADS = 4
HEAD_DIM = 128
SSM_HEADS = 128
SSM_DIM = 32
STATE = 128
SEQ = 2048
ROWS = 128
HALF = 64
CTX = 16
DP = 8
WIDTH = 256
OWN = 8
QCOLS = 512
BLOCK = 256
SPAN = 5
SCALE = HEAD_DIM ** (-0.5)
FAR = -1e30

MESH = pl.DeviceIdType.MESH
HIGHEST = lax.Precision.HIGHEST
F32 = jnp.float32
BF16 = jnp.bfloat16


def dot(a, b, dims, precision=None):
    return lax.dot_general(a, b, (dims, ((), ())), precision=precision, preferred_element_type=F32)


NN = ((1,), (0,))
NT = ((1,), (1,))
TN = ((0,), (0,))


def three(a):
    high = a.astype(BF16)
    rest = a - high.astype(F32)
    mid = rest.astype(BF16)
    low = (rest - mid.astype(F32)).astype(BF16)
    return high, mid, low


def greet(axis, count):
    me = lax.axis_index(axis)
    barrier = pltpu.get_barrier_semaphore()

    def one(off, _):
        pl.semaphore_signal(barrier, inc=1, device_id={axis: lax.rem(me + off, count)}, device_id_type=MESH)
        return 0

    lax.fori_loop(1, count, one, 0)


def await_greetings(total):
    pl.semaphore_wait(pltpu.get_barrier_semaphore(), total)


def slot(device):
    return device // 4 * 4 + device % 2 * 2 + device // 2 % 2


def early_rows(device):
    return pl.ds(pl.multiple_of(device * HALF, HALF), HALF)


def late_rows(device):
    return pl.ds(pl.multiple_of((2 * CTX - 1 - device) * HALF, HALF), HALF)


def device_rows(device):
    return pl.ds(pl.multiple_of(device * ROWS, ROWS), ROWS)


def block_rows(i):
    return pl.ds(pl.multiple_of(i * BLOCK, BLOCK), BLOCK)


def columns(start, width):
    return pl.ds(pl.multiple_of(start * width, width), width)


def pack_small(out_grad, saved, ids, step, alog, small):
    docs = jnp.broadcast_to(ids[...].astype(F32), (4, ROWS))
    rate = step[0] * -jnp.exp(alog[...])
    upto = lax.broadcasted_iota(jnp.int32, (ROWS, ROWS), 0) <= lax.broadcasted_iota(jnp.int32, (ROWS, ROWS), 1)
    totals = dot(rate, upto.astype(F32), TN, HIGHEST)
    steps = step[0].T
    lane = lax.broadcasted_iota(jnp.int32, (ROWS, ROWS), 1)
    deltas = jnp.zeros((ROWS, ROWS), F32)
    for h in range(QHEADS):
        cols = slice(h * HEAD_DIM, (h + 1) * HEAD_DIM)
        product = out_grad[0, :, cols].astype(F32) * saved[0, :, cols].astype(F32)
        deltas = jnp.where(lane == h, jnp.sum(product, axis=1, keepdims=True), deltas)
    deltas = deltas.T
    for j in range(CTX):
        at = 8 * slot(j)
        small[j, 0:8, :] = steps[at : at + 8]
        small[j, 8:16, :] = totals[at : at + 8]
        pair = 4 * (j // 4 * 2 + j % 2)
        small[j, 16:20, :] = deltas[pair : pair + 4]
        small[j, 20:24, :] = docs


def spread_columns(small, doccol):
    doccol[0:8, :] = jnp.full((8, ROWS), -1.0, F32)
    row = lax.broadcasted_iota(jnp.int32, (8, ROWS), 0)
    pick = jnp.where(row == 4, 1.0, 0.0).astype(BF16)

    def one(src, _):
        docs = jnp.where(row == 4, small[src, 16:24, :], 0.0).astype(BF16)
        doccol[pl.ds(pl.multiple_of(8 + src * ROWS, 8), ROWS), :] = dot(docs, pick, TN)
        return 0

    lax.fori_loop(0, CTX, one, 0)


def query_rows(src, late):
    block = src // 4 + late * (7 - 2 * (src // 4))
    second = src % 2 + late * (1 - 2 * (src % 2))
    return pl.ds(pl.multiple_of(block * ROWS + second * HALF, HALF), HALF)


def transpose_keys(kv, kt):
    def one(n, _):
        rows = device_rows(n)
        kt[:, rows] = kv[0, rows, :].T
        return 0

    lax.fori_loop(0, CTX, one, 0)


def attention_block(i, off, zz, q, d, kv, kt, small, doccol, dkv, q2, d2, qt, dt, s_ref, dq, whole):
    rows = device_rows(i)
    for h in range(4):
        part = pl.ds(h * ROWS, ROWS)
        q2[part, :] = q[rows, h * HEAD_DIM : (h + 1) * HEAD_DIM]
        d2[part, :] = d[rows, h * HEAD_DIM : (h + 1) * HEAD_DIM]
        qt[:, part] = q[rows, h * HEAD_DIM : (h + 1) * HEAD_DIM].T
        dt[:, part] = d[rows, h * HEAD_DIM : (h + 1) * HEAD_DIM].T
    dq[...] = jnp.zeros(dq.shape, F32)
    first = jnp.maximum(i - (SPAN - 1), 0)

    def each(body, carry):
        if not whole:
            return lax.fori_loop(0, i + 1 - first, body, carry)
        for n in range(SPAN):
            carry = body(n, carry)
        return carry

    ahead = lax.broadcasted_iota(jnp.int32, (BLOCK, ROWS), 1) - lax.broadcasted_iota(jnp.int32, (BLOCK, ROWS), 0)
    own = small[2 * i + off // ROWS, 20:21, :]
    late = i // 4
    plane = i + late * (7 - 2 * i)
    base = 4 * plane + 2 * zz
    lo, hi = small[base + late, 16:24, :], small[base + 1 - late, 16:24, :]
    left = lax.broadcasted_iota(jnp.int32, (8, ROWS), 1) < HALF
    early_tile = jnp.where(left, lo, jnp.roll(hi, HALF, 1))
    late_tile = jnp.where(left, jnp.roll(lo, HALF, 1), hi)
    tile = jnp.where(late == 1, late_tile, early_tile)
    delta = jnp.concatenate([tile[h : h + 1, :] for h in range(4)], axis=1)

    def scores(n, m):
        j = first + n
        keys = kv[0, block_rows(j), :]
        theirs = doccol[pl.ds(pl.multiple_of(8 + j * BLOCK, 8), BLOCK), :]
        allowed = (own == theirs) & (ahead >= (j - i) * BLOCK - off)
        parts = []
        for half in range(2):
            s = dot(keys, qt[:, pl.ds(half * BLOCK, BLOCK)], NN)
            s = jnp.where(jnp.concatenate([allowed, allowed], axis=1), s, FAR)
            s_ref[n, :, pl.ds(half * BLOCK, BLOCK)] = s
            parts.append(jnp.max(s.reshape(BLOCK // 8, 8, BLOCK), axis=0))
        return jnp.maximum(m, jnp.concatenate(parts, axis=1))

    m = each(scores, jnp.full((8, 4 * ROWS), FAR, F32))
    m = jnp.max(m, axis=0, keepdims=True)

    def exps(n, total):
        parts = []
        for half in range(2):
            cols = pl.ds(half * BLOCK, BLOCK)
            e = jnp.exp((s_ref[n, :, cols] - m[:, half * BLOCK : (half + 1) * BLOCK]) * SCALE)
            s_ref[n, :, cols] = e
            parts.append(jnp.sum(e.reshape(BLOCK // 8, 8, BLOCK), axis=0))
        return total + jnp.concatenate(parts, axis=1)

    total = each(exps, jnp.zeros((8, 4 * ROWS), F32))
    inv = 1.0 / jnp.sum(total, axis=0, keepdims=True)

    def grads(n, _):
        j = first + n
        there = block_rows(j)
        vals, keys_t = kv[1, there, :], kt[:, there]
        probs, scaled = [], []
        for half in range(4):
            cols = slice(half * ROWS, (half + 1) * ROWS)
            p = s_ref[n, :, pl.ds(half * ROWS, ROWS)] * inv[:, cols]
            dp = dot(vals, dt[:, pl.ds(half * ROWS, ROWS)], NN) - delta[:, cols]
            ds = (p * dp * SCALE).astype(BF16)
            dq[:, cols] += dot(keys_t, ds, NN)
            probs.append(p.astype(BF16))
            scaled.append(ds)
        dkv[0, there, :] += dot(jnp.concatenate(scaled, axis=1), q2[...], NN)
        dkv[1, there, :] += dot(jnp.concatenate(probs, axis=1), d2[...], NN)
        return 0

    each(grads, 0)


def spread_matrix(spread):
    row = lax.broadcasted_iota(jnp.int32, spread.shape, 0)
    lane = lax.broadcasted_iota(jnp.int32, spread.shape, 1)
    head = row % OWN
    a = (lane < 1024) & (row < 24) & (lane // ROWS == head)
    b = (lane >= 1024) & (lane < 1280) & (row < 24) & ((lane - 1024) // SSM_DIM == head)
    c = (lane >= 1280) & (row >= 24) & ((lane - 1280) // SSM_DIM == head)
    spread[...] = jnp.where(a | b | c, 1.0, 0.0).astype(BF16)


def ssm_chunk(c, bcm, small, doccol, cot, skip, spread, gstate, gtimed, timed_out, dx):
    base = pl.multiple_of(c * ROWS, ROWS)
    here = pl.ds(base, ROWS)
    bc, cc = bcm[0, here, :], bcm[1, here, :]
    dyb = cot[here, :]
    dy = dyb.astype(F32)
    steps, totals = small[c, 0:8, :], small[c, 8:16, :]
    parts = jnp.concatenate([p.astype(F32) for p in three(totals) + three(steps)], axis=0).astype(BF16)
    wide = dot(parts, spread[...], TN)
    te, se = wide[:, 1024:1280], wide[:, 1280:1536]
    docs = doccol[pl.ds(pl.multiple_of(8 + base, 8), ROWS), :]
    before = doccol[pl.ds(7 + base, 1), :]
    last = doccol[pl.ds(7 + ROWS + base, 1), :]
    docrow = small[c, 20:21, :]
    sub = lax.broadcasted_iota(jnp.int32, (ROWS, ROWS), 0)
    lane = lax.broadcasted_iota(jnp.int32, (ROWS, ROWS), 1)
    inner = jnp.where((sub <= lane) & (docs == docrow), dot(bc, cc, NT), 0.0)

    plain, timed = [], []
    for half in range(2):
        dyh = dyb[:, half * 128 : half * 128 + 128]
        total = None
        for pair in range(2):
            tops, lows, rights = [], [], []
            for one in range(2):
                local = 2 * pair + one
                h = 4 * half + local
                gap = totals[h : h + 1, :] - wide[:, ROWS * h : ROWS * h + ROWS]
                w = inner * jnp.exp(gap)
                tops.append(w.astype(BF16))
                lows.append((w * gap).astype(BF16))
                rights.append(jnp.where(lane // SSM_DIM == local, dyh.astype(F32), 0.0).astype(BF16))
            left = jnp.concatenate([jnp.concatenate(tops, axis=1), jnp.concatenate(lows, axis=1)], axis=0)
            out = dot(left, jnp.concatenate(rights, axis=0), NN)
            total = out if total is None else total + out
        plain.append(total[:ROWS])
        timed.append(total[ROWS:])
    intra = jnp.concatenate(plain, axis=1)
    intra_t = jnp.concatenate(timed, axis=1)

    both = jnp.concatenate([gstate[...], gtimed[...]], axis=1).astype(BF16)
    inter = dot(bc, both, NN)
    te_last = te[ROWS - 1 : ROWS, :]
    docs2 = jnp.concatenate([docs, docs], axis=1)
    before2 = jnp.concatenate([before, before], axis=1)
    last2 = jnp.concatenate([last, last], axis=1)
    left_time = te_last - te
    leave = jnp.where(docs2 == last2, jnp.exp(left_time), 0.0)
    got = intra + leave * inter[:, :WIDTH]
    got_t = intra_t + leave * (left_time * inter[:, :WIDTH] + inter[:, WIDTH:])
    dx[here, :] = (se * got + skip[0:1, :] * dy).astype(BF16)
    timed_out[here, :] = se * got_t

    enter = jnp.where(docs2 == before2, jnp.exp(te), 0.0)
    dye = dy * enter
    fresh = dot(cc, jnp.concatenate([dye, dye * te], axis=1).astype(BF16), TN)
    whole = jnp.where(last2 == before2, jnp.exp(te_last), 0.0)
    old = gstate[...]
    gtimed[...] = whole * (gtimed[...] + te_last * old) + fresh[:, WIDTH:]
    gstate[...] = whole * old + fresh[:, :WIDTH]


def own_heads(me):
    row = lax.broadcasted_iota(jnp.int32, (SSM_HEADS, WIDTH), 0)
    lane = lax.broadcasted_iota(jnp.int32, (SSM_HEADS, WIDTH), 1)
    return jnp.where(lane // SSM_DIM + slot(me) * OWN == row, 1.0, 0.0)


def finish_decay(me, acc_a, acc_s):
    sums = jnp.concatenate(
        [jnp.sum(acc_a[...], axis=0, keepdims=True), jnp.sum(acc_s[...], axis=0, keepdims=True), jnp.zeros((6, WIDTH), F32)],
        axis=0,
    )
    return dot(sums, own_heads(me), NT, HIGHEST)


BLOCKS = SEQ // BLOCK
LAG = 1
KV_EARLY, KV_LATE, BC = range(3)


def kernel(q, d, k, v, x, b, c, dvm, o, ids, step, alog, skip_in,
           grad_x, grad_kv, grad_d, lx, hop, pass_x,
           lq, ld, lkv, lbc, xv, xv_sem, ls, small,
           x_in_send, x_in_recv, hop_send, hop_recv, hop_on_send, small_send, small_recv, first_send, first_recv,
           z_send, core_send, relay_send, fwd_recv, q_send, q_recv, own_sem,
           dkv, q2, d2, qt, dt, kt, s_ref, dq, doccol, spread, gstate, gtimed, timed, acc_a, acc_s, skip,
           dx, x_send, x_recv, x_own, pass_send, pass_recv, pass_on_send,
           cot, cot_out, cot_send, cot_recv,
           pair_in, pair_send, pair_recv, half_out, half_in, half_send, half_recv,
           done, done_send, done_recv, done_own,
           decay, ctx_decay, seq_decay, all_decay, ctx_send, ctx_recv, ctx_own, dp_send, dp_recv, dp_own):
    me = lax.axis_index("ctx")
    row = lax.axis_index("dp")
    xx, zz, cc, zc = me // 4, me // 2 % 2, me % 2, me % 4
    core_peer = me + 1 - 2 * cc
    z_peer = me + 2 - 4 * zz
    first, second = pl.ds(0, HALF), pl.ds(HALF, HALF)

    def remote(src, dst, send_sem, recv_sem, peer):
        return pltpu.make_async_remote_copy(
            src_ref=src, dst_ref=dst, send_sem=send_sem, recv_sem=recv_sem,
            device_id={"ctx": peer}, device_id_type=MESH,
        )

    def group_moves(plane, frm):
        cols = columns(plane, HEAD_DIM)
        return [
            (k.at[0, first, cols], lkv.at[0, early_rows(frm), :]),
            (v.at[0, first, cols], lkv.at[1, early_rows(frm), :]),
            (k.at[0, second, cols], lkv.at[0, late_rows(frm), :]),
            (v.at[0, second, cols], lkv.at[1, late_rows(frm), :]),
            (b.at[0, :, cols], lbc.at[0, device_rows(frm), :]),
            (c.at[0, :, cols], lbc.at[1, device_rows(frm), :]),
        ]

    def first_copy(kind, to, frm, peer):
        src, dst = group_moves(to // 4, frm)[kind]
        return remote(src, dst, first_send.at[kind, peer // 4], first_recv.at[kind, frm], peer)

    def landed(kind, src):
        return (
            lkv.at[:, early_rows(src), :],
            lkv.at[:, late_rows(src), :],
            lbc.at[:, device_rows(src), :],
        )[kind]

    def forward(kind, src, sems, peer):
        ref = landed(kind, src)
        return remote(ref, ref, sems.at[kind, src // 4], fwd_recv.at[kind, src], peer)

    def others_x(body):
        def one(n, _):
            body(lax.rem(xx + n, 4) * 4 + zc)
            return 0

        lax.fori_loop(1, 4, one, 0)

    def each_x(body):
        def one(n, _):
            body(lax.rem(xx + n, 4) * 4 + zc)
            return 0

        lax.fori_loop(0, 4, one, 0)

    def send_first(kinds):
        others_x(lambda to: [first_copy(kind, to, me, to).start() for kind in kinds])

    def q_copy(array, late, to, frm, peer):
        src = ((q, d)[array]).at[0, pl.ds(late * HALF, HALF), columns(to // 4 * 2 + to % 2, QCOLS)]
        dst = ((lq, ld)[array]).at[query_rows(frm, late), :]
        return remote(src, dst, q_send.at[2 * array + late, peer], q_recv.at[2 * array + late, frm], peer)

    def send_q(late):
        def one(n, _):
            to = lax.rem(xx + n // 2, 4) * 4 + 2 * zz + lax.rem(cc + n, 2)
            for array in range(2):
                q_copy(array, late, to, me, to).start()
            return 0

        lax.fori_loop(1, 8, one, 0)

    def q_arrived(src, late):
        @pl.when(src != me)
        def _():
            for array in range(2):
                q_copy(array, late, me, src, src).wait_recv()

    def x_in_copy(to, frm, peer):
        return remote(x.at[0, :, columns(slot(to), WIDTH)], lx.at[device_rows(frm), :],
                      x_in_send.at[peer], x_in_recv.at[frm], peer)

    def small_copy(to, frm, peer):
        return remote(small.at[to], ls.at[frm], small_send.at[peer], small_recv.at[frm], peer)

    def to_all(body):
        def one(n, _):
            body(lax.rem(me + n, CTX))
            return 0

        lax.fori_loop(1, CTX, one, 0)

    def own_copies():
        moves = group_moves(xx, me)
        for array in range(2):
            for late in range(2):
                moves.append((((q, d)[array]).at[0, pl.ds(late * HALF, HALF), columns(xx * 2 + cc, QCOLS)],
                              ((lq, ld)[array]).at[query_rows(me, late), :]))
        moves.append((x.at[0, :, columns(slot(me), WIDTH)], xv.at[device_rows(me), :]))
        moves.append((small.at[me], ls.at[me]))
        return [pltpu.make_async_copy(src, dst, own_sem.at[n]) for n, (src, dst) in enumerate(moves)]

    greet("ctx", CTX)
    greet("dp", DP)
    await_greetings(CTX - 1 + DP - 1)
    send_first((0, 1, 2, 3))
    own = own_copies()
    for copy in own[:-1]:
        copy.start()

    def direct_x_in(over, flip_z, flip_c):
        to = lax.rem(xx + over, 4) * 4 + 2 * lax.rem(zz + flip_z, 2) + lax.rem(cc + flip_c, 2)
        return x_in_copy(to, me, to)

    def hop_copy(over, core):
        to = lax.rem(xx + over, 4) * 4 + 2 - 2 * zz + core
        return remote(x.at[0, :, columns(slot(to), WIDTH)], hop.at[over - 1, core],
                      hop_send.at[over - 1, core], hop_recv.at[over - 1, core], z_peer)

    def hop_on(over, core):
        to = lax.rem(xx + over, 4) * 4 + 2 * zz + core
        return remote(hop.at[over - 1, core], lx.at[device_rows(z_peer), :],
                      hop_on_send.at[over - 1, core], x_in_recv.at[z_peer], to)

    direct_x_in(0, 1, 0).start()
    direct_x_in(0, 1, 1).start()

    @pl.when(xx >= 2)
    def _():
        send_first((4, 5))

    pack_small(dvm, o, ids, step, alog, small)
    to_all(lambda to: small_copy(to, me, to).start())
    own[-1].start()
    send_q(1)

    @pl.when(xx < 2)
    def _():
        send_first((4, 5))

    for copy in own:
        copy.wait()

    def planes(first, count, body):
        def one(n, _):
            body(n * 4 + zc)
            return 0

        lax.fori_loop(first, first + count, one, 0)

    def pass_on(kinds, parts, first, count):
        def one(src):
            @pl.when(src != me)
            def _():
                for kind in kinds:
                    first_copy(kind, me, src, src).wait_recv()

            for part in parts:
                forward(part, src, z_send, z_peer).start()
                forward(part, src, core_send, core_peer).start()

        planes(first, count, one)

    def relay(parts, first, count):
        def one(src):
            src = src + 2 - 4 * zz
            for part in parts:
                forward(part, src, z_send, z_peer).wait_recv()
                forward(part, src, relay_send, core_peer).start()

        planes(first, count, one)

    def from_core(parts, first, count):
        def one(src):
            for flip in (0, 1):
                at = src + 1 - 2 * cc + flip * (2 - 4 * zz)
                for part in parts:
                    forward(part, at, core_send, core_peer).wait_recv()

        planes(first, count, one)

    pass_on((0, 1, 2, 3), (KV_EARLY, KV_LATE), 0, 4)
    pass_on((4, 5), (BC,), 2, 2)
    send_q(0)
    for over in range(1, 4):
        for core in range(2):
            hop_copy(over, core).start()

    for ref in (dkv, gstate, gtimed, acc_a, acc_s):
        ref[...] = jnp.zeros(ref.shape, F32)
    skip[...] = dot(jnp.broadcast_to(skip_in[...], (8, SSM_HEADS)), own_heads(me), NN, HIGHEST)
    spread_matrix(spread)
    relay((KV_EARLY, KV_LATE), 0, 4)
    to_all(lambda src: small_copy(me, src, src).wait_recv())
    spread_columns(ls, doccol)
    from_core((KV_EARLY, KV_LATE), 0, 4)
    transpose_keys(lkv, kt)
    relay((BC,), 2, 2)

    def x_copy(to, frm, peer):
        return remote(dx.at[device_rows(to), :], grad_x.at[0, :, columns(slot(frm), WIDTH)],
                      x_send.at[peer], x_recv.at[frm], peer)

    def x_mine():
        return pltpu.make_async_copy(dx.at[device_rows(me), :], grad_x.at[0, :, columns(slot(me), WIDTH)], x_own)

    def pass_copy(i):
        return remote(dx.at[block_rows(i), :], pass_x.at[i // 2], pass_send.at[i // 2], pass_recv.at[i // 2], z_peer)

    def passed_copy(i, sub):
        owner = 2 * i + sub
        return remote(pass_x.at[i // 2, pl.ds(sub * ROWS, ROWS), :], grad_x.at[0, :, columns(slot(z_peer), WIDTH)],
                      pass_on_send.at[i // 2, sub], x_recv.at[z_peer], owner)

    def passes(i):
        return (i % 2 != zz) & (i // 2 != xx) & (i >= 2)

    def passed(i):
        return (i % 2 == zz) & (i // 2 != xx) & (i >= 2)

    def own_off(i):
        late = i // 4
        return (zz + late - 2 * zz * late) * ROWS

    def cot_copy(i, off):
        return remote(cot_out.at[i], cot.at[pl.ds(pl.multiple_of(i * BLOCK + off, ROWS), ROWS), :],
                      cot_send.at[i], cot_recv.at[i], z_peer)

    def pair_copy(i, which):
        return remote(dkv.at[which, block_rows(i), :], pair_in.at[i], pair_send.at[i], pair_recv.at[i], core_peer)

    def half_copy(i):
        return remote(half_out.at[i], half_in.at[i], half_send.at[i], half_recv.at[i], z_peer)

    def done_owner(i, r):
        late = i // 4
        chunk = 4 * i + own_off(i) // HALF + r
        return chunk + late * (2 * CTX - 1 - 2 * chunk)

    def done_copy(i, r, core, plane, late, peer):
        return remote(done.at[i, pl.ds(r * HALF, HALF), :],
                      grad_kv.at[core, pl.ds(pl.multiple_of(late * HALF, HALF), HALF), columns(plane, HEAD_DIM)],
                      done_send.at[i, r], done_recv.at[core, late, plane], peer)

    def done_mine(i, r):
        late = i // 4
        return pltpu.make_async_copy(
            done.at[i, pl.ds(r * HALF, HALF), :],
            grad_kv.at[cc, pl.ds(pl.multiple_of(late * HALF, HALF), HALF), columns(xx, HEAD_DIM)],
            done_own.at[late],
        )

    def sum_pair(i):
        pair_copy(i, 1 - cc).wait_recv()
        off = ROWS - own_off(i)
        there = pl.ds(pl.multiple_of(i * BLOCK + off, ROWS), ROWS)
        half_out[i] = (dkv[cc, there, :] + pair_in[i, pl.ds(pl.multiple_of(off, ROWS), ROWS), :]).astype(BF16)
        half_copy(i).start()

    def sum_half(i):
        half_copy(i).wait_recv()
        off = own_off(i)
        there = pl.ds(pl.multiple_of(i * BLOCK + off, ROWS), ROWS)
        mine = dkv[cc, there, :] + pair_in[i, pl.ds(pl.multiple_of(off, ROWS), ROWS), :]
        done[i] = (mine + half_in[i].astype(F32)).astype(BF16)
        for r in range(2):
            owner = done_owner(i, r)

            @pl.when(owner != me)
            def _():
                done_copy(i, r, cc, xx, i // 4, owner).start()

            @pl.when(owner == me)
            def _():
                done_mine(i, r).start()

    def take_in(src):
        return pltpu.make_async_copy(lx.at[device_rows(src), :], xv.at[device_rows(src), :], xv_sem.at[src])

    def landed_x(src):
        x_in_copy(me, src, src).wait_recv()
        take_in(src).start()

    def block(n, _):
        @pl.when(n < BLOCKS)
        def _():
            i = BLOCKS - 1 - n
            off = own_off(i)

            @pl.when(i >= 4)
            def _():
                for r in range(2):
                    q_arrived(4 * (7 - i) + 2 * zz + r, 1)

            @pl.when(i < 4)
            def _():
                for r in range(2):
                    q_arrived(4 * i + 2 * zz + r, 0)

            for whole in (True, False):
                @pl.when((i >= SPAN - 1) == whole)
                def _():
                    attention_block(i, off, zz, lq, ld, lkv, kt, ls, doccol, dkv, q2, d2, qt, dt, s_ref, dq, whole)

            pair_copy(i, 1 - cc).start()
            here = pl.ds(pl.multiple_of(i * BLOCK + off, ROWS), ROWS)
            for e in range(2):
                cols = slice(e * HEAD_DIM, (e + 1) * HEAD_DIM)
                cot[here, cols] = dq[:, columns(2 * zz + e, ROWS)].T.astype(BF16)
                cot_out[i, :, cols] = dq[:, columns(2 - 2 * zz + e, ROWS)].T.astype(BF16)
            cot_copy(i, off).start()

        @pl.when(n == 0)
        def _():
            pass_on((4, 5), (BC,), 0, 2)
            direct_x_in(0, 0, 1).start()

        @pl.when(n < 3)
        def _():
            direct_x_in(n + 1, 0, 0).start()
            direct_x_in(n + 1, 0, 1).start()

        @pl.when((n >= 2) & (n < 5))
        def _():
            for core in range(2):
                hop_copy(n - 1, core).wait_recv()
                hop_on(n - 1, core).start()

        @pl.when((n >= 2) & passed(BLOCKS + 1 - n))
        def _():
            i = BLOCKS + 1 - n
            pass_copy(i).wait_recv()
            for sub in range(2):
                passed_copy(i, sub).start()

        @pl.when(n == 1)
        def _():
            from_core((BC,), 2, 2)

        @pl.when(n == 2)
        def _():
            relay((BC,), 0, 2)

        @pl.when(n == 4)
        def _():
            from_core((BC,), 0, 2)

        @pl.when((n >= 1) & (n <= BLOCKS))
        def _():
            sum_pair(BLOCKS - n)

        @pl.when(n >= 2)
        def _():
            sum_half(BLOCKS + 1 - n)

        @pl.when(n == BLOCKS)
        def _():
            to_all(landed_x)

        @pl.when(n >= LAG)
        def _():
            i = BLOCKS - 1 + LAG - n
            cot_copy(i, ROWS - own_off(i)).wait_recv()
            for sub in (1, 0):
                owner = 2 * i + sub

                ssm_chunk(owner, lbc, ls, doccol, cot, skip, spread, gstate, gtimed, timed, dx)

                @pl.when((owner != me) & jnp.logical_not(passes(i)))
                def _():
                    x_copy(owner, me, owner).start()

                @pl.when(owner == me)
                def _():
                    x_mine().start()

            @pl.when(passes(i))
            def _():
                pass_copy(i).start()

        return 0

    lax.fori_loop(0, BLOCKS + LAG, block, 0)
    sum_half(0)

    to_all(lambda src: take_in(src).wait())

    def gather(c, _):
        here = device_rows(c)
        xc = xv[here, :].astype(F32)
        acc_a[...] += xc * timed[here, :]
        acc_s[...] += xc * cot[here, :].astype(F32)
        return 0

    lax.fori_loop(0, CTX, gather, 0)
    decay[...] = finish_decay(me, acc_a, acc_s)

    def ctx_copy(frm, peer):
        return remote(decay, ctx_decay.at[frm], ctx_send.at[peer], ctx_recv.at[frm], peer)

    def dp_copy(frm, peer):
        return pltpu.make_async_remote_copy(
            src_ref=seq_decay, dst_ref=all_decay.at[frm], send_sem=dp_send.at[peer], recv_sem=dp_recv.at[frm],
            device_id={"dp": peer}, device_id_type=MESH,
        )

    to_all(lambda to: ctx_copy(me, to).start())
    ctx_mine = pltpu.make_async_copy(decay, ctx_decay.at[me], ctx_own)
    ctx_mine.start()
    to_all(lambda frm: ctx_copy(frm, frm).wait_recv())
    ctx_mine.wait()
    seq_decay[...] = jnp.sum(ctx_decay[...], axis=0)

    def start_dp(off, _):
        dp_copy(row, lax.rem(row + off, DP)).start()
        return 0

    lax.fori_loop(1, DP, start_dp, 0)
    dp_mine = pltpu.make_async_copy(seq_decay, all_decay.at[row], dp_own)
    dp_mine.start()

    def sent(to):
        small_copy(to, me, to).wait_send()

        @pl.when(jnp.logical_not(passes(to // 2)))
        def _():
            x_copy(to, me, to).wait_send()

        ctx_copy(me, to).wait_send()

    to_all(sent)
    for over in range(4):
        for core in range(2):
            if over:
                hop_copy(over, core).wait_send()
                hop_on(over, core).wait_send()
            else:
                direct_x_in(0, 1, core).wait_send()
            if over or core:
                direct_x_in(over, 0, core).wait_send()
    others_x(lambda to: [first_copy(kind, to, me, to).wait_send() for kind in range(6)])

    def forwarded(src):
        other = src + 2 - 4 * zz
        for part in range(3):
            forward(part, src, z_send, z_peer).wait_send()
            forward(part, src, core_send, core_peer).wait_send()
            forward(part, other, relay_send, core_peer).wait_send()

    each_x(forwarded)

    def sent_q(n, _):
        to = lax.rem(xx + n // 2, 4) * 4 + 2 * zz + lax.rem(cc + n, 2)
        for array in range(2):
            for late in range(2):
                q_copy(array, late, to, me, to).wait_send()
        return 0

    lax.fori_loop(1, 8, sent_q, 0)

    def sent_blocks(i, _):
        @pl.when(passes(i))
        def _():
            pass_copy(i).wait_send()

        @pl.when(passed(i))
        def _():
            for sub in range(2):
                passed_copy(i, sub).wait_send()

        cot_copy(i, own_off(i)).wait_send()
        pair_copy(i, 1 - cc).wait_send()
        half_copy(i).wait_send()
        for r in range(2):
            owner = done_owner(i, r)

            @pl.when(owner != me)
            def _():
                done_copy(i, r, cc, xx, i // 4, owner).wait_send()

            @pl.when(owner == me)
            def _():
                done_mine(i, r).wait()

        return 0

    lax.fori_loop(0, BLOCKS, sent_blocks, 0)

    for core in range(2):
        for late in range(2):
            for plane in range(4):
                @pl.when(plane * 4 + 2 * zz + core != me)
                def _():
                    done_copy(0, 0, core, plane, late, core_peer).wait_recv()

    def end_dp(off, _):
        frm = lax.rem(row + DP - off, DP)
        dp_copy(frm, frm).wait_recv()
        dp_copy(row, frm).wait_send()
        return 0

    lax.fori_loop(1, DP, end_dp, 0)
    dp_mine.wait()
    total = all_decay[0]
    for other in range(1, DP):
        total += all_decay[other]
    grad_d[...] = total[:2]
    to_all(lambda frm: x_copy(me, frm, frm).wait_recv())
    x_mine().wait()


DMA = pltpu.SemaphoreType.DMA
SCRATCH = [
    pltpu.VMEM((SEQ // 2, QCOLS), BF16),
    pltpu.VMEM((SEQ // 2, QCOLS), BF16),
    pltpu.VMEM((2, SEQ, HEAD_DIM), BF16),
    pltpu.VMEM((2, SEQ, STATE), BF16),
    pltpu.VMEM((SEQ, WIDTH), BF16),
    DMA((CTX,)),
    pltpu.VMEM((CTX, 24, ROWS), F32),
    pltpu.VMEM((CTX, 24, ROWS), F32),
    DMA((CTX,)),
    DMA((CTX,)),
    DMA((3, 2)),
    DMA((3, 2)),
    DMA((3, 2)),
    DMA((CTX,)),
    DMA((CTX,)),
    DMA((6, 4)),
    DMA((6, CTX)),
    DMA((3, 4)),
    DMA((3, 4)),
    DMA((3, 4)),
    DMA((3, CTX)),
    DMA((4, CTX)),
    DMA((4, CTX)),
    DMA((12,)),
    pltpu.VMEM((2, SEQ, HEAD_DIM), F32),
    pltpu.VMEM((4 * ROWS, HEAD_DIM), BF16),
    pltpu.VMEM((4 * ROWS, HEAD_DIM), BF16),
    pltpu.VMEM((HEAD_DIM, 4 * ROWS), BF16),
    pltpu.VMEM((HEAD_DIM, 4 * ROWS), BF16),
    pltpu.VMEM((HEAD_DIM, SEQ), BF16),
    pltpu.VMEM((SPAN, BLOCK, 4 * ROWS), F32),
    pltpu.VMEM((HEAD_DIM, 4 * ROWS), F32),
    pltpu.VMEM((SEQ + 8, ROWS), F32),
    pltpu.VMEM((48, 1536), BF16),
    pltpu.VMEM((STATE, WIDTH), F32),
    pltpu.VMEM((STATE, WIDTH), F32),
    pltpu.VMEM((SEQ, WIDTH), F32),
    pltpu.VMEM((ROWS, WIDTH), F32),
    pltpu.VMEM((ROWS, WIDTH), F32),
    pltpu.VMEM((8, WIDTH), F32),
    pltpu.VMEM((SEQ, WIDTH), BF16),
    DMA((CTX,)),
    DMA((CTX,)),
    DMA,
    DMA((4,)),
    DMA((4,)),
    DMA((4, 2)),
    pltpu.VMEM((SEQ, WIDTH), BF16),
    pltpu.VMEM((BLOCKS, ROWS, WIDTH), BF16),
    DMA((BLOCKS,)),
    DMA((BLOCKS,)),
    pltpu.VMEM((BLOCKS, BLOCK, HEAD_DIM), F32),
    DMA((BLOCKS,)),
    DMA((BLOCKS,)),
    pltpu.VMEM((BLOCKS, ROWS, HEAD_DIM), BF16),
    pltpu.VMEM((BLOCKS, ROWS, HEAD_DIM), BF16),
    DMA((BLOCKS,)),
    DMA((BLOCKS,)),
    pltpu.VMEM((BLOCKS, ROWS, HEAD_DIM), BF16),
    DMA((BLOCKS, 2)),
    DMA((2, 2, 4)),
    DMA((2,)),
    pltpu.VMEM((8, SSM_HEADS), F32),
    pltpu.VMEM((CTX, 8, SSM_HEADS), F32),
    pltpu.VMEM((8, SSM_HEADS), F32),
    pltpu.VMEM((DP, 8, SSM_HEADS), F32),
    DMA((CTX,)),
    DMA((CTX,)),
    DMA,
    DMA((DP,)),
    DMA((DP,)),
    DMA,
]


def gradients(q, k, v, o, d, ids, x, b, c, step, alog, skip):
    hbm = pl.BlockSpec(memory_space=pl.ANY)
    vmem = pl.BlockSpec(memory_space=pltpu.VMEM)
    return pl.pallas_call(
        kernel,
        out_shape=[
            jax.ShapeDtypeStruct((1, ROWS, SSM_HEADS * SSM_DIM), BF16),
            jax.ShapeDtypeStruct((2, ROWS, KVHEADS * HEAD_DIM), BF16),
            jax.ShapeDtypeStruct((2, SSM_HEADS), F32),
            jax.ShapeDtypeStruct((SEQ, WIDTH), BF16),
            jax.ShapeDtypeStruct((3, 2, ROWS, WIDTH), BF16),
            jax.ShapeDtypeStruct((4, BLOCK, WIDTH), BF16),
        ],
        in_specs=[hbm] * 7 + [vmem] * 6,
        out_specs=[hbm, hbm, vmem, hbm, hbm, hbm],
        scratch_shapes=SCRATCH,
        compiler_params=pltpu.CompilerParams(
            collective_id=0, has_side_effects=True, vmem_limit_bytes=60 * 2**20
        ),
        name="gradients",
    )(q, d, k, v, x, b, c, d, o, ids, step, alog, skip)[:3]


def settle_kernel(x, kv, dec, grad_k, grad_v, grad_x, grad_d):
    grad_x[...] = x[...]
    grad_k[0] = kv[0]
    grad_v[0] = kv[1]
    grad_d[...] = dec[...]


def settle(x, kv, dec):
    vmem = pl.BlockSpec(memory_space=pltpu.VMEM)
    narrow = jax.ShapeDtypeStruct((1, ROWS, KVHEADS * HEAD_DIM), BF16)
    return pl.pallas_call(
        settle_kernel,
        out_shape=[narrow, narrow, jax.ShapeDtypeStruct(x.shape, BF16), jax.ShapeDtypeStruct(dec.shape, F32)],
        in_specs=[vmem] * 3,
        out_specs=[vmem] * 4,
        compiler_params=pltpu.CompilerParams(vmem_limit_bytes=60 * 2**20),
        name="settle",
    )(x, kv, dec)


def shards(queries, keys, values, saved, out_grad, doc_ids, inputs, bmat, cmat, step, alog, skip):
    return tuple(settle(*gradients(
        queries, keys, values, saved, out_grad, doc_ids, inputs, bmat, cmat, step, alog[None], skip[None]
    )))


def solution(mesh):
    return jax.shard_map(
        shards,
        mesh=mesh,
        in_specs=(
            P("dp", "ctx", None),
            P("dp", "ctx", None),
            P("dp", "ctx", None),
            P("dp", "ctx", None),
            P("dp", "ctx", None),
            P("dp", "ctx"),
            P("dp", "ctx", None),
            P("dp", "ctx", None),
            P("dp", "ctx", None),
            P("dp", "ctx", None),
            P(),
            P(),
        ),
        out_specs=(P("dp", "ctx", None), P("dp", "ctx", None), P("dp", "ctx", None), P()),
        check_vma=False,
    )
```
